32 devices in a mesh: fsdp: 8 (over y, x, core), ns: 4 (over z).
Axes of the slice: x: 2, y: 2, z: 4, core: 2. Of those that a mesh axis runs over, the one named last changes fastest.
Arguments:
- tokens: bfloat16 [32, 256, 1024], P(('fsdp', 'ns')), may hold values from -6 to 6
- out_grad: bfloat16 [32, 256, 1024], P(('fsdp', 'ns')), may hold values from -6 to 6
- doc_lengths: int32 [32, 4], P(('fsdp', 'ns')), may hold values from 1 to 128, 256 in all within a row
- in_proj: float32 [4096, 1024], P(('fsdp', 'ns')), may hold values from -0.1875 to 0.1875
- inner_projection_weight: float32 [2048, 96], P(('fsdp', 'ns')), may hold values from -0.125 to 0.125
- dt_proj: float32 [2048, 64], P(('fsdp', 'ns')), may hold values from -0.75 to 0.75
- out_proj: float32 [2048, 1024], P(('fsdp', 'ns')), may hold values from -0.375 to 0.375
- in_moment: float32 [4096, 1024], P(('fsdp', 'ns')), may hold values from -162.9174 to 162.9174
- x_moment: float32 [2048, 96], P(('fsdp', 'ns')), may hold values from -244.3761 to 244.3761
- dt_moment: float32 [2048, 64], P(('fsdp', 'ns')), may hold values from -244.3761 to 244.3761
- out_moment: float32 [2048, 1024], P(('fsdp', 'ns')), may hold values from -244.3761 to 244.3761
- vectors: float32 [23, 2048], P(None, ('fsdp', 'ns')), may hold values from -7 to 3, as said below
- vector_first: float32 [23, 2048], P(None, ('fsdp', 'ns')), may hold values from -9.050967 to 9.050967
- vector_second: float32 [23, 2048], P(None, ('fsdp', 'ns')), may hold values from 0.016384 to 327.68
- norm_gain: float32 [1024], P(('fsdp', 'ns')), may hold values from 0.5 to 1.5
- gain_first: float32 [1024], P(('fsdp', 'ns')), may hold values from -16 to 16
- gain_second: float32 [1024], P(('fsdp', 'ns')), may hold values from 19.6608 to 311.296
Outputs:
- block_out: float32 [32, 256, 1024], P(('fsdp', 'ns'))
- grad_tokens: float32 [32, 256, 1024], P(('fsdp', 'ns'))
- in_proj_new: float32 [4096, 1024], P(('fsdp', 'ns'))
- in_moment_new: float32 [4096, 1024], P(('fsdp', 'ns'))
- x_proj_new: float32 [2048, 96], P(('fsdp', 'ns'))
- x_moment_new: float32 [2048, 96], P(('fsdp', 'ns'))
- dt_proj_new: float32 [2048, 64], P(('fsdp', 'ns'))
- dt_moment_new: float32 [2048, 64], P(('fsdp', 'ns'))
- out_proj_new: float32 [2048, 1024], P(('fsdp', 'ns'))
- out_moment_new: float32 [2048, 1024], P(('fsdp', 'ns'))
- vectors_new: float32 [23, 2048], P(None, ('fsdp', 'ns'))
- vector_first_new: float32 [23, 2048], P(None, ('fsdp', 'ns'))
- vector_second_new: float32 [23, 2048], P(None, ('fsdp', 'ns'))
- norm_gain_new: float32 [1024], P(('fsdp', 'ns'))
- gain_first_new: float32 [1024], P(('fsdp', 'ns'))
- gain_second_new: float32 [1024], P(('fsdp', 'ns'))
The draws below stay inside these ranges and needn't reach their ends.
Inputs may be any that keep to these rules, and one draw needn't show every extreme that they name: `doc_lengths`: each row's lengths add up to 256. `vectors`: a_log rows lie in 0 to log 16, skip gains in 0.5 to 1.5.
All inputs are finite; a program needn't handle non-finite values.
Results may differ from the reference program's by a relative error of at most 0.012.
Values may be sent and summed in bfloat16 or wider, within the bound.
A program may use at most 192 MiB of HBM per device.

```python
import math
import jax
import jax.numpy as jnp
import numpy as np
from jax import lax

DMODEL = 1024
DINNER = 2048
DSTATE = 16
DTRANK = 64
KCONV = 4
ROW_LEN = 256
NDOC = 4
BLOCK_LEN = 64
NS_STEPS = 4
STEP_NO = 10
XCOLS = 96
ROWS = 32
TOKENS = 8192


def growth(row_count, top_value):
    places = jnp.arange(row_count, dtype=jnp.float32) / max(row_count - 1, 1)
    return 1.0 + (top_value - 1.0) * places


def vector_scales():
    parts = [jnp.full((KCONV,), 0.3, jnp.float32), jnp.array([0.3, 0.03, 0.3], jnp.float32), jnp.full((DSTATE,), 0.01, jnp.float32)]
    return jnp.concatenate(parts) * math.sqrt(TOKENS)


def draw_in_moment(key, part):
    key = jax.random.fold_in(key, 11)
    shape = (2 * DINNER, DMODEL)
    base = jax.random.truncated_normal(key, -3.0, 3.0, shape, jnp.float32)
    top_value = 3.0
    return base * growth(shape[0], top_value)[:, None] * (0.2 * math.sqrt(TOKENS))


def draw_x_moment(key, part):
    key = jax.random.fold_in(key, 12)
    shape = (DINNER, DTRANK + 2 * DSTATE)
    base = jax.random.truncated_normal(key, -3.0, 3.0, shape, jnp.float32)
    top_value = 3.0
    return base * growth(shape[0], top_value)[:, None] * (0.3 * math.sqrt(TOKENS))


def draw_dt_moment(key, part):
    key = jax.random.fold_in(key, 13)
    shape = (DINNER, DTRANK)
    base = jax.random.truncated_normal(key, -3.0, 3.0, shape, jnp.float32)
    top_value = 3.0
    return base * growth(shape[0], top_value)[:, None] * (0.3 * math.sqrt(TOKENS))


def draw_out_moment(key, part):
    key = jax.random.fold_in(key, 14)
    shape = (DINNER, DMODEL)
    base = jax.random.truncated_normal(key, -3.0, 3.0, shape, jnp.float32)
    top_value = 3.0
    return base * growth(shape[0], top_value)[:, None] * (0.3 * math.sqrt(TOKENS))


def draw_vectors(key, part):
    key = jax.random.fold_in(key, 21)
    keys = jax.random.split(key, 5)
    taps = 0.5 * jax.random.truncated_normal(keys[0], -3.0, 3.0, (KCONV, DINNER), jnp.float32)
    conv_bias = jax.random.uniform(keys[1], (1, DINNER), jnp.float32, -0.3, 0.3)
    dt_value = jnp.exp(jax.random.uniform(keys[2], (1, DINNER), jnp.float32, math.log(0.001), math.log(0.1)))
    dt_bias = dt_value + jnp.log(-jnp.expm1(-dt_value))
    skip_gain = jax.random.uniform(keys[3], (1, DINNER), jnp.float32, 0.5, 1.5)
    a_log = jax.random.uniform(keys[4], (DSTATE, DINNER), jnp.float32, 0.0, math.log(16.0))
    return jnp.concatenate([taps, conv_bias, dt_bias, skip_gain, a_log], axis=0)


def draw_vector_first(key, part):
    key = jax.random.fold_in(key, 22)
    shape = (KCONV + 3 + DSTATE, DINNER)
    base = jax.random.truncated_normal(key, -3.0, 3.0, shape, jnp.float32)
    return base * 0.11 * vector_scales()[:, None]


def draw_vector_second(key, part):
    key = jax.random.fold_in(key, 23)
    shape = (KCONV + 3 + DSTATE, DINNER)
    factor = jnp.exp(jax.random.uniform(key, shape, jnp.float32, math.log(0.5), math.log(8.0)))
    scales = vector_scales()
    return factor * 0.0526 * (scales * scales)[:, None]


def steps_of(own_key, shape, shards, least, high):
    gain = 1.0
    for position, blocks in shards:
        heights = jax.random.uniform(jax.random.fold_in(jax.random.fold_in(own_key, 6), position), (blocks,), jnp.float32, least / len(shards), high / len(shards))
        gain = gain * jnp.repeat(jnp.exp(heights), shape[position] // blocks).reshape((-1,) + (1,) * (len(shape) - 1 - position))
    return gain


def length_profile(count, total, bound, lean):
    weights = [(1 << 20) // math.isqrt(standing ** lean) + 1 for standing in range(2, count + 1)]
    rest, counts = total - bound - (count - 1), [1] * (count - 1)
    while rest > 0:
        movable = [i for i in range(count - 1) if counts[i] < bound]
        pool, remaining = sum([weights[i] for i in movable]), rest
        for i in movable:
            addition = min(bound - counts[i], max(1, remaining * weights[i] // pool), rest)
            counts[i] = counts[i] + addition
            rest = rest - addition
    return np.array([bound] + counts)


def uneven_parts(stream_key, number_of, total, bound, lean):
    if number_of == 2:
        one = jax.random.randint(stream_key, (), max(1, total - bound), min(bound, total - 1) + 1)
        return jnp.stack([one, total - one])
    sizes = jnp.asarray(length_profile(number_of, total, bound, lean), jnp.int32)
    twos = (number_of - 1) // 2
    source_of, receiver = sizes[1:1 + 2 * twos:2], sizes[2:2 + 2 * twos:2]
    margin = jnp.minimum(source_of - 1, bound - receiver)
    shifted = jax.random.randint(jax.random.fold_in(stream_key, 1), (twos,), 0, 1 << 20) % (margin + 1)
    sizes = sizes.at[1:1 + 2 * twos:2].set(source_of - shifted).at[2:2 + 2 * twos:2].set(receiver + shifted)
    return sizes[jax.random.permutation(jax.random.fold_in(stream_key, 2), number_of)]


def normal_values(own_key, extent, scale, bound, cuts=(), held_as=jnp.bfloat16):
    result = scale * jax.random.normal(own_key, extent, jnp.float32)
    if cuts:
        result = result * steps_of(own_key, extent, cuts, -0.22, 0.18)
    return jnp.clip(result, -bound, bound).astype(held_as)


def setup_inputs(seed: int = 0) -> dict:
    streams_of = jax.random.split(jax.random.key(seed), 18)
    return {
        "tokens": normal_values(streams_of[0], (ROWS, ROW_LEN, DMODEL), 1.0, 6.0, ((0, 32),)),
        "out_grad": normal_values(streams_of[1], (ROWS, ROW_LEN, DMODEL), 1.0, 6.0, ((0, 32),)),
        "doc_lengths": jax.vmap(lambda own: uneven_parts(own, NDOC, ROW_LEN, ROW_LEN // 2, 0))(jax.random.split(streams_of[2], ROWS)).reshape((ROWS, NDOC)).astype(jnp.int32),
        "in_proj": normal_values(streams_of[3], (2 * DINNER, DMODEL), DMODEL ** -0.5, 0.1875, ((0, 32),), jnp.float32),
        "inner_projection_weight": normal_values(streams_of[4], (DINNER, XCOLS), DINNER ** -0.5, 0.125, ((0, 32),), jnp.float32),
        "dt_proj": normal_values(streams_of[5], (DINNER, DTRANK), DTRANK ** -0.5, 0.75, ((0, 32),), jnp.float32),
        "out_proj": normal_values(streams_of[6], (DINNER, DMODEL), (DINNER // 8) ** -0.5, 0.375, ((0, 32),), jnp.float32),
        "in_moment": draw_in_moment(jax.random.fold_in(streams_of[17], 71), 0),
        "x_moment": draw_x_moment(jax.random.fold_in(streams_of[17], 71), 0),
        "dt_moment": draw_dt_moment(jax.random.fold_in(streams_of[17], 71), 0),
        "out_moment": draw_out_moment(jax.random.fold_in(streams_of[17], 71), 0),
        "vectors": draw_vectors(jax.random.fold_in(streams_of[17], 71), 0),
        "vector_first": draw_vector_first(jax.random.fold_in(streams_of[17], 71), 0),
        "vector_second": draw_vector_second(jax.random.fold_in(streams_of[17], 71), 0),
        "norm_gain": jnp.clip(1.0 + 0.1 * jax.random.normal(streams_of[14], (DMODEL,), jnp.float32), 0.5, 1.5),
        "gain_first": normal_values(streams_of[15], (DMODEL,), (0.033 * TOKENS ** 0.5), 16.0, ((0, 32),), jnp.float32),
        "gain_second": jnp.clip(jnp.exp(math.log(311.296) - 2.7621173 * jax.random.uniform(streams_of[16], (DMODEL,), jnp.float32) ** steps_of(streams_of[16], (DMODEL,), ((0, 32),), -0.2, 0.2)), 19.6608, 311.296),
    }


PRECISION_HIGH = lax.Precision.HIGHEST
NORM_EPS = 1e-05
FROB_EPS = 1e-07
COEF_A = 3.4445
COEF_B = -4.775
COEF_C = 2.0315
MOMENTUM = 0.95
SHRINK = 0.001
FIRST_MOMENT_BETA = 0.9
BETA_SECOND = 0.95
ADAM_EPS = 1e-08
ADAM_RATE = 1.0
ADAM_DECAY = 0.001

@jax.custom_vjp
def low(v):
    return lax.optimization_barrier(v.astype(jnp.bfloat16)).astype(jnp.float32)

@jax.custom_vjp
def lowered_backward(v):
    return v

def low_keep(v):
    return (low(v), None)

def low_pass(kept, grad):
    return (grad,)

def back_keep(v):
    return (v, None)

def back_low(kept, grad):
    return (low(grad),)
low.defvjp(low_keep, low_pass)
lowered_backward.defvjp(back_keep, back_low)

def rounded(value):
    return lax.optimization_barrier(value.astype(jnp.bfloat16)).astype(jnp.float32)

def segment_ids(lengths, length):
    ends = jnp.cumsum(lengths, axis=-1).astype(jnp.int32)
    starts = (ends - lengths).astype(jnp.int32)
    places = jnp.arange(length, dtype=jnp.int32)
    return lax.optimization_barrier(jnp.sum((places[None, :, None] >= starts[:, None, :]).astype(jnp.int32), axis=-1, dtype=jnp.int32))

def same_lag(segment, lag_index):
    length = segment.shape[1]
    earlier = jnp.pad(segment, ((0, 0), (lag_index, 0)), constant_values=-1)[:, :length]
    return (earlier == segment).astype(jnp.float32)

def delayed(value, lag_index):
    length = value.shape[1]
    return jnp.pad(value, ((0, 0), (lag_index, 0), (0, 0)))[:, :length]

def step_state(carry, item):
    state, a_matrix = carry
    delta_t, b_t, c_t, u_t, keep_t = item
    state = jnp.exp(delta_t[:, None, :] * a_matrix) * keep_t[:, None, None] * state + (delta_t * u_t)[:, None, :] * b_t[:, :, None]
    return ((state, a_matrix), lax.optimization_barrier(jnp.sum(state * c_t[:, :, None], axis=1)))

def block_run(state, a_matrix, pieces):
    (state, unused), outputs = lax.scan(step_state, (state, a_matrix), pieces)
    return (state, outputs)
checked_block = jax.checkpoint(block_run)

def selective(delta, b_rows, c_rows, scan_input_value, keep, a_matrix):
    groups, length, inner_channel_width = delta.shape
    count = length // BLOCK_LEN

    def cut(value):
        moved = jnp.moveaxis(value, 1, 0)
        return moved.reshape((count, BLOCK_LEN) + moved.shape[1:])
    pieces = tuple((cut(value) for value in (delta, b_rows, c_rows, scan_input_value, keep)))

    def outer(state, piece):
        return checked_block(state, a_matrix, piece)
    start = jnp.zeros((groups, DSTATE, inner_channel_width), jnp.float32)
    unused, outputs = lax.scan(outer, start, pieces)
    return jnp.moveaxis(outputs.reshape((length, groups, inner_channel_width)), 0, 1)

def forward(tokens, in_proj, inner_projection_weight, dt_proj, out_proj, vectors, norm_gain, segment):
    inner_channel_width = inner_projection_weight.shape[0]
    square_mean = lax.optimization_barrier(jnp.mean(tokens * tokens, axis=-1, keepdims=True))
    hidden = low(tokens * lax.rsqrt(square_mean + NORM_EPS) * norm_gain)
    mixed = lowered_backward(jnp.einsum('gld,fd->glf', hidden, in_proj, precision=PRECISION_HIGH))
    x_part = mixed[..., :inner_channel_width]
    gate_in = mixed[..., inner_channel_width:]
    conv_pre = vectors[KCONV]
    for lag_index in range(KCONV):
        conv_pre = conv_pre + vectors[lag_index] * delayed(x_part, lag_index) * same_lag(segment, lag_index)[..., None]
    scan_input_value = low(jax.nn.silu(conv_pre))
    projected_values = lowered_backward(jnp.einsum('tau,us->tas', scan_input_value, inner_projection_weight, precision=PRECISION_HIGH))
    dt_low = low(projected_values[..., :DTRANK])
    b_rows = projected_values[..., DTRANK:DTRANK + DSTATE]
    c_rows = projected_values[..., DTRANK + DSTATE:]
    dt_pre = lowered_backward(jnp.einsum('glr,er->gle', dt_low, dt_proj, precision=PRECISION_HIGH)) + vectors[KCONV + 1]
    delta = jax.nn.softplus(dt_pre)
    a_matrix = -jnp.exp(vectors[KCONV + 3:])
    scanned = selective(delta, b_rows, c_rows, scan_input_value, same_lag(segment, 1), a_matrix)
    y_state = scanned + vectors[KCONV + 2] * scan_input_value
    gated = low(y_state * jax.nn.silu(gate_in))
    return tokens + jnp.einsum('gle,ed->gld', gated, out_proj, precision=PRECISION_HIGH)

def orthogonal(moment):
    scale = jnp.sqrt(jnp.sum(moment * moment)) + FROB_EPS
    current = rounded(moment / scale)
    for step_index in range(NS_STEPS):
        gram = rounded(jnp.dot(current.T, current, precision=PRECISION_HIGH))
        square = jnp.dot(gram, gram, precision=PRECISION_HIGH)
        poly = rounded(COEF_B * gram + COEF_C * square)
        current = rounded(COEF_A * current + jnp.dot(current, poly, precision=PRECISION_HIGH))
    return current

def muon_update(weight, moment, grad, fan):
    moment_new = MOMENTUM * moment + grad
    rate = 0.5 * math.sqrt(weight.shape[0] / fan)
    return ((1.0 - SHRINK) * weight - rate * orthogonal(moment_new), moment_new)

def adamw_update(param, first, second, grad):
    first_new = FIRST_MOMENT_BETA * first + (1.0 - FIRST_MOMENT_BETA) * grad
    second_new = BETA_SECOND * second + (1.0 - BETA_SECOND) * grad * grad
    first_hat = first_new / (1.0 - FIRST_MOMENT_BETA ** STEP_NO)
    second_hat = second_new / (1.0 - BETA_SECOND ** STEP_NO)
    param_new = param * (1.0 - ADAM_RATE * ADAM_DECAY) - ADAM_RATE * first_hat / (jnp.sqrt(second_hat) + ADAM_EPS)
    return (param_new, first_new, second_new)

def reference(tokens, out_grad, doc_lengths, in_proj, inner_projection_weight, dt_proj, out_proj, in_moment, x_moment, dt_moment, out_moment, vectors, vector_first, vector_second, norm_gain, gain_first, gain_second):
    masters = (in_proj, inner_projection_weight, dt_proj, out_proj, vectors, norm_gain)
    lowered = tuple((rounded(master) for master in masters))
    row_total, length, width = tokens.shape
    group = math.gcd(row_total, max(1, 4096 // length))
    count = row_total // group
    inputs = tokens.astype(jnp.float32).reshape(count, group, length, width)
    cotangents = out_grad.astype(jnp.float32).reshape(count, group, length, width)
    lengths = doc_lengths.reshape(count, group, NDOC)

    def one_group(totals, item):
        x_group, dy_group, len_group = item
        segment = segment_ids(len_group, length)

        def apply(x_in, *weights):
            return forward(x_in, *weights, segment)
        y_group, pull = jax.vjp(apply, x_group, *lowered)
        grads = pull(dy_group)
        new_totals = tuple((total_part + new_part for total_part, new_part in zip(totals, grads[1:])))
        return (new_totals, (y_group, grads[0]))
    zeros = tuple((jnp.zeros_like(weight) for weight in lowered))
    totals, (y_all, dx_all) = lax.scan(one_group, zeros, (inputs, cotangents, lengths))
    block_out = y_all.reshape(row_total, length, width)
    grad_tokens = dx_all.reshape(row_total, length, width)
    in_new, in_mom = muon_update(in_proj, in_moment, totals[0], DMODEL)
    x_new, x_mom = muon_update(inner_projection_weight, x_moment, totals[1], DINNER)
    dt_new, dt_mom = muon_update(dt_proj, dt_moment, totals[2], DTRANK)
    out_new, out_mom = muon_update(out_proj, out_moment, totals[3], DINNER // 8)
    vec_new, vec_first, vec_second = adamw_update(vectors, vector_first, vector_second, totals[4])
    gain_new, gain_m, gain_v = adamw_update(norm_gain, gain_first, gain_second, totals[5])
    return (block_out, grad_tokens, in_new, in_mom, x_new, x_mom, dt_new, dt_mom, out_new, out_mom, vec_new, vec_first, vec_second, gain_new, gain_m, gain_v)
```

```python
import functools
import math

import jax
import jax.numpy as jnp
from jax import lax
from jax.experimental import pallas as pl
from jax.experimental.pallas import tpu as pltpu
from jax.sharding import PartitionSpec as P

DMODEL = 1024
DINNER = 2048
DSTATE = 16
DTRANK = 64
KCONV = 4
NS_STEPS = 4
STEP_NO = 10


NORM_EPS = 1e-05
FROB_EPS = 1e-07
COEF_A = 3.4445
COEF_B = -4.775
COEF_C = 2.0315
MOMENTUM = 0.95
SHRINK = 0.001
FIRST_MOMENT_BETA = 0.9
BETA_SECOND = 0.95
ADAM_EPS = 1e-08
ADAM_RATE = 1.0
ADAM_DECAY = 0.001


def contract(left, right, left_dim, right_dim):
    return lax.dot_general(
        left, right, (((left_dim,), (right_dim,)), ((), ())), preferred_element_type=jnp.float32
    )


MESH = pl.DeviceIdType.MESH
LANES = 128
SUBS = 8
PASS = LANES * SUBS
STEPS = 4
RESET = 1.0e4
LOG2E = math.log2(math.e)
LN2 = math.log(2.0)
TAPS = DSTATE
CBIAS = TAPS + KCONV
DTBIAS = CBIAS + 1
SKIP = CBIAS + 2
GAIN = CBIAS + 3
VECS = CBIAS + 4
CHUNKS = 16
BAND = 512
SMALL_COLUMNS = 2 * LANES
VEC_AT = LANES + DTRANK


def lane_tile(j):
    return pl.ds(j * LANES, LANES)


def scan_kernel(
    bc_ref,
    proj_ref,
    masks_ref,
    dtw_ref,
    u_ref,
    gate_ref,
    tokens_ref,
    cot_ref,
    outw_ref,
    vec_ref,
    dgate_ref,
    du_ref,
    ddt_ref,
    gsum_ref,
    gamat_ref,
    dbc_ref,
    gout_ref,
    block_ref,
    gated_s,
    amat_s,
    gamat_s,
    pre_s,
    dg_s,
    delta_s,
    dec_s,
    drive_s,
    dstate_s,
    y_s,
    pull_s,
    ddelta_s,
    states,
    prod_a,
    prod_b,
    sums_b,
    sums_c,
):
    length = u_ref.shape[0]
    half = pl.program_id(0)
    bias_row = vec_ref[DTBIAS : DTBIAS + 1, :]

    pre_s[...] = contract(proj_ref[...].astype(jnp.bfloat16), dtw_ref[...], 1, 1) + bias_row
    dg_s[...] = contract(cot_ref[...], outw_ref[...], 1, 1)

    for j in range(SUBS):
        rates = -LOG2E * jnp.exp(vec_ref[0:DSTATE, j * LANES : (j + 1) * LANES])
        amat_s[pl.ds(j, DSTATE, stride=SUBS), :] = rates

    def amat_of(n):
        return amat_s[n * SUBS : (n + 1) * SUBS, :]

    rows = 16

    def prepare(i, carry):
        r = pl.multiple_of(i * rows, rows)
        keep = masks_ref[pl.ds(r, rows), 1:2] > 0.0
        for j in range(SUBS):
            at = (pl.ds(r, rows), lane_tile(j))
            delta = jax.nn.softplus(pre_s[at])
            u = u_ref[at].astype(jnp.float32)
            gate = gate_ref[at]
            delta_s[at] = delta
            to = (pl.ds(r * SUBS + j, rows, stride=SUBS), slice(None))
            dec_s[to] = jnp.where(keep, delta, RESET)
            drive_s[to] = delta * u
            dstate_s[to] = dg_s[at] * (gate * jax.nn.sigmoid(gate))
        return carry

    lax.fori_loop(0, length // rows, prepare, 0)

    for n in range(DSTATE):
        states[n] = jnp.zeros((SUBS, LANES), jnp.float32)

    def tile_of(ref, t):
        return ref[pl.ds(pl.multiple_of(t * SUBS, SUBS), SUBS), :]

    def put_tile(ref, t, value):
        ref[pl.ds(pl.multiple_of(t * SUBS, SUBS), SUBS), :] = value

    def ahead(i, carry):
        state = list(carry)
        for k in range(STEPS):
            t = i * STEPS + k
            dec, drive = tile_of(dec_s, t), tile_of(drive_s, t)
            parts = [None, None]
            for n in range(DSTATE):
                s = jnp.exp2(dec * amat_of(n)) * state[n] + drive * bc_ref[t, DTRANK + n]
                state[n] = s
                states[(t + 1) * DSTATE + n] = s
                term = s * bc_ref[t, DTRANK + DSTATE + n]
                parts[n % 2] = term if parts[n % 2] is None else parts[n % 2] + term
            put_tile(y_s, t, parts[0] + parts[1])
        return tuple(state)

    zero = jnp.zeros((SUBS, LANES), jnp.float32)
    lax.fori_loop(0, length // STEPS, ahead, (zero,) * DSTATE)

    pick = (
        lax.broadcasted_iota(jnp.int32, (2 * DSTATE, 2 * LANES), 1) // SUBS
        == lax.broadcasted_iota(jnp.int32, (2 * DSTATE, 2 * LANES), 0)
    ).astype(jnp.bfloat16)
    span = DSTATE * SUBS

    def channel_sums(products, t0):
        for k in range(0, STEPS, 2):
            block = products[k * span : (k + 2) * span, :]
            row = pl.multiple_of((t0 + k) * DSTATE, 2 * DSTATE)
            both = jnp.dot(pick, block, preferred_element_type=jnp.float32)
            sums_b[pl.ds(row, 2 * DSTATE), :] = both[:, 0:LANES]
            sums_c[pl.ds(row, 2 * DSTATE), :] = both[:, LANES : 2 * LANES]

    def behind_steps(t0, products, flow, g_amat):
        for k in reversed(range(STEPS)):
            t = t0 + k
            dec, drive, dstate = tile_of(dec_s, t), tile_of(drive_s, t), tile_of(dstate_s, t)
            pull, back = [None, None], [None, None]
            pend_b, pend_c = None, None
            for n in range(DSTATE):
                amat = amat_of(n)
                adj = dstate * bc_ref[t, DTRANK + DSTATE + n] + flow[n]
                term = adj * bc_ref[t, DTRANK + n]
                pull[n % 2] = term if pull[n % 2] is None else pull[n % 2] + term
                flow[n] = jnp.exp2(dec * amat) * adj
                weighted = flow[n] * states[t * DSTATE + n]
                g_amat[n] = g_amat[n] + weighted * dec
                term = weighted * amat
                back[n % 2] = term if back[n % 2] is None else back[n % 2] + term
                prod_b_n = adj * drive
                prod_c_n = states[(t + 1) * DSTATE + n] * dstate
                if n % 2:
                    row = k * span + (n - 1) * SUBS
                    products[row : row + 2 * SUBS, 0:LANES] = jnp.concatenate(
                        [pend_b, prod_b_n], axis=0
                    ).astype(jnp.bfloat16)
                    products[row : row + 2 * SUBS, LANES : 2 * LANES] = jnp.concatenate(
                        [pend_c, prod_c_n], axis=0
                    ).astype(jnp.bfloat16)
                pend_b, pend_c = prod_b_n, prod_c_n
            put_tile(pull_s, t, pull[0] + pull[1])
            put_tile(ddelta_s, t, back[0] + back[1])

    groups = length // (2 * STEPS)

    def behind(i, carry):
        flow, g_amat = list(carry[0]), list(carry[1])
        t1 = length - (2 * i + 1) * STEPS
        channel_sums(prod_b, t1 + STEPS)
        behind_steps(t1, prod_a, flow, g_amat)
        channel_sums(prod_a, t1)
        behind_steps(t1 - STEPS, prod_b, flow, g_amat)
        return (tuple(flow), tuple(g_amat))

    unused, g_amat = lax.fori_loop(0, groups, behind, ((zero,) * DSTATE, (zero,) * DSTATE))
    channel_sums(prod_b, 0)
    for n in range(DSTATE):
        gamat_s[n * SUBS : (n + 1) * SUBS, :] = g_amat[n]
    for j in range(SUBS):
        cols = slice(j * LANES, (j + 1) * LANES)
        of_rates = gamat_s[pl.ds(j, DSTATE, stride=SUBS), :]
        gamat_ref[:, cols] = of_rates * -jnp.exp(vec_ref[0:DSTATE, cols])

    line = lax.broadcasted_iota(jnp.int32, (2 * LANES, LANES), 0)
    column = lax.broadcasted_iota(jnp.int32, (2 * LANES, LANES), 1)
    first = line < LANES
    total = jnp.zeros((length, LANES), jnp.float32)
    for n in range(DSTATE):
        goes = jnp.where(first, DTRANK + n, DTRANK + DSTATE + n) == column
        goes = goes.astype(jnp.bfloat16)
        for side, sums in enumerate((sums_b, sums_c)):
            value = sums[pl.ds(n, length, stride=DSTATE), :]
            upper = value.astype(jnp.bfloat16)
            lower = (value - upper.astype(jnp.float32)).astype(jnp.bfloat16)
            part = goes[side * LANES : (side + 1) * LANES, :]
            total = total + jnp.dot(upper, part, preferred_element_type=jnp.float32)
            total = total + jnp.dot(lower, part, preferred_element_type=jnp.float32)

    @pl.when(half == 0)
    def _():
        dbc_ref[...] = total

    @pl.when(half > 0)
    def _():
        dbc_ref[...] += total

    gsum_ref[...] = jnp.zeros_like(gsum_ref)

    def finish(i, carry):
        r = pl.multiple_of(i * rows, rows)
        for j in range(SUBS):
            at = (pl.ds(r, rows), lane_tile(j))
            of = (pl.ds(r * SUBS + j, rows, stride=SUBS), slice(None))
            skip = vec_ref[SKIP : SKIP + 1, j * LANES : (j + 1) * LANES]
            u = u_ref[at].astype(jnp.float32)
            gate = gate_ref[at]
            sig = jax.nn.sigmoid(gate)
            act = gate * sig
            dg = dg_s[at]
            y = y_s[of] + skip * u
            gated_s[at] = (y * act).astype(jnp.bfloat16)
            dgate_ref[at] = (dg * y * sig * (1.0 + gate * (1.0 - sig))).astype(jnp.bfloat16)
            dstate = dg * act
            pull = pull_s[of]
            du_ref[at] = dstate * skip + pull * delta_s[at]
            ddt = (ddelta_s[of] * LN2 + pull * u) * jax.nn.sigmoid(pre_s[at])
            ddt_ref[at] = ddt.astype(jnp.bfloat16)
            cols = slice(j * LANES, (j + 1) * LANES)
            g_skip = dstate * u
            gsum_ref[0:8, cols] += g_skip[0:8] + g_skip[8:16]
            gsum_ref[8:16, cols] += ddt[0:8] + ddt[8:16]
        return carry

    lax.fori_loop(0, length // rows, finish, 0)

    for b in range(0, PASS, BAND):
        strip = slice(b, b + BAND)
        gout_ref[strip, :] = contract(gated_s[:, strip], cot_ref[...], 0, 0).astype(jnp.bfloat16)
    through = jnp.dot(gated_s[...], outw_ref[...], preferred_element_type=jnp.float32)

    @pl.when(half == 0)
    def _():
        block_ref[...] = tokens_ref[...].astype(jnp.float32) + through

    @pl.when(half > 0)
    def _():
        block_ref[...] += through


def scan_both(proj, masks, dt_rows, u_low, gate_in, tokens, cotangent, out_low, vecs):
    length, inner = u_low.shape
    width = out_low.shape[1]
    by_channel = lambda h: (0, h)
    whole = lambda h: (0, 0)
    rows_of = lambda h: (h, 0)
    f32, b16 = jnp.float32, jnp.bfloat16
    return pl.pallas_call(
        scan_kernel,
        grid=(inner // PASS,),
        in_specs=[
            pl.BlockSpec(memory_space=pltpu.SMEM),
            pl.BlockSpec((length, LANES), whole),
            pl.BlockSpec((length, LANES), whole),
            pl.BlockSpec((PASS, LANES), rows_of),
            pl.BlockSpec((length, PASS), by_channel),
            pl.BlockSpec((length, PASS), by_channel),
            pl.BlockSpec((length, width), whole),
            pl.BlockSpec((length, width), whole),
            pl.BlockSpec((PASS, width), rows_of),
            pl.BlockSpec((VECS, PASS), by_channel),
        ],
        out_specs=[
            pl.BlockSpec((length, PASS), by_channel),
            pl.BlockSpec((length, PASS), by_channel),
            pl.BlockSpec((length, PASS), by_channel),
            pl.BlockSpec((16, PASS), by_channel),
            pl.BlockSpec((DSTATE, PASS), by_channel),
            pl.BlockSpec((length, LANES), whole),
            pl.BlockSpec((PASS, width), rows_of),
            pl.BlockSpec((length, width), whole),
        ],
        out_shape=[
            jax.ShapeDtypeStruct((length, inner), b16),
            jax.ShapeDtypeStruct((length, inner), f32),
            jax.ShapeDtypeStruct((length, inner), b16),
            jax.ShapeDtypeStruct((16, inner), f32),
            jax.ShapeDtypeStruct((DSTATE, inner), f32),
            jax.ShapeDtypeStruct((length, LANES), f32),
            jax.ShapeDtypeStruct((inner, width), b16),
            jax.ShapeDtypeStruct((length, width), f32),
        ],
        scratch_shapes=[
            pltpu.VMEM((length, PASS), b16),
            pltpu.VMEM((DSTATE * SUBS, LANES), f32),
            pltpu.VMEM((DSTATE * SUBS, LANES), f32),
        ]
        + [pltpu.VMEM((length, PASS), f32)] * 3
        + [pltpu.VMEM((length * SUBS, LANES), f32)] * 6
        + [
            pltpu.VMEM(((length + 1) * DSTATE, SUBS, LANES), f32),
            pltpu.VMEM((STEPS * DSTATE * SUBS, 2 * LANES), b16),
            pltpu.VMEM((STEPS * DSTATE * SUBS, 2 * LANES), b16),
            pltpu.VMEM(((length + STEPS) * DSTATE, LANES), f32),
            pltpu.VMEM(((length + STEPS) * DSTATE, LANES), f32),
        ],
        compiler_params=pltpu.CompilerParams(vmem_limit_bytes=60 * 1024 * 1024),
        cost_estimate=pl.CostEstimate(
            flops=24 * length * inner * DSTATE,
            bytes_accessed=24 * length * inner,
            transcendentals=2 * length * inner * DSTATE,
        ),
    )(proj, proj, masks, dt_rows, u_low, gate_in, tokens, cotangent, out_low, vecs)


def flipped(index, bit):
    return index + bit * (1 - 2 * lax.rem(lax.div(index, bit), 2))


ROUTES = 3


def each_mask(first, last, body):
    count = abs(last - first)
    sign = 1 if last > first else -1
    if count <= 4:
        for k in range(count):
            body(first + sign * k)
        return

    def step(k, carry):
        body(first + sign * k)
        return carry

    lax.fori_loop(0, count, step, 0)


def routes_of(width, share=4):
    tiles = width // LANES
    last = tiles // share
    counts = ((tiles - last + 1) // 2, (tiles - last) // 2, last)
    firsts = (0, counts[0], counts[0] + counts[1])
    return [(g, firsts[g] * LANES, counts[g] * LANES) for g in range(ROUTES) if counts[g]]


class Cube:
    def __init__(self, fsdp, ns):
        self.fsdp, self.ns = fsdp, ns
        self.shards, self.pieces, self.masks = fsdp * ns, fsdp * ns // 2, fsdp // 2
        order = [2 << k for k in range(fsdp.bit_length() - 2)]
        self.orders = (order, order[:-2] + [order[-1], order[-2]], order)
        self.places = len(order)
        self.row, self.col = lax.axis_index("fsdp"), lax.axis_index("ns")
        self.me = self.row * ns + self.col
        self.sibling = (flipped(self.row, 1), self.col)
        self.sibling_step = (flipped(self.row, 1) - self.row) * ns
        self.core = lax.rem(self.row, 2)
        self.above, self.below = (self.row, self.col + 1), (self.row, self.col - 1)
        self.has_above, self.has_below = self.col < ns - 1, self.col > 0
        self.half_row = lax.div(self.row, 2)
        moves = {bit: flipped(self.row, bit) - self.row for bit in order}
        halves = {bit: flipped(self.half_row, bit // 2) - self.half_row for bit in order}
        self.steps = [[moves[bit] for bit in bits] for bits in self.orders]
        self.half_steps = [[halves[bit] for bit in bits] for bits in self.orders]

    def partner(self, route, place):
        return (self.row + self.steps[route][place], self.col)

    def flips(self, mask, steps, start):
        for place, step in enumerate(steps):
            if isinstance(mask, int):
                start = start + step if mask >> place & 1 else start
            else:
                start = start + lax.rem(lax.div(mask, 1 << place), 2) * step
        return start

    def at(self, mask, col, route):
        return self.flips(mask, self.steps[route], self.row) * self.ns + col

    def spot(self, mask, col, route):
        return self.flips(mask, self.half_steps[route], self.half_row) * self.ns + col

    def wrapped(self, distance):
        col = self.col + distance
        return jnp.where(col < self.ns, col, col - self.ns)

    def greet(self, others=()):
        barrier = pltpu.get_barrier_semaphore()

        def signal(device):
            pl.semaphore_signal(barrier, inc=1, device_id=device, device_id_type=MESH)

        for place in range(self.places):
            signal(self.partner(0, place))
        signal(self.sibling)
        for other in others:
            signal(other)
        pl.when(self.has_above)(lambda: signal(self.above))
        pl.when(self.has_below)(lambda: signal(self.below))
        ends = jnp.where(self.has_above, 1, 0) + jnp.where(self.has_below, 1, 0)
        pl.semaphore_wait(barrier, self.places + 1 + len(others) + ends)

    def along_line(self, distance, step_to):
        pl.when(self.col - distance >= 0)(lambda: step_to(self.col - distance, "above"))
        pl.when(self.col + distance < self.ns)(lambda: step_to(self.col + distance, "below"))

    def upward(self, step, after=None, own=True, between=lambda: None, third=True):
        after = after or (lambda place, k: None)
        nothing, every, both = 0, range(self.places), ("above", "below")
        if own:
            step((0, 1, 2), nothing, self.col, both, every, True)
            after(-1, nothing)

        def along(d, carry):
            self.along_line(
                d, lambda col, way: step((0, 1), nothing, col, (way,), every, False)
            )
            after(-1, d)
            return carry

        lax.fori_loop(1, self.ns, along, 0)
        for place in every if third else ():
            later = range(place + 1, self.places)
            each_mask(
                1 << place,
                2 << place,
                lambda mask: step((2,), mask, self.col, both, later, False),
            )
        done = 1
        for place in every:
            between()
            later = range(place + 1, self.places)

            def of_mask(mask):
                def across(k, carry):
                    step((0, 1), mask, self.wrapped(k), (), later, False)
                    after(place, mask * self.ns + k)
                    return carry

                lax.fori_loop(0, self.ns, across, 0)

            each_mask(1 << place, 2 << place, of_mask)
            until = self.ns if place == self.places - 1 else min(done + 1, self.ns)
            if not third:
                continue

            def last(distance, carry):
                def of_mask(mask):
                    self.along_line(
                        distance, lambda col, way: step((2,), mask, col, (way,), (), False)
                    )

                each_mask(0, self.masks, of_mask)
                return carry

            lax.fori_loop(done, until, last, 0)
            done = until

    def down_stage(self, stage, step, after=None, third=True):
        after = after or (lambda place, k: None)
        nothing, every, both = 0, range(self.places), ("below", "above")
        source = {"above": ("below",), "below": ("above",)}
        if stage > self.places:
            step((0, 1, 2), nothing, self.col, None, both, every)
            return
        if stage == self.places:

            def along(k, carry):
                self.along_line(
                    self.ns - 1 - k,
                    lambda col, way: step((0, 1), nothing, col, other(way), source[other(way)], every),
                )
                after(-1, k)
                return carry

            lax.fori_loop(0, self.ns - 1, along, 0)
            for place in reversed(every if third else ()):
                later = range(place + 1, self.places)
                each_mask(
                    (2 << place) - 1,
                    (1 << place) - 1,
                    lambda mask: step((2,), mask, self.col, place, both, later),
                )
            return
        place = self.places - 1 - stage
        later = range(place + 1, self.places)

        def of_mask(mask):
            def across(i, carry):
                far = jnp.where(2 * self.col < self.ns, self.ns - 1 - i, 1 + i)
                far = jnp.where(far == self.ns, 0, far)
                step((0, 1), mask, self.wrapped(far), place, (), later)
                after(place, ((2 << place) - 1 - mask) * self.ns + i)
                return carry

            lax.fori_loop(0, self.ns, across, 0)

        each_mask((2 << place) - 1, (1 << place) - 1, of_mask)
        first = self.ns - 1 if stage == 0 else 1
        last = 2 if stage == 0 and self.places > 1 else 1

        def line_first(k, carry):
            def of_mask(mask):
                self.along_line(
                    first - k,
                    lambda col, way: step((2,), mask, col, other(way), source[other(way)], ()),
                )

            each_mask(self.masks - 1, -1, of_mask)
            return carry

        if stage < 2 and third:
            lax.fori_loop(0, first - last + 1, line_first, 0)

    def downward(self, step):
        for stage in range(self.places + 2):
            self.down_stage(stage, step)


def other(way):
    return "below" if way == "above" else "above"


def send(src, dst, send_sem, recv_sem, device):
    pltpu.make_async_remote_copy(
        src_ref=src,
        dst_ref=dst,
        send_sem=send_sem,
        recv_sem=recv_sem,
        device_id=device,
        device_id_type=MESH,
    ).start()


def await_bytes(ref, sem):
    pltpu.make_async_copy(ref, ref, sem).wait()


def pass_on(cube, route, mask, col, ways, places, source, target, send_sem, sem_of):
    if "above" in ways:
        pl.when(cube.has_above)(
            lambda: send(source, target, send_sem.at[1], sem_of(mask, col), cube.above)
        )
    if "below" in ways:
        pl.when(cube.has_below)(
            lambda: send(source, target, send_sem.at[2], sem_of(mask, col), cube.below)
        )
    for p in places:
        partner = cube.partner(route, p)
        send(source, target, send_sem.at[0], sem_of(mask + (1 << p), col), partner)


def await_passed(cube, route, ref, send_sem):
    many = cube.masks if route == 2 else 1
    crossed = cube.masks - 1 if route == 2 else cube.pieces - cube.ns
    await_bytes(ref.at[pl.ds(0, crossed)], send_sem.at[0])
    for col in range(cube.ns):

        @pl.when(cube.col == col)
        def _():
            if col + 1 < cube.ns:
                await_bytes(ref.at[pl.ds(0, many * (col + 1))], send_sem.at[1])
            if col:
                await_bytes(ref.at[pl.ds(0, many * (cube.ns - col))], send_sem.at[2])


def gather_step(cube, ins, outs, sems):
    send_sem, recv_sem, pair_send, pair_sem = sems

    def step(routes, mask, col, ways, places, own):
        for a, (mine, out) in enumerate(zip(ins, outs)):
            for route, first, count in routes_of(mine.shape[1]):
                if route not in routes:
                    continue
                cols = pl.ds(first, count)
                block = out.at[cube.at(mask, col, route), :, cols]

                def sem_of(mask, col):
                    return recv_sem.at[a, route, mask, col]

                if not own:
                    await_bytes(block, sem_of(mask, col))
                source = mine.at[:, cols] if own else block
                pass_on(
                    cube, route, mask, col, ways, places, source, block, send_sem.at[a, route], sem_of
                )
                send(source, block, pair_send.at[a], pair_sem.at[a], cube.sibling)

    return step


def own_step(cube, step):
    step((0, 1, 2), 0, cube.col, ("above", "below"), range(cube.places), True)


def front_kernel(
    fsdp,
    ns,
    per_device,
    gains,
    lengths_ref,
    tokens_ref,
    in_ref,
    out_ref,
    x_own,
    dt_own,
    vectors_own,
    gain_own,
    all_in,
    all_out,
    x_rows,
    dt_rows,
    vec_ref,
    gain_ref,
    xpart_far,
    gate_far,
    upre_far,
    u_far,
    proj_ref,
    masks_ref,
    hidden_ref,
    inverse_ref,
    xpart_ref,
    gate_ref,
    upre_ref,
    u_ref,
    away_sem,
    normed_s,
    in_all,
    small_all,
    in_low,
    out_low,
    small_ref,
    small_s,
    x_s,
    dt_s,
    mask_s,
    own_sem,
    send_sem,
    recv_sem,
    pair_send,
    pair_sem,
    send_out,
    recv_out,
    give_out,
    pair_out,
):
    cube = Cube(fsdp, ns)
    length, width = tokens_ref.shape
    in_low[...] = in_ref[...].astype(jnp.bfloat16)
    out_low[...] = out_ref[...].astype(jnp.bfloat16)
    small_s[...] = jnp.zeros_like(small_s)
    small_s[0:per_device, 0 : x_own.shape[1]] = x_own[...]
    small_s[0:per_device, LANES : LANES + dt_own.shape[1]] = dt_own[...]
    small_s[0:DSTATE, VEC_AT : VEC_AT + per_device] = vectors_own[KCONV + 3 :, :]
    small_s[DSTATE:GAIN, VEC_AT : VEC_AT + per_device] = vectors_own[0 : KCONV + 3, :]
    small_s[GAIN:VECS, VEC_AT : VEC_AT + gains] = gain_own[...]
    small_ref[...] = small_s[...].astype(jnp.bfloat16)
    cube.greet()
    first = gather_step(
        cube, (in_low, small_ref), (in_all, small_all), (send_sem, recv_sem, pair_send, pair_sem)
    )
    later = gather_step(cube, (out_low,), (all_out,), (send_out, recv_out, give_out, pair_out))
    own_step(cube, first)
    in_all[cube.me] = in_low[...]
    small_all[cube.me] = small_ref[...]
    own = pltpu.make_async_copy(out_low, all_out.at[cube.me], own_sem.at[0])
    own.start()

    place = lax.broadcasted_iota(jnp.int32, (length, LANES), 0)
    lane = lax.broadcasted_iota(jnp.int32, (length, LANES), 1)
    masks = jnp.ones((length, LANES), jnp.float32)
    for k in range(1, KCONV):
        same = place >= k
        start = jnp.int32(0)
        for d in range(lengths_ref.shape[1]):
            inside = jnp.logical_and(place >= start, place - k < start)
            same = jnp.logical_and(same, jnp.logical_not(inside))
            start = start + lengths_ref[0, d]
        mask_s[k - 1] = jnp.where(same, 1.0, 0.0)
        masks = jnp.where(lane == k, mask_s[k - 1], masks)
    masks_ref[...] = masks

    stage = [0]

    def between():
        stage[0] += 1
        if stage[0] == cube.places:
            own_step(cube, later)

    tokens = tokens_ref[...].astype(jnp.float32)
    inverse = lax.rsqrt(jnp.mean(tokens * tokens, axis=-1, keepdims=True) + NORM_EPS)
    normed_s[...] = tokens * inverse
    inverse_ref[...] = jnp.broadcast_to(inverse, inverse_ref.shape)
    cube.upward(first, own=False, between=between)
    for a, out in enumerate((in_all, small_all)):
        await_bytes(out.at[pl.ds(0, cube.pieces)], pair_sem.at[a])
    keep_in = pltpu.make_async_copy(in_all, all_in, own_sem.at[1])
    keep_in.start()

    def unpack(d, carry):
        at = pl.ds(pl.multiple_of(d * per_device, per_device), per_device)
        x_s[at, :] = small_all[d, 0:per_device, 0:LANES].astype(jnp.float32)
        both = small_all[d, 0:per_device, LANES : 2 * LANES].astype(jnp.float32)
        own_lanes = lax.broadcasted_iota(jnp.int32, both.shape, 1) < DTRANK
        dt_s[at, :] = jnp.where(own_lanes, both, 0.0)
        return carry

    lax.fori_loop(0, cube.shards, unpack, 0)
    x_rows[...] = x_s[...].astype(jnp.bfloat16)
    dt_rows[...] = dt_s[...].astype(jnp.bfloat16)
    for d in range(cube.shards):
        block = small_all[d, 0:32, LANES : 2 * LANES].astype(jnp.float32)[:, DTRANK:]
        vec_ref[:, d * per_device : (d + 1) * per_device] = block[0:VECS, 0:per_device]
        gain_ref[:, d * gains : (d + 1) * gains] = block[GAIN : GAIN + 1, 0:gains]

    hidden_ref[...] = (normed_s[...] * gain_ref[...]).astype(jnp.bfloat16)
    span = 2 * x_s.shape[0] // CHUNKS
    group = cube.shards // CHUNKS

    def mixed_of(chunk, many):
        weights = in_all[pl.ds(chunk * group, many * group)].reshape(many * span, width)
        return contract(hidden_ref[...], weights, 1, 1)

    def x_block(i, carry):
        cols = pl.ds(pl.multiple_of(2 * i * span, 2 * span), 2 * span)
        xpart_ref[:, cols] = mixed_of(2 * i, 2)
        return carry

    lax.fori_loop(0, CHUNKS // 4, x_block, 0)

    def x_chunk(chunk):
        base = pl.multiple_of(chunk * span, span)
        for j in range(span // LANES):
            cols = pl.ds(pl.multiple_of(base + j * LANES, LANES), LANES)
            x = xpart_ref[:, cols]
            upre = vec_ref[CBIAS : CBIAS + 1, cols] + vec_ref[TAPS : TAPS + 1, cols] * x
            for k in range(1, KCONV):
                moved = pltpu.roll(x, k, 0) * mask_s[k - 1]
                upre = upre + vec_ref[TAPS + k : TAPS + k + 1, cols] * moved
            upre_ref[:, cols] = upre
            u_ref[:, cols] = (upre * jax.nn.sigmoid(upre)).astype(jnp.bfloat16)

    def gate_chunk(chunk):
        base = pl.multiple_of((chunk - CHUNKS // 2) * span, span)
        gate_ref[:, pl.ds(base, span)] = mixed_of(chunk, 1)

    away = [
        pltpu.make_async_copy(source, target, away_sem.at[k])
        for k, (source, target) in enumerate(
            ((xpart_ref, xpart_far), (upre_ref, upre_far), (u_ref, u_far), (gate_ref, gate_far))
        )
    ]
    away[0].start()
    seen = [0]

    def halfway():
        seen[0] += 1
        if seen[0] == cube.places:
            away[1].start()
            away[2].start()

    every = cube.pieces // CHUNKS

    def work(place, k):
        run = gate_chunk if place == cube.places - 1 else x_chunk
        if every == 1:
            run(k)
        else:

            @pl.when(lax.rem(k, every) == 0)
            def _():
                run(lax.div(k, every))

    work(-1, jnp.int32(0))
    cube.upward(later, work, own=False, between=halfway)
    away[3].start()
    proj_ref[...] = jnp.dot(u_ref[...], x_rows[...], preferred_element_type=jnp.float32)
    own.wait()
    keep_in.wait()
    for copy in away:
        copy.wait()
    await_bytes(all_out.at[pl.ds(0, cube.pieces)], pair_out.at[0])
    sent = [
        (in_all, send_sem.at[0], pair_send.at[0]),
        (small_all, send_sem.at[1], pair_send.at[1]),
        (all_out, send_out.at[0], give_out.at[0]),
    ]
    for ref, sems, pair in sent:
        await_bytes(ref.at[pl.ds(0, cube.pieces)], pair)
        for route, start, count in routes_of(ref.shape[2]):
            await_passed(cube, route, ref.at[:, :, pl.ds(start, count)], sems.at[route])


def small_rows(per_device):
    return -(-max(per_device, VECS) // 16) * 16


def gather_and_front(lengths, tokens, params, fsdp, ns):
    shards = fsdp * ns
    length, width = tokens.shape
    in_proj, out_proj, x_own, unused, unused, gain = params
    per_device, gains = x_own.shape[0], gain.shape[1]
    inner = per_device * shards
    small = (small_rows(per_device), SMALL_COLUMNS)
    f32, b16 = jnp.float32, jnp.bfloat16
    held = pl.BlockSpec(memory_space=pltpu.VMEM)
    far = pl.BlockSpec(memory_space=pl.ANY)

    def shape(*dims, dtype=f32):
        return jax.ShapeDtypeStruct(dims, dtype)

    return pl.pallas_call(
        functools.partial(front_kernel, fsdp, ns, per_device, gains),
        in_specs=[pl.BlockSpec(memory_space=pltpu.SMEM)] + [held] * 7,
        out_specs=[far] * 2 + [held] * 4 + [far] * 4 + [held] * 4,
        out_shape=[
            shape(shards, *in_proj.shape, dtype=b16),
            shape(shards, *out_proj.shape, dtype=b16),
            shape(inner, LANES, dtype=b16),
            shape(inner, LANES, dtype=b16),
            shape(VECS, inner),
            shape(1, width),
            shape(length, inner),
            shape(length, inner),
            shape(length, inner),
            shape(length, inner, dtype=b16),
            shape(length, LANES),
            shape(length, LANES),
            shape(length, width, dtype=b16),
            shape(length, LANES),
        ],
        scratch_shapes=[
            pltpu.VMEM((length, inner), f32),
            pltpu.VMEM((length, inner), f32),
            pltpu.VMEM((length, inner), f32),
            pltpu.VMEM((length, inner), b16),
            pltpu.SemaphoreType.DMA((4,)),
            pltpu.VMEM((length, width), f32),
            pltpu.VMEM((shards,) + in_proj.shape, b16),
            pltpu.VMEM((shards,) + small, b16),
            pltpu.VMEM(in_proj.shape, b16),
            pltpu.VMEM(out_proj.shape, b16),
            pltpu.VMEM(small, b16),
            pltpu.VMEM(small, f32),
            pltpu.VMEM((inner, LANES), f32),
            pltpu.VMEM((inner, LANES), f32),
            pltpu.VMEM((KCONV - 1, length, LANES), f32),
            pltpu.SemaphoreType.DMA((2,)),
            pltpu.SemaphoreType.DMA((2, ROUTES, 3)),
            pltpu.SemaphoreType.DMA((2, ROUTES, fsdp // 2, ns)),
            pltpu.SemaphoreType.DMA((2,)),
            pltpu.SemaphoreType.DMA((2,)),
            pltpu.SemaphoreType.DMA((1, ROUTES, 3)),
            pltpu.SemaphoreType.DMA((1, ROUTES, fsdp // 2, ns)),
            pltpu.SemaphoreType.DMA((1,)),
            pltpu.SemaphoreType.DMA((1,)),
        ],
        compiler_params=pltpu.CompilerParams(
            collective_id=0, has_side_effects=True, vmem_limit_bytes=56 * 1024 * 1024
        ),
    )(lengths, tokens, *params)


def slots_of(cube, route):
    if route == 2:

        def over(mask, col):
            if isinstance(mask, int):
                return (2 * cube.masks + mask // cube.ns, mask % cube.ns)
            return (2 * cube.masks + lax.div(mask, cube.ns), lax.rem(mask, cube.ns))

        below = lambda mask, col: (mask, col)
        above = lambda mask, col: (cube.masks + mask, col)
        return (below, above, over, cube.masks)
    return (
        lambda mask, col: (0, col),
        lambda mask, col: (1, col),
        lambda mask, col: (mask + 1, col),
        1,
    )


def slot_count(fsdp, ns, route):
    masks = fsdp // 2
    return 2 * masks + -(-masks // ns) if route == 2 else masks + 1


def clear_ends(cube, route, land):
    many = slots_of(cube, route)[3]

    def clear(first):
        ref = land.at[pl.ds(first, many)]
        ref[...] = jnp.zeros_like(ref)

    pl.when(jnp.logical_not(cube.has_below))(lambda: clear(0))
    pl.when(jnp.logical_not(cube.has_above))(lambda: clear(many))


def arrivals(cube, route, mask, col, lines, places, wait):
    below, above, over, unused = slots_of(cube, route)
    slots = [over(mask + (1 << p), col) for p in places]
    for slot in slots:
        wait(slot)
    if "below" in lines:
        pl.when(cube.has_below)(lambda: wait(below(mask, col)))
        slots.append(below(mask, col))
    if "above" in lines:
        pl.when(cube.has_above)(lambda: wait(above(mask, col)))
        slots.append(above(mask, col))
    return slots


def hand_on(cube, route, mask, col, to, give):
    below, above, over, unused = slots_of(cube, route)
    if to == "above":
        give(below(mask, col), cube.above)
    elif to == "below":
        give(above(mask, col), cube.below)
    elif to is not None:
        give(over(mask, col), cube.partner(route, to))


def scatter_steps(cube, parts, sums, pairs, lands, sems):
    send_sem, recv_sem, pair_sem = sems

    def pieces(routes):
        for a, part in enumerate(parts):
            for k, (route, first, count) in enumerate(routes_of(part.shape[2])):
                if route in routes:
                    yield (a, route, pl.ds(first, count), pairs[a][k], lands[a][k])

    def give_pair(routes, mask, col, to, lines, places):
        for a, route, cols, pair, unused in pieces(routes):
            index = cube.at(mask, col, route) + cube.sibling_step
            send(
                parts[a].at[index, :, cols],
                pair.at[mask, col],
                send_sem.at[a],
                pair_sem.at[a, route, mask, col],
                cube.sibling,
            )

    def step(routes, mask, col, to, lines, places):
        for a, route, cols, pair, land in pieces(routes):
            index = cube.at(mask, col, route)
            rows = parts[a].shape[1]
            await_bytes(pair.at[mask, col], pair_sem.at[a, route, mask, col])

            def wait(slot):
                await_bytes(land.at[slot], recv_sem.at[(a, route) + slot])

            slots = arrivals(cube, route, mask, col, lines, places, wait)
            deep = min(rows, 16)
            for r in range(0, rows, deep):
                at = pl.ds(r, deep)
                total = parts[a][index, at, cols].astype(jnp.float32)
                total = total + pair[mask, col, at, :].astype(jnp.float32)
                for slot in slots:
                    total = total + land[slot + (at, slice(None))].astype(jnp.float32)
                if to is not None:
                    pair[mask, col, at, :] = total.astype(jnp.bfloat16)
                else:
                    sums[a][at, cols] = total

            def give(slot, device):
                send(
                    pair.at[mask, col],
                    land.at[slot],
                    send_sem.at[a],
                    recv_sem.at[(a, route) + slot],
                    device,
                )

            hand_on(cube, route, mask, col, to, give)

    return (give_pair, step)


def back_kernel(
    fsdp,
    ns,
    per_device,
    far,
    inverse_ref,
    masks_ref,
    proj_ref,
    x_rows,
    dt_rows,
    vec_ref,
    gain_ref,
    gsum_ref,
    gamat_ref,
    dbc_ref,
    all_in,
    dtok_ref,
    ggain_ref,
    sum_in,
    sum_out,
    sum_small,
    sum_vec,
    near,
    near_sem,
    part_in,
    part_small,
    small_s,
    pair_in,
    pair_out,
    pair_small,
    land_in,
    land_out,
    land_small,
    dx_s,
    dhidden_s,
    weights,
    mask_s,
    dproj_s,
    dtin_s,
    du_s,
    gx_s,
    gdt_s,
    last_s,
    load_sem,
    send_first,
    recv_first,
    pair_first,
    send_sem,
    recv_sem,
    pair_sem,
):
    copies = [
        pltpu.make_async_copy(source, target, near_sem.at[k])
        for k, (source, target) in enumerate(zip(far, near))
    ]
    for copy in copies:
        copy.start()
    (
        gout_ref,
        dgate_ref,
        hidden_ref,
        ddt_ref,
        du_ref,
        u_ref,
        upre_ref,
        xpart_ref,
        tokens_ref,
        cot_ref,
    ) = near
    cube = Cube(fsdp, ns)
    length, width = tokens_ref.shape
    inner = x_rows.shape[0]
    cube.greet()
    give_out, step_out = scatter_steps(
        cube, (gout_ref,), (sum_out,), (pair_out,), (land_out,), (send_first, recv_first, pair_first)
    )
    give_in, step_in = scatter_steps(
        cube,
        (part_in, part_small),
        (sum_in, sum_small),
        (pair_in, pair_small),
        (land_in, land_small),
        (send_sem, recv_sem, pair_sem),
    )
    copies[0].wait()
    cube.downward(give_out)
    for part, land in ((gout_ref, land_out), (part_in, land_in), (part_small, land_small)):
        for (route, unused, unused), where in zip(routes_of(part.shape[2]), land):
            clear_ends(cube, route, where)

    group = BAND // part_in.shape[1]

    def into_part(first, source):
        def band(i, carry):
            cols = pl.ds(pl.multiple_of(i * BAND, BAND), BAND)
            gradient = contract(source[:, cols], hidden_ref[...], 0, 0).astype(jnp.bfloat16)
            at = pl.ds(first + i * group, group)
            part_in[at] = gradient.reshape(group, part_in.shape[1], width)
            return carry

        lax.fori_loop(0, inner // BAND, band, 0)

    for copy in copies[1:3]:
        copy.wait()
    into_part(cube.shards // 2, dgate_ref)
    for k in range(1, KCONV):
        mask_s[k - 1] = jnp.broadcast_to(masks_ref[:, k : k + 1], (length, LANES))
    for copy in copies[3:]:
        copy.wait()
    d_dtin = jnp.dot(ddt_ref[...], dt_rows[...], preferred_element_type=jnp.float32)
    dproj_s[...] = (d_dtin + dbc_ref[...]).astype(jnp.bfloat16)
    lane = lax.broadcasted_iota(jnp.int32, (length, LANES), 1)
    dtin_s[...] = jnp.where(lane < DTRANK, proj_ref[...], 0.0).astype(jnp.bfloat16)
    sub = lax.broadcasted_iota(jnp.int32, (SUBS, LANES), 0)

    def state_band(i, carry):
        at = pl.ds(pl.multiple_of(i * BAND, BAND), BAND)
        du_s[:, at] = du_ref[:, at] + contract(dproj_s[...], x_rows[at, :], 1, 1)
        gx_s[at, :] = contract(u_ref[:, at], dproj_s[...], 0, 0)
        gdt_s[at, :] = contract(ddt_ref[:, at], dtin_s[...], 0, 0)
        return carry

    lax.fori_loop(0, inner // BAND, state_band, 0)

    def x_chunk(chunk):
        cols = pl.ds(pl.multiple_of(chunk * LANES, LANES), LANES)
        x, upre = xpart_ref[:, cols], upre_ref[:, cols]
        sig = jax.nn.sigmoid(upre)
        dpre = du_s[:, cols] * sig * (1.0 + upre * (1.0 - sig))
        dx = vec_ref[TAPS : TAPS + 1, cols] * dpre
        sums = [jnp.sum(dpre * x, axis=0, keepdims=True)]
        for k in range(1, KCONV):
            masked = mask_s[k - 1] * dpre
            dx = dx + vec_ref[TAPS + k : TAPS + k + 1, cols] * pltpu.roll(masked, length - k, 0)
            sums.append(jnp.sum(masked * pltpu.roll(x, k, 0), axis=0, keepdims=True))
        sums.append(jnp.sum(dpre, axis=0, keepdims=True))
        sums.append(jnp.sum(gsum_ref[SUBS : 2 * SUBS, cols], axis=0, keepdims=True))
        sums.append(jnp.sum(gsum_ref[0:SUBS, cols], axis=0, keepdims=True))
        last = jnp.zeros((SUBS, LANES), jnp.float32)
        for k, value in enumerate(sums):
            last = jnp.where(sub == k, value, last)
        last_s[:, cols] = last
        dx_s[:, cols] = dx.astype(jnp.bfloat16)

    steps = ns << (cube.places - 1)
    many = max(CHUNKS // steps, 1)
    every = max(steps // CHUNKS, 1)

    def x_chunks(place, k):
        def run():
            for i in range(many):
                x_chunk((k if every == 1 else lax.div(k, every)) * many + i)

        if every == 1:
            run()
        else:
            pl.when(lax.rem(k, every) == 0)(run)

    cube.down_stage(0, step_out, x_chunks)
    into_part(0, dx_s)

    small_s[...] = jnp.zeros_like(small_s)
    owners = LANES // per_device

    def small_chunk(chunk, carry):
        cols = pl.ds(pl.multiple_of(chunk * LANES, LANES), LANES)
        shape = (owners, per_device, LANES)
        small_s[:, 0:per_device, 0:LANES] = gx_s[cols, :].reshape(shape)
        small_s[:, 0:per_device, LANES:VEC_AT] = gdt_s[cols, :].reshape(shape)[:, :, 0:DTRANK]
        rates, last = gamat_ref[:, cols], last_s[:, cols]
        for o in range(owners):
            mine = slice(o * per_device, (o + 1) * per_device)
            small_s[o, 0:DSTATE, VEC_AT : VEC_AT + per_device] = rates[:, mine]
            small_s[o, DSTATE:VECS, VEC_AT : VEC_AT + per_device] = last[:, mine]
        part_small[pl.ds(chunk * owners, owners)] = small_s[...].astype(jnp.bfloat16)
        return carry

    lax.fori_loop(0, inner // LANES, small_chunk, 0)
    cube.downward(give_in)

    share = cube.shards // CHUNKS
    span = 2 * inner // CHUNKS

    def load(chunk):
        slot = lax.rem(chunk, 2)
        return pltpu.make_async_copy(
            all_in.at[pl.ds(chunk * share, share)], weights.at[slot], load_sem.at[slot]
        )

    dhidden_s[...] = jnp.zeros_like(dhidden_s)
    load(jnp.int32(0)).start()

    def hidden_chunk(chunk, left, base):
        load(chunk).wait()
        pl.when(chunk + 1 < CHUNKS)(lambda: load(chunk + 1).start())
        cols = pl.ds(pl.multiple_of((chunk - base) * span, span), span)
        right = weights[lax.rem(chunk, 2)].reshape(span, width)
        dhidden_s[...] += jnp.dot(left[:, cols], right, preferred_element_type=jnp.float32)

    def tokens_rows(i, total):
        at = pl.ds(pl.multiple_of(i * 16, 16), 16)
        inverse = inverse_ref[at, 0:1]
        normed = tokens_ref[at, :].astype(jnp.float32) * inverse
        dhidden = dhidden_s[at, :]
        product = dhidden * normed
        scaled = dhidden * gain_ref[...]
        mean = jnp.mean(scaled * normed, axis=-1, keepdims=True)
        dtok_ref[at, :] = cot_ref[at, :].astype(jnp.float32) + inverse * (scaled - normed * mean)
        return total + product[0:8] + product[8:16]

    part = CHUNKS // 2

    def hidden_chunks(first, last, left, base):
        def body(chunk, carry):
            hidden_chunk(chunk, left, base)
            return carry

        lax.fori_loop(first, last, body, 0)

    for stage in range(cube.places + 2):
        if stage < cube.places + 1:
            cube.down_stage(stage + 1, step_out)
        cube.down_stage(stage, step_in)
        if stage == 0:
            hidden_chunks(0, part, dx_s, 0)
        if stage == 1:
            hidden_chunks(part, CHUNKS, dgate_ref, part)
        if stage == cube.places:
            zero = jnp.zeros((SUBS, width), jnp.float32)
            total = lax.fori_loop(0, length // 16, tokens_rows, zero)
            row = jnp.sum(total, axis=0, keepdims=True)
            ggain_ref[...] = jnp.zeros_like(ggain_ref)
            for k in range(width // LANES):
                ggain_ref[k : k + 1, :] = row[:, k * LANES : (k + 1) * LANES]
    vectors = sum_small[0:VECS, VEC_AT : VEC_AT + per_device]
    sum_vec[0 : KCONV + 3, :] = vectors[DSTATE:GAIN, :]
    sum_vec[KCONV + 3 :, :] = vectors[0:DSTATE, :]
    await_bytes(gout_ref.at[pl.ds(0, cube.shards - 1)], send_first.at[0])
    await_bytes(part_in.at[pl.ds(0, cube.shards - 1)], send_sem.at[0])
    await_bytes(part_small.at[pl.ds(0, cube.shards - 1)], send_sem.at[1])


def back_and_scatter(far, arrays, all_in, per_device, small, fsdp, ns):
    length, width = arrays[0].shape[0], all_in.shape[2]
    inner = per_device * fsdp * ns
    shards, masks = fsdp * ns, fsdp // 2
    f32, b16 = jnp.float32, jnp.bfloat16
    blocks = [(2 * per_device, width), (per_device, width), (small, SMALL_COLUMNS)]

    def inbox(slots):
        return [
            [
                pltpu.VMEM((slots(route), ns, rows, count), b16)
                for route, unused, count in routes_of(columns)
            ]
            for rows, columns in blocks
        ]

    most = slot_count(fsdp, ns, 2)
    return pl.pallas_call(
        functools.partial(back_kernel, fsdp, ns, per_device),
        in_specs=[
            [pl.BlockSpec(memory_space=pl.ANY)] * len(far),
            *[pl.BlockSpec(memory_space=pltpu.VMEM)] * len(arrays),
            pl.BlockSpec(memory_space=pl.ANY),
        ],
        out_specs=[pl.BlockSpec(memory_space=pltpu.VMEM)] * 6,
        out_shape=[
            jax.ShapeDtypeStruct((length, width), f32),
            jax.ShapeDtypeStruct((-(-width // LANES // 16) * 16, LANES), f32),
        ]
        + [jax.ShapeDtypeStruct(block, f32) for block in blocks]
        + [jax.ShapeDtypeStruct((GAIN, per_device), f32)],
        scratch_shapes=[
            [pltpu.VMEM(array.shape, array.dtype) for array in far],
            pltpu.SemaphoreType.DMA((len(far),)),
            pltpu.VMEM((shards,) + blocks[0], b16),
            pltpu.VMEM((shards,) + blocks[2], b16),
            pltpu.VMEM((LANES // per_device,) + blocks[2], f32),
        ]
        + inbox(lambda route: masks)
        + inbox(functools.partial(slot_count, fsdp, ns))
        + [
            pltpu.VMEM((length, inner), b16),
            pltpu.VMEM((length, width), f32),
            pltpu.VMEM((2, shards // CHUNKS) + blocks[0], b16),
            pltpu.VMEM((KCONV - 1, length, LANES), f32),
            pltpu.VMEM((length, LANES), b16),
            pltpu.VMEM((length, LANES), b16),
            pltpu.VMEM((length, inner), f32),
            pltpu.VMEM((inner, LANES), f32),
            pltpu.VMEM((inner, LANES), f32),
            pltpu.VMEM((SUBS, inner), f32),
            pltpu.SemaphoreType.DMA((2,)),
            pltpu.SemaphoreType.DMA((1,)),
            pltpu.SemaphoreType.DMA((1, ROUTES, most, ns)),
            pltpu.SemaphoreType.DMA((1, ROUTES, masks, ns)),
            pltpu.SemaphoreType.DMA((2,)),
            pltpu.SemaphoreType.DMA((2, ROUTES, most, ns)),
            pltpu.SemaphoreType.DMA((2, ROUTES, masks, ns)),
        ],
        compiler_params=pltpu.CompilerParams(
            collective_id=1, has_side_effects=True, vmem_limit_bytes=60 * 1024 * 1024
        ),
    )(far, *arrays, all_in)


def halves_of(deep, wide):
    if deep >= 32:
        return [(g, (g * (deep // 2), deep // 2), (0, wide)) for g in range(2)]
    return [(g, (0, deep), (first, count)) for g, first, count in routes_of(wide, wide)]


def muon_kernel(
    fsdp,
    ns,
    starts,
    sum_in,
    sum_out,
    in_moment,
    out_moment,
    low_ref,
    gain_ref,
    x_out,
    low_out,
    gain_out,
    rows_s,
    turn,
    back_s,
    mine,
    outbox,
    lands,
    pieces_s,
    gram,
    now,
    poly,
    small_now,
    small_land,
    small_gram,
    low_s,
    send_sem,
    gather_sem,
    recv_sem,
    came_sem,
    swap_sem,
    small_send,
    small_recv,
):
    cube = Cube(fsdp, ns)
    pieces, deep, wide = pieces_s.shape
    width = now.shape[0]
    rows = sum_in.shape[0]
    blocks = width // LANES
    each = LANES // deep
    split = halves_of(deep, wide)
    ways = [cube.sibling] + [cube.partner(0, place) for place in range(cube.places)]
    ways += [(cube.row, flipped(cube.col, 1 << k)) for k in range(ns.bit_length() - 1)]
    stages = len(ways)
    cube.greet(ways[cube.places + 2 :])

    short = sum_out.shape[0]
    rows_s[0] = (MOMENTUM * in_moment[...] + sum_in[...]).astype(jnp.bfloat16)
    rows_s[1, 0:short, :] = (MOMENTUM * out_moment[...] + sum_out[...]).astype(jnp.bfloat16)
    rows_s[1, short:, :] = jnp.zeros((rows - short, width), jnp.bfloat16)

    def swap(source, target, which):
        return pltpu.make_async_remote_copy(
            src_ref=source,
            dst_ref=target,
            send_sem=swap_sem.at[which, 0],
            recv_sem=swap_sem.at[which, 1],
            device_id=cube.sibling,
            device_id_type=MESH,
        )

    there = swap(rows_s.at[1 - cube.core], turn.at[pl.ds(rows, rows)], 0)
    there.start()
    turn[0:rows] = rows_s[cube.core]

    def small_copy(k):
        return pltpu.make_async_remote_copy(
            src_ref=small_now.at[k],
            dst_ref=small_land.at[k],
            send_sem=small_send.at[k],
            recv_sem=small_recv.at[k],
            device_id=ways[k],
            device_id_type=MESH,
        )

    def inverse(total):
        return 1.0 / (jnp.sqrt(jnp.full((1, 1), total, jnp.float32)) + FROB_EPS)

    def diagonal(block):
        on = lax.broadcasted_iota(jnp.int32, block.shape, 0) == lax.broadcasted_iota(
            jnp.int32, block.shape, 1
        )
        return jnp.sum(jnp.where(on, block, 0.0))

    def small_step(k):
        small_copy(k).wait()
        total = small_now[k].astype(jnp.float32) + small_land[k].astype(jnp.float32)
        if k + 1 < stages:
            small_now[k + 1] = total.astype(jnp.bfloat16)
            small_copy(k + 1).start()
            return
        gain_out[...] = total[starts[2] :]
        for which in range(2):
            deep = starts[which + 1] - starts[which]
            whole = jnp.pad(total[starts[which] : starts[which + 1]], ((0, LANES - deep), (0, 0)))
            scale = inverse(diagonal(whole))
            small_gram[which] = whole * (scale * scale)
            low_s[which] = (low_ref[which] * scale).astype(jnp.bfloat16)

    for which in range(2):
        low = low_ref[which].astype(jnp.bfloat16)
        term = contract(low, low, 0, 0)[0 : starts[which + 1] - starts[which]]
        small_now[0, starts[which] : starts[which + 1], :] = term.astype(jnp.bfloat16)
    small_now[0, starts[2] :, :] = gain_ref[...].astype(jnp.bfloat16)
    small_copy(0).start()
    left = list(range(stages))

    def between():
        if left:
            small_step(left.pop(0))

    for (route, unused, unused), land in zip(split, lands):
        clear_ends(cube, route, land)

    there.wait()
    for b in range(blocks):
        if b % 2 == 0:
            band = contract(turn[:, b * LANES : (b + 2) * LANES], turn[...], 0, 0)
        block = band[b % 2 * LANES : (b % 2 + 1) * LANES]
        for c in range(wide // LANES):
            at = (b + c) % blocks * LANES
            for r in range(each):
                strip = block[r * deep : (r + 1) * deep, at : at + LANES]
                mine[b * each + r, :, c * LANES : (c + 1) * LANES] = strip

    def step(routes, mask, col, to, lines, places):
        for (route, rows_at, cols_at), land in zip(split, lands):
            if route not in routes:
                continue
            at = (cube.spot(mask, col, route), pl.ds(*rows_at), pl.ds(*cols_at))

            def wait(slot):
                await_bytes(land.at[slot], recv_sem.at[(route,) + slot])

            total = mine[at]
            for slot in arrivals(cube, route, mask, col, lines, places, wait):
                total = total + land[slot].astype(jnp.float32)
            if to is not None:
                outbox[at] = total.astype(jnp.bfloat16)
            else:
                pieces_s[at] = total.astype(jnp.bfloat16)

            def give(slot, device):
                send(
                    outbox.at[at],
                    land.at[slot],
                    send_sem,
                    recv_sem.at[(route,) + slot],
                    device,
                )

            hand_on(cube, route, mask, col, to, give)

    for stage in range(cube.places + 2):
        cube.down_stage(stage, step, third=False)
        if stage <= cube.places:
            between()

    def spread(routes, mask, col, ways, places, own):
        for route, rows_at, cols_at in split:
            if route not in routes:
                continue
            block = pieces_s.at[cube.spot(mask, col, route), pl.ds(*rows_at), pl.ds(*cols_at)]

            def sem_of(mask, col):
                return came_sem.at[route, mask, col]

            if not own:
                await_bytes(block, sem_of(mask, col))
            sems = gather_sem.at[route]
            pass_on(cube, route, mask, col, ways, places, block, block, sems, sem_of)

    def small_newton():
        for which in range(2):
            whole = small_gram[which]
            low = whole.astype(jnp.bfloat16)
            power = jnp.dot(low, low, preferred_element_type=jnp.float32)
            mixed = (COEF_B * whole + COEF_C * power).astype(jnp.bfloat16)
            block = low_s[which]
            low_s[which] = (
                COEF_A * block.astype(jnp.float32)
                + jnp.dot(block, mixed, preferred_element_type=jnp.float32)
            ).astype(jnp.bfloat16)
            half = COEF_A * whole + jnp.dot(low, mixed, preferred_element_type=jnp.float32)
            small_gram[which] = COEF_A * half + jnp.dot(
                half.astype(jnp.bfloat16), mixed, preferred_element_type=jnp.float32
            )

    def after(place, k):
        if place == cube.places - 1:
            pl.when(k - (ns << place) < NS_STEPS)(small_newton)

    cube.upward(spread, after=after, between=between, third=False)
    low_out[...] = low_s[...]

    for b in range(blocks):
        for c in range(wide // LANES):
            at = (b + c) % blocks * LANES
            for r in range(each):
                now[b * LANES + r * deep : b * LANES + (r + 1) * deep, at : at + LANES] = pieces_s[
                    b * each + r, :, c * LANES : (c + 1) * LANES
                ]
    for b in range(blocks):
        for c in range(wide // LANES, blocks):
            other = (b + c) % blocks
            block = now[other * LANES : (other + 1) * LANES, b * LANES : (b + 1) * LANES]
            flip = block.astype(jnp.float32).T.astype(jnp.bfloat16)
            now[b * LANES : (b + 1) * LANES, other * LANES : (other + 1) * LANES] = flip

    total = jnp.zeros((), jnp.float32)
    for b in range(0, width, LANES):
        total = total + diagonal(now[b : b + LANES, b : b + LANES].astype(jnp.float32))
    factor = inverse(total)
    square = factor * factor
    strip = min(BAND, width)

    def turned(block, k):
        moved = COEF_A * block.astype(jnp.float32) + jnp.dot(
            block, poly[...], preferred_element_type=jnp.float32
        )
        if k == 0:
            moved = moved * factor
        return moved.astype(jnp.bfloat16)

    for k in range(NS_STEPS):

        def poly_strip(i, carry, k=k):
            at = pl.ds(pl.multiple_of(i * strip, strip), strip)
            low = now[at, :]
            power = jnp.dot(low, now[...], preferred_element_type=jnp.float32)
            if k == 0:
                mixed = COEF_B * square * low.astype(jnp.float32) + (COEF_C * square * square) * power
            else:
                mixed = COEF_B * gram[at, :] + COEF_C * power
            poly[at, :] = mixed.astype(jnp.bfloat16)
            return carry

        lax.fori_loop(0, width // strip, poly_strip, 0)
        if k + 1 == NS_STEPS:
            break
        turn[...] = turned(turn[...], k)

        def gram_strip(i, carry, k=k):
            at = pl.ds(pl.multiple_of(i * strip, strip), strip)
            low = now[at, :]
            full = low.astype(jnp.float32) if k == 0 else gram[at, :]
            half = COEF_A * full + jnp.dot(low, poly[...], preferred_element_type=jnp.float32)
            if k == 0:
                half = half * square
            renewed = COEF_A * half + jnp.dot(
                half.astype(jnp.bfloat16), poly[...], preferred_element_type=jnp.float32
            )
            gram[at, :] = renewed
            now[at, :] = renewed.astype(jnp.bfloat16)
            return carry

        lax.fori_loop(0, width // strip, gram_strip, 0)
    turn[rows:] = turned(turn[rows:], NS_STEPS - 1)
    home = swap(turn.at[pl.ds(rows, rows)], back_s, 1)
    home.start()
    x_out[cube.core] = turned(turn[0:rows], NS_STEPS - 1)
    home.wait()
    x_out[1 - cube.core] = back_s[...]
    await_bytes(outbox.at[pl.ds(0, pieces - 1)], send_sem)
    for route, rows_at, cols_at in split:
        sent = pieces_s.at[:, pl.ds(*rows_at), pl.ds(*cols_at)]
        await_passed(cube, route, sent, gather_sem.at[route])


def muon_rows(sum_in, sum_out, in_moment, out_moment, low, columns, gain, fsdp, ns):
    pieces = fsdp * ns // 2
    rows, width = sum_in.shape
    wide = (width // LANES // 2 + 1) * LANES
    deep = width // pieces
    block = (pieces, deep, wide)
    stages = (fsdp * ns).bit_length() - 1
    starts = (0, columns[0], sum(columns))
    small = (sum(columns) + gain.shape[0], LANES)
    f32, b16 = jnp.float32, jnp.bfloat16
    landing = [
        pltpu.VMEM((slot_count(fsdp, ns, route), ns, rows_at[1], cols_at[1]), b16)
        for route, rows_at, cols_at in halves_of(deep, wide)
    ]
    held = pl.BlockSpec(memory_space=pltpu.VMEM)
    return pl.pallas_call(
        functools.partial(muon_kernel, fsdp, ns, starts),
        in_specs=[held] * 6,
        out_specs=[held] * 3,
        out_shape=[
            jax.ShapeDtypeStruct((2, rows, width), b16),
            jax.ShapeDtypeStruct(low.shape, b16),
            jax.ShapeDtypeStruct(gain.shape, f32),
        ],
        scratch_shapes=[
            pltpu.VMEM((2, rows, width), b16),
            pltpu.VMEM((2 * rows, width), b16),
            pltpu.VMEM((rows, width), b16),
            pltpu.VMEM(block, f32),
            pltpu.VMEM(block, b16),
        ]
        + [
            landing,
            pltpu.VMEM(block, b16),
            pltpu.VMEM((width, width), f32),
            pltpu.VMEM((width, width), b16),
            pltpu.VMEM((width, width), b16),
            pltpu.VMEM((stages,) + small, b16),
            pltpu.VMEM((stages,) + small, b16),
            pltpu.VMEM((2, LANES, LANES), f32),
            pltpu.VMEM(low.shape, b16),
            pltpu.SemaphoreType.DMA,
            pltpu.SemaphoreType.DMA((ROUTES, 3)),
            pltpu.SemaphoreType.DMA((ROUTES, slot_count(fsdp, ns, 2), ns)),
            pltpu.SemaphoreType.DMA((ROUTES, fsdp // 2, ns)),
            pltpu.SemaphoreType.DMA((2, 2)),
            pltpu.SemaphoreType.DMA((stages,)),
            pltpu.SemaphoreType.DMA((stages,)),
        ],
        compiler_params=pltpu.CompilerParams(
            collective_id=2, has_side_effects=True, vmem_limit_bytes=48 * 1024 * 1024
        ),
    )(sum_in, sum_out, in_moment, out_moment, low, gain)


def layer(tokens, out_grad, lengths, params, fsdp, ns):
    flat_low, grad_flat = tokens[0], out_grad[0]
    length, width = flat_low.shape
    (
        all_in,
        all_out,
        x_rows,
        dt_rows,
        vecs,
        gain,
        x_part,
        gate_in,
        conv_flat,
        u_low,
        proj,
        masks,
        hidden,
        inverse,
    ) = gather_and_front(lengths, flat_low, params, fsdp, ns)
    per_device = params[2].shape[0]
    inner = x_rows.shape[0]
    out_low = all_out.reshape(inner, width)
    d_gate, d_u, d_dtlow, vec_parts, grad_amat, d_bc, grad_out, block_out = scan_both(
        proj, masks, dt_rows, u_low, gate_in, flat_low, grad_flat, out_low, vecs
    )
    d_tokens, grad_gain, sum_in, sum_out, sum_small, sum_vec = back_and_scatter(
        [
            grad_out.reshape(fsdp * ns, per_device, width),
            d_gate,
            hidden,
            d_dtlow,
            d_u,
            u_low,
            conv_flat,
            x_part,
            flat_low,
            grad_flat,
        ],
        (inverse, masks, proj, x_rows, dt_rows, vecs, gain, vec_parts, grad_amat, d_bc),
        all_in,
        per_device,
        small_rows(per_device),
        fsdp,
        ns,
    )
    return (block_out[None], d_tokens[None], grad_gain, sum_in, sum_out, sum_small, sum_vec)


def adamw_update(param, first, second, grad):
    first_new = FIRST_MOMENT_BETA * first + (1.0 - FIRST_MOMENT_BETA) * grad
    second_new = BETA_SECOND * second + (1.0 - BETA_SECOND) * grad * grad
    first_hat = first_new / (1.0 - FIRST_MOMENT_BETA**STEP_NO)
    second_hat = second_new / (1.0 - BETA_SECOND**STEP_NO)
    param_new = param * (1.0 - ADAM_RATE * ADAM_DECAY) - ADAM_RATE * first_hat / (
        jnp.sqrt(second_hat) + ADAM_EPS
    )
    return (param_new, first_new, second_new)


def on_device(
    tokens,
    out_grad,
    doc_lengths,
    in_proj,
    inner_projection_weight,
    dt_proj,
    out_proj,
    in_moment,
    x_moment,
    dt_moment,
    out_moment,
    vectors,
    vector_first,
    vector_second,
    norm_gain,
    gain_first,
    gain_second,
):
    fsdp, ns = lax.axis_size("fsdp"), lax.axis_size("ns")
    shards = fsdp * ns
    per_device, columns = inner_projection_weight.shape
    rank, gains = dt_proj.shape[1], norm_gain.shape[0]
    block_out, grad_tokens, grad_gain, sum_in, sum_out, sum_small, sum_vec = layer(
        tokens,
        out_grad,
        doc_lengths,
        (
            in_proj,
            out_proj,
            inner_projection_weight,
            dt_proj,
            vectors,
            norm_gain[None],
        ),
        fsdp,
        ns,
    )
    sum_x = sum_small[:per_device, :columns]
    sum_dt = sum_small[:per_device, LANES : LANES + rank]
    summed = (sum_in, sum_x, sum_dt, sum_out, sum_vec)
    old_moments = (in_moment, x_moment, dt_moment, out_moment)
    moments = tuple((MOMENTUM * moment + grad for moment, grad in zip(old_moments, summed[:4])))
    gap = -per_device % 16
    low = jnp.stack(
        [
            jnp.pad(moments[1], ((0, gap), (0, LANES - columns))),
            jnp.pad(moments[2], ((0, gap), (0, LANES - rank))),
        ]
    )
    big, low, sum_gain = muon_rows(
        sum_in, sum_out, in_moment, out_moment, low, (columns, rank), grad_gain, fsdp, ns
    )
    place = lax.axis_index("fsdp") * ns + lax.axis_index("ns")
    sum_gain = lax.dynamic_slice_in_dim(sum_gain.reshape(-1), place * gains, gains, 0)
    own_blocks = (
        big[0],
        low[0, :per_device, :columns],
        low[1, :per_device, :rank],
        big[1, :per_device],
    )
    weights = (in_proj, inner_projection_weight, dt_proj, out_proj)
    fans = (DMODEL, DINNER, DTRANK, DINNER // 8)
    results = []
    for weight, moment, block, fan in zip(weights, moments, own_blocks, fans):
        rate = 0.5 * math.sqrt(weight.shape[0] * shards / fan)
        results.append((1.0 - SHRINK) * weight - rate * block.astype(jnp.float32))
        results.append(moment)
    vec_new, vec_first, vec_second = adamw_update(vectors, vector_first, vector_second, summed[4])
    gain_new, gain_m, gain_v = adamw_update(norm_gain, gain_first, gain_second, sum_gain)
    return (
        block_out,
        grad_tokens,
        results[0],
        results[1],
        results[2],
        results[3],
        results[4],
        results[5],
        results[6],
        results[7],
        vec_new,
        vec_first,
        vec_second,
        gain_new,
        gain_m,
        gain_v,
    )


def solution(mesh):
    placed = (
        P(("fsdp", "ns"), None, None),
        P(("fsdp", "ns"), None, None),
        P(("fsdp", "ns"), None),
        P(("fsdp", "ns"), None),
        P(("fsdp", "ns"), None),
        P(("fsdp", "ns"), None),
        P(("fsdp", "ns"), None),
        P(("fsdp", "ns"), None),
        P(("fsdp", "ns"), None),
        P(("fsdp", "ns"), None),
        P(("fsdp", "ns"), None),
        P(None, ("fsdp", "ns")),
        P(None, ("fsdp", "ns")),
        P(None, ("fsdp", "ns")),
        P(("fsdp", "ns")),
        P(("fsdp", "ns")),
        P(("fsdp", "ns")),
    )
    return jax.shard_map(
        on_device,
        mesh=mesh,
        in_specs=placed,
        out_specs=(
            P(("fsdp", "ns"), None, None),
            P(("fsdp", "ns"), None, None),
            P(("fsdp", "ns"), None),
            P(("fsdp", "ns"), None),
            P(("fsdp", "ns"), None),
            P(("fsdp", "ns"), None),
            P(("fsdp", "ns"), None),
            P(("fsdp", "ns"), None),
            P(("fsdp", "ns"), None),
            P(("fsdp", "ns"), None),
            P(None, ("fsdp", "ns")),
            P(None, ("fsdp", "ns")),
            P(None, ("fsdp", "ns")),
            P(("fsdp", "ns")),
            P(("fsdp", "ns")),
            P(("fsdp", "ns")),
        ),
        check_vma=False,
    )
```

```python
import functools
import math

import jax
import jax.numpy as jnp
from jax import lax
from jax.experimental import pallas as pl
from jax.experimental.pallas import tpu as pltpu
from jax.sharding import PartitionSpec as P

DMODEL = 1024
DINNER = 2048
DSTATE = 16
DTRANK = 64
KCONV = 4
NS_STEPS = 4
STEP_NO = 10


NORM_EPS = 1e-05
FROB_EPS = 1e-07
COEF_A = 3.4445
COEF_B = -4.775
COEF_C = 2.0315
MOMENTUM = 0.95
SHRINK = 0.001
FIRST_MOMENT_BETA = 0.9
BETA_SECOND = 0.95
ADAM_EPS = 1e-08
ADAM_RATE = 1.0
ADAM_DECAY = 0.001


def contract(left, right, left_dim, right_dim):
    return lax.dot_general(
        left, right, (((left_dim,), (right_dim,)), ((), ())), preferred_element_type=jnp.float32
    )


MESH = pl.DeviceIdType.MESH
LANES = 128
SUBS = 8
PASS = LANES * SUBS
STEPS = 4
RESET = 1.0e4
LOG2E = math.log2(math.e)
LN2 = math.log(2.0)
TAPS = DSTATE
CBIAS = TAPS + KCONV
DTBIAS = CBIAS + 1
SKIP = CBIAS + 2
GAIN = CBIAS + 3
VECS = CBIAS + 4
CHUNKS = 16
BAND = 512
SMALL_COLUMNS = 2 * LANES
VEC_AT = LANES + DTRANK


def lane_tile(j):
    return pl.ds(j * LANES, LANES)


def scan_kernel(
    bc_ref,
    proj_ref,
    masks_ref,
    dtw_ref,
    u_ref,
    gate_ref,
    tokens_ref,
    cot_ref,
    outw_ref,
    vec_ref,
    dgate_ref,
    du_ref,
    ddt_ref,
    gsum_ref,
    gamat_ref,
    dbc_ref,
    gout_ref,
    block_ref,
    gated_s,
    amat_s,
    gamat_s,
    pre_s,
    dg_s,
    delta_s,
    dec_s,
    drive_s,
    dstate_s,
    y_s,
    pull_s,
    ddelta_s,
    states,
    prod_a,
    prod_b,
    sums_b,
    sums_c,
):
    length = u_ref.shape[0]
    half = pl.program_id(0)
    bias_row = vec_ref[DTBIAS : DTBIAS + 1, :]

    pre_s[...] = contract(proj_ref[...].astype(jnp.bfloat16), dtw_ref[...], 1, 1) + bias_row
    dg_s[...] = contract(cot_ref[...], outw_ref[...], 1, 1)

    for j in range(SUBS):
        rates = -LOG2E * jnp.exp(vec_ref[0:DSTATE, j * LANES : (j + 1) * LANES])
        amat_s[pl.ds(j, DSTATE, stride=SUBS), :] = rates

    def amat_of(n):
        return amat_s[n * SUBS : (n + 1) * SUBS, :]

    rows = 16

    def prepare(i, carry):
        r = pl.multiple_of(i * rows, rows)
        keep = masks_ref[pl.ds(r, rows), 1:2] > 0.0
        for j in range(SUBS):
            at = (pl.ds(r, rows), lane_tile(j))
            delta = jax.nn.softplus(pre_s[at])
            u = u_ref[at].astype(jnp.float32)
            gate = gate_ref[at]
            delta_s[at] = delta
            to = (pl.ds(r * SUBS + j, rows, stride=SUBS), slice(None))
            dec_s[to] = jnp.where(keep, delta, RESET)
            drive_s[to] = delta * u
            dstate_s[to] = dg_s[at] * (gate * jax.nn.sigmoid(gate))
        return carry

    lax.fori_loop(0, length // rows, prepare, 0)

    for n in range(DSTATE):
        states[n] = jnp.zeros((SUBS, LANES), jnp.float32)

    def tile_of(ref, t):
        return ref[pl.ds(pl.multiple_of(t * SUBS, SUBS), SUBS), :]

    def put_tile(ref, t, value):
        ref[pl.ds(pl.multiple_of(t * SUBS, SUBS), SUBS), :] = value

    def ahead(i, carry):
        state = list(carry)
        for k in range(STEPS):
            t = i * STEPS + k
            dec, drive = tile_of(dec_s, t), tile_of(drive_s, t)
            parts = [None, None]
            for n in range(DSTATE):
                s = jnp.exp2(dec * amat_of(n)) * state[n] + drive * bc_ref[t, DTRANK + n]
                state[n] = s
                states[(t + 1) * DSTATE + n] = s
                term = s * bc_ref[t, DTRANK + DSTATE + n]
                parts[n % 2] = term if parts[n % 2] is None else parts[n % 2] + term
            put_tile(y_s, t, parts[0] + parts[1])
        return tuple(state)

    zero = jnp.zeros((SUBS, LANES), jnp.float32)
    lax.fori_loop(0, length // STEPS, ahead, (zero,) * DSTATE)

    pick = (
        lax.broadcasted_iota(jnp.int32, (2 * DSTATE, 2 * LANES), 1) // SUBS
        == lax.broadcasted_iota(jnp.int32, (2 * DSTATE, 2 * LANES), 0)
    ).astype(jnp.bfloat16)
    span = DSTATE * SUBS

    def channel_sums(products, t0):
        for k in range(0, STEPS, 2):
            block = products[k * span : (k + 2) * span, :]
            row = pl.multiple_of((t0 + k) * DSTATE, 2 * DSTATE)
            both = jnp.dot(pick, block, preferred_element_type=jnp.float32)
            sums_b[pl.ds(row, 2 * DSTATE), :] = both[:, 0:LANES]
            sums_c[pl.ds(row, 2 * DSTATE), :] = both[:, LANES : 2 * LANES]

    def behind_steps(t0, products, flow, g_amat):
        for k in reversed(range(STEPS)):
            t = t0 + k
            dec, drive, dstate = tile_of(dec_s, t), tile_of(drive_s, t), tile_of(dstate_s, t)
            pull, back = [None, None], [None, None]
            pend_b, pend_c = None, None
            for n in range(DSTATE):
                amat = amat_of(n)
                adj = dstate * bc_ref[t, DTRANK + DSTATE + n] + flow[n]
                term = adj * bc_ref[t, DTRANK + n]
                pull[n % 2] = term if pull[n % 2] is None else pull[n % 2] + term
                flow[n] = jnp.exp2(dec * amat) * adj
                weighted = flow[n] * states[t * DSTATE + n]
                g_amat[n] = g_amat[n] + weighted * dec
                term = weighted * amat
                back[n % 2] = term if back[n % 2] is None else back[n % 2] + term
                prod_b_n = adj * drive
                prod_c_n = states[(t + 1) * DSTATE + n] * dstate
                if n % 2:
                    row = k * span + (n - 1) * SUBS
                    products[row : row + 2 * SUBS, 0:LANES] = jnp.concatenate(
                        [pend_b, prod_b_n], axis=0
                    ).astype(jnp.bfloat16)
                    products[row : row + 2 * SUBS, LANES : 2 * LANES] = jnp.concatenate(
                        [pend_c, prod_c_n], axis=0
                    ).astype(jnp.bfloat16)
                pend_b, pend_c = prod_b_n, prod_c_n
            put_tile(pull_s, t, pull[0] + pull[1])
            put_tile(ddelta_s, t, back[0] + back[1])

    groups = length // (2 * STEPS)

    def behind(i, carry):
        flow, g_amat = list(carry[0]), list(carry[1])
        t1 = length - (2 * i + 1) * STEPS
        channel_sums(prod_b, t1 + STEPS)
        behind_steps(t1, prod_a, flow, g_amat)
        channel_sums(prod_a, t1)
        behind_steps(t1 - STEPS, prod_b, flow, g_amat)
        return (tuple(flow), tuple(g_amat))

    unused, g_amat = lax.fori_loop(0, groups, behind, ((zero,) * DSTATE, (zero,) * DSTATE))
    channel_sums(prod_b, 0)
    for n in range(DSTATE):
        gamat_s[n * SUBS : (n + 1) * SUBS, :] = g_amat[n]
    for j in range(SUBS):
        cols = slice(j * LANES, (j + 1) * LANES)
        of_rates = gamat_s[pl.ds(j, DSTATE, stride=SUBS), :]
        gamat_ref[:, cols] = of_rates * -jnp.exp(vec_ref[0:DSTATE, cols])

    line = lax.broadcasted_iota(jnp.int32, (2 * LANES, LANES), 0)
    column = lax.broadcasted_iota(jnp.int32, (2 * LANES, LANES), 1)
    first = line < LANES
    total = jnp.zeros((length, LANES), jnp.float32)
    for n in range(DSTATE):
        goes = jnp.where(first, DTRANK + n, DTRANK + DSTATE + n) == column
        at = (pl.ds(n, length, stride=DSTATE), slice(None))
        both = jnp.concatenate([sums_b[at], sums_c[at]], axis=1).astype(jnp.bfloat16)
        total = total + jnp.dot(
            both, goes.astype(jnp.bfloat16), preferred_element_type=jnp.float32
        )

    @pl.when(half == 0)
    def _():
        dbc_ref[...] = total

    @pl.when(half > 0)
    def _():
        dbc_ref[...] += total

    gsum_ref[...] = jnp.zeros_like(gsum_ref)

    def finish(i, carry):
        r = pl.multiple_of(i * rows, rows)
        for j in range(SUBS):
            at = (pl.ds(r, rows), lane_tile(j))
            of = (pl.ds(r * SUBS + j, rows, stride=SUBS), slice(None))
            skip = vec_ref[SKIP : SKIP + 1, j * LANES : (j + 1) * LANES]
            u = u_ref[at].astype(jnp.float32)
            gate = gate_ref[at]
            sig = jax.nn.sigmoid(gate)
            act = gate * sig
            dg = dg_s[at]
            y = y_s[of] + skip * u
            gated_s[at] = (y * act).astype(jnp.bfloat16)
            dgate_ref[at] = (dg * y * sig * (1.0 + gate * (1.0 - sig))).astype(jnp.bfloat16)
            dstate = dg * act
            pull = pull_s[of]
            du_ref[at] = dstate * skip + pull * delta_s[at]
            ddt = (ddelta_s[of] * LN2 + pull * u) * jax.nn.sigmoid(pre_s[at])
            ddt_ref[at] = ddt.astype(jnp.bfloat16)
            cols = slice(j * LANES, (j + 1) * LANES)
            g_skip = dstate * u
            gsum_ref[0:8, cols] += g_skip[0:8] + g_skip[8:16]
            gsum_ref[8:16, cols] += ddt[0:8] + ddt[8:16]
        return carry

    lax.fori_loop(0, length // rows, finish, 0)

    for b in range(0, PASS, BAND):
        strip = slice(b, b + BAND)
        gout_ref[strip, :] = contract(gated_s[:, strip], cot_ref[...], 0, 0).astype(jnp.bfloat16)
    through = jnp.dot(gated_s[...], outw_ref[...], preferred_element_type=jnp.float32)

    @pl.when(half == 0)
    def _():
        block_ref[...] = tokens_ref[...].astype(jnp.float32) + through

    @pl.when(half > 0)
    def _():
        block_ref[...] += through


def scan_both(proj, masks, dt_rows, u_low, gate_in, tokens, cotangent, out_low, vecs):
    length, inner = u_low.shape
    width = out_low.shape[1]
    by_channel = lambda h: (0, h)
    whole = lambda h: (0, 0)
    rows_of = lambda h: (h, 0)
    f32, b16 = jnp.float32, jnp.bfloat16
    return pl.pallas_call(
        scan_kernel,
        grid=(inner // PASS,),
        in_specs=[
            pl.BlockSpec(memory_space=pltpu.SMEM),
            pl.BlockSpec((length, LANES), whole),
            pl.BlockSpec((length, LANES), whole),
            pl.BlockSpec((PASS, LANES), rows_of),
            pl.BlockSpec((length, PASS), by_channel),
            pl.BlockSpec((length, PASS), by_channel),
            pl.BlockSpec((length, width), whole),
            pl.BlockSpec((length, width), whole),
            pl.BlockSpec((PASS, width), rows_of),
            pl.BlockSpec((VECS, PASS), by_channel),
        ],
        out_specs=[
            pl.BlockSpec((length, PASS), by_channel),
            pl.BlockSpec((length, PASS), by_channel),
            pl.BlockSpec((length, PASS), by_channel),
            pl.BlockSpec((16, PASS), by_channel),
            pl.BlockSpec((DSTATE, PASS), by_channel),
            pl.BlockSpec((length, LANES), whole),
            pl.BlockSpec((PASS, width), rows_of),
            pl.BlockSpec((length, width), whole),
        ],
        out_shape=[
            jax.ShapeDtypeStruct((length, inner), b16),
            jax.ShapeDtypeStruct((length, inner), f32),
            jax.ShapeDtypeStruct((length, inner), b16),
            jax.ShapeDtypeStruct((16, inner), f32),
            jax.ShapeDtypeStruct((DSTATE, inner), f32),
            jax.ShapeDtypeStruct((length, LANES), f32),
            jax.ShapeDtypeStruct((inner, width), b16),
            jax.ShapeDtypeStruct((length, width), f32),
        ],
        scratch_shapes=[
            pltpu.VMEM((length, PASS), b16),
            pltpu.VMEM((DSTATE * SUBS, LANES), f32),
            pltpu.VMEM((DSTATE * SUBS, LANES), f32),
        ]
        + [pltpu.VMEM((length, PASS), f32)] * 3
        + [pltpu.VMEM((length * SUBS, LANES), f32)] * 6
        + [
            pltpu.VMEM(((length + 1) * DSTATE, SUBS, LANES), f32),
            pltpu.VMEM((STEPS * DSTATE * SUBS, 2 * LANES), b16),
            pltpu.VMEM((STEPS * DSTATE * SUBS, 2 * LANES), b16),
            pltpu.VMEM(((length + STEPS) * DSTATE, LANES), f32),
            pltpu.VMEM(((length + STEPS) * DSTATE, LANES), f32),
        ],
        compiler_params=pltpu.CompilerParams(vmem_limit_bytes=60 * 1024 * 1024),
        cost_estimate=pl.CostEstimate(
            flops=24 * length * inner * DSTATE,
            bytes_accessed=24 * length * inner,
            transcendentals=2 * length * inner * DSTATE,
        ),
    )(proj, proj, masks, dt_rows, u_low, gate_in, tokens, cotangent, out_low, vecs)


def flipped(index, bit):
    return index + bit * (1 - 2 * lax.rem(lax.div(index, bit), 2))


ROUTES = 3


def each_mask(first, last, body):
    count = abs(last - first)
    sign = 1 if last > first else -1
    if count <= 4:
        for k in range(count):
            body(first + sign * k)
        return

    def step(k, carry):
        body(first + sign * k)
        return carry

    lax.fori_loop(0, count, step, 0)


def routes_of(width, share=4):
    tiles = width // LANES
    last = tiles // share
    counts = ((tiles - last + 1) // 2, (tiles - last) // 2, last)
    firsts = (0, counts[0], counts[0] + counts[1])
    return [(g, firsts[g] * LANES, counts[g] * LANES) for g in range(ROUTES) if counts[g]]


class Cube:
    def __init__(self, fsdp, ns):
        self.fsdp, self.ns = fsdp, ns
        self.shards, self.pieces, self.masks = fsdp * ns, fsdp * ns // 2, fsdp // 2
        order = [2 << k for k in range(fsdp.bit_length() - 2)]
        self.orders = (order, order[:-2] + [order[-1], order[-2]], order)
        self.places = len(order)
        self.row, self.col = lax.axis_index("fsdp"), lax.axis_index("ns")
        self.me = self.row * ns + self.col
        self.sibling = (flipped(self.row, 1), self.col)
        self.sibling_step = (flipped(self.row, 1) - self.row) * ns
        self.core = lax.rem(self.row, 2)
        self.above, self.below = (self.row, self.col + 1), (self.row, self.col - 1)
        self.has_above, self.has_below = self.col < ns - 1, self.col > 0
        self.half_row = lax.div(self.row, 2)
        moves = {bit: flipped(self.row, bit) - self.row for bit in order}
        halves = {bit: flipped(self.half_row, bit // 2) - self.half_row for bit in order}
        self.steps = [[moves[bit] for bit in bits] for bits in self.orders]
        self.half_steps = [[halves[bit] for bit in bits] for bits in self.orders]

    def partner(self, route, place):
        return (self.row + self.steps[route][place], self.col)

    def flips(self, mask, steps, start):
        for place, step in enumerate(steps):
            if isinstance(mask, int):
                start = start + step if mask >> place & 1 else start
            else:
                start = start + lax.rem(lax.div(mask, 1 << place), 2) * step
        return start

    def at(self, mask, col, route):
        return self.flips(mask, self.steps[route], self.row) * self.ns + col

    def spot(self, mask, col, route):
        return self.flips(mask, self.half_steps[route], self.half_row) * self.ns + col

    def wrapped(self, distance):
        col = self.col + distance
        return jnp.where(col < self.ns, col, col - self.ns)

    def greet(self, others=()):
        barrier = pltpu.get_barrier_semaphore()

        def signal(device):
            pl.semaphore_signal(barrier, inc=1, device_id=device, device_id_type=MESH)

        for place in range(self.places):
            signal(self.partner(0, place))
        signal(self.sibling)
        for other in others:
            signal(other)
        pl.when(self.has_above)(lambda: signal(self.above))
        pl.when(self.has_below)(lambda: signal(self.below))
        ends = jnp.where(self.has_above, 1, 0) + jnp.where(self.has_below, 1, 0)
        pl.semaphore_wait(barrier, self.places + 1 + len(others) + ends)

    def along_line(self, distance, step_to):
        pl.when(self.col - distance >= 0)(lambda: step_to(self.col - distance, "above"))
        pl.when(self.col + distance < self.ns)(lambda: step_to(self.col + distance, "below"))

    def upward(self, step, after=None, own=True, between=lambda: None, third=True):
        after = after or (lambda place, k: None)
        nothing, every, both = 0, range(self.places), ("above", "below")
        if own:
            step((0, 1, 2), nothing, self.col, both, every, True)
            after(-1, nothing)

        def along(d, carry):
            self.along_line(
                d, lambda col, way: step((0, 1), nothing, col, (way,), every, False)
            )
            after(-1, d)
            return carry

        lax.fori_loop(1, self.ns, along, 0)
        for place in every if third else ():
            later = range(place + 1, self.places)
            each_mask(
                1 << place,
                2 << place,
                lambda mask: step((2,), mask, self.col, both, later, False),
            )
        done = 1
        for place in every:
            between()
            later = range(place + 1, self.places)

            def of_mask(mask):
                def across(k, carry):
                    step((0, 1), mask, self.wrapped(k), (), later, False)
                    after(place, mask * self.ns + k)
                    return carry

                lax.fori_loop(0, self.ns, across, 0)

            each_mask(1 << place, 2 << place, of_mask)
            until = self.ns if place == self.places - 1 else min(done + 1, self.ns)
            if not third:
                continue

            def last(distance, carry):
                def of_mask(mask):
                    self.along_line(
                        distance, lambda col, way: step((2,), mask, col, (way,), (), False)
                    )

                each_mask(0, self.masks, of_mask)
                return carry

            lax.fori_loop(done, until, last, 0)
            done = until

    def down_stage(self, stage, step, after=None, third=True):
        after = after or (lambda place, k: None)
        nothing, every, both = 0, range(self.places), ("below", "above")
        source = {"above": ("below",), "below": ("above",)}
        if stage > self.places:
            step((0, 1, 2), nothing, self.col, None, both, every)
            return
        if stage == self.places:

            def along(k, carry):
                self.along_line(
                    self.ns - 1 - k,
                    lambda col, way: step((0, 1), nothing, col, other(way), source[other(way)], every),
                )
                after(-1, k)
                return carry

            lax.fori_loop(0, self.ns - 1, along, 0)
            for place in reversed(every if third else ()):
                later = range(place + 1, self.places)
                each_mask(
                    (2 << place) - 1,
                    (1 << place) - 1,
                    lambda mask: step((2,), mask, self.col, place, both, later),
                )
            return
        place = self.places - 1 - stage
        later = range(place + 1, self.places)

        def of_mask(mask):
            def across(i, carry):
                far = jnp.where(2 * self.col < self.ns, self.ns - 1 - i, 1 + i)
                far = jnp.where(far == self.ns, 0, far)
                step((0, 1), mask, self.wrapped(far), place, (), later)
                after(place, ((2 << place) - 1 - mask) * self.ns + i)
                return carry

            lax.fori_loop(0, self.ns, across, 0)

        each_mask((2 << place) - 1, (1 << place) - 1, of_mask)
        first = self.ns - 1 if stage == 0 else 1
        last = 2 if stage == 0 and self.places > 1 else 1

        def line_first(k, carry):
            def of_mask(mask):
                self.along_line(
                    first - k,
                    lambda col, way: step((2,), mask, col, other(way), source[other(way)], ()),
                )

            each_mask(self.masks - 1, -1, of_mask)
            return carry

        if stage < 2 and third:
            lax.fori_loop(0, first - last + 1, line_first, 0)

    def downward(self, step):
        for stage in range(self.places + 2):
            self.down_stage(stage, step)


def other(way):
    return "below" if way == "above" else "above"


def send(src, dst, send_sem, recv_sem, device):
    pltpu.make_async_remote_copy(
        src_ref=src,
        dst_ref=dst,
        send_sem=send_sem,
        recv_sem=recv_sem,
        device_id=device,
        device_id_type=MESH,
    ).start()


def await_bytes(ref, sem):
    pltpu.make_async_copy(ref, ref, sem).wait()


def pass_on(cube, route, mask, col, ways, places, source, target, send_sem, sem_of):
    if "above" in ways:
        pl.when(cube.has_above)(
            lambda: send(source, target, send_sem.at[1], sem_of(mask, col), cube.above)
        )
    if "below" in ways:
        pl.when(cube.has_below)(
            lambda: send(source, target, send_sem.at[2], sem_of(mask, col), cube.below)
        )
    for p in places:
        partner = cube.partner(route, p)
        send(source, target, send_sem.at[0], sem_of(mask + (1 << p), col), partner)


def await_passed(cube, route, ref, send_sem):
    many = cube.masks if route == 2 else 1
    crossed = cube.masks - 1 if route == 2 else cube.pieces - cube.ns
    await_bytes(ref.at[pl.ds(0, crossed)], send_sem.at[0])
    for col in range(cube.ns):

        @pl.when(cube.col == col)
        def _():
            if col + 1 < cube.ns:
                await_bytes(ref.at[pl.ds(0, many * (col + 1))], send_sem.at[1])
            if col:
                await_bytes(ref.at[pl.ds(0, many * (cube.ns - col))], send_sem.at[2])


def gather_step(cube, ins, outs, sems):
    send_sem, recv_sem, pair_send, pair_sem = sems

    def step(routes, mask, col, ways, places, own):
        for a, (mine, out) in enumerate(zip(ins, outs)):
            for route, first, count in routes_of(mine.shape[1]):
                if route not in routes:
                    continue
                cols = pl.ds(first, count)
                block = out.at[cube.at(mask, col, route), :, cols]

                def sem_of(mask, col):
                    return recv_sem.at[a, route, mask, col]

                if not own:
                    await_bytes(block, sem_of(mask, col))
                source = mine.at[:, cols] if own else block
                pass_on(
                    cube, route, mask, col, ways, places, source, block, send_sem.at[a, route], sem_of
                )
                send(source, block, pair_send.at[a], pair_sem.at[a], cube.sibling)

    return step


def own_step(cube, step):
    step((0, 1, 2), 0, cube.col, ("above", "below"), range(cube.places), True)


def front_kernel(
    fsdp,
    ns,
    per_device,
    gains,
    lengths_ref,
    tokens_ref,
    in_ref,
    out_ref,
    x_own,
    dt_own,
    vectors_own,
    gain_own,
    all_in,
    all_out,
    x_rows,
    dt_rows,
    vec_ref,
    gain_ref,
    xpart_far,
    gate_far,
    upre_far,
    u_far,
    proj_ref,
    masks_ref,
    hidden_ref,
    inverse_ref,
    xpart_ref,
    gate_ref,
    upre_ref,
    u_ref,
    away_sem,
    normed_s,
    in_all,
    small_all,
    in_low,
    out_low,
    small_ref,
    small_s,
    x_s,
    dt_s,
    mask_s,
    own_sem,
    send_sem,
    recv_sem,
    pair_send,
    pair_sem,
    send_out,
    recv_out,
    give_out,
    pair_out,
):
    cube = Cube(fsdp, ns)
    length, width = tokens_ref.shape
    in_low[...] = in_ref[...].astype(jnp.bfloat16)
    out_low[...] = out_ref[...].astype(jnp.bfloat16)
    small_s[...] = jnp.zeros_like(small_s)
    small_s[0:per_device, 0 : x_own.shape[1]] = x_own[...]
    small_s[0:per_device, LANES : LANES + dt_own.shape[1]] = dt_own[...]
    small_s[0:DSTATE, VEC_AT : VEC_AT + per_device] = vectors_own[KCONV + 3 :, :]
    small_s[DSTATE:GAIN, VEC_AT : VEC_AT + per_device] = vectors_own[0 : KCONV + 3, :]
    small_s[GAIN:VECS, VEC_AT : VEC_AT + gains] = gain_own[...]
    small_ref[...] = small_s[...].astype(jnp.bfloat16)
    cube.greet()
    first = gather_step(
        cube, (in_low, small_ref), (in_all, small_all), (send_sem, recv_sem, pair_send, pair_sem)
    )
    later = gather_step(cube, (out_low,), (all_out,), (send_out, recv_out, give_out, pair_out))
    own_step(cube, first)
    in_all[cube.me] = in_low[...]
    small_all[cube.me] = small_ref[...]
    own = pltpu.make_async_copy(out_low, all_out.at[cube.me], own_sem.at[0])
    own.start()

    place = lax.broadcasted_iota(jnp.int32, (length, LANES), 0)
    lane = lax.broadcasted_iota(jnp.int32, (length, LANES), 1)
    masks = jnp.ones((length, LANES), jnp.float32)
    for k in range(1, KCONV):
        same = place >= k
        start = jnp.int32(0)
        for d in range(lengths_ref.shape[1]):
            inside = jnp.logical_and(place >= start, place - k < start)
            same = jnp.logical_and(same, jnp.logical_not(inside))
            start = start + lengths_ref[0, d]
        mask_s[k - 1] = jnp.where(same, 1.0, 0.0)
        masks = jnp.where(lane == k, mask_s[k - 1], masks)
    masks_ref[...] = masks

    stage = [0]

    def between():
        stage[0] += 1
        if stage[0] == cube.places:
            own_step(cube, later)

    tokens = tokens_ref[...].astype(jnp.float32)
    inverse = lax.rsqrt(jnp.mean(tokens * tokens, axis=-1, keepdims=True) + NORM_EPS)
    normed_s[...] = tokens * inverse
    inverse_ref[...] = jnp.broadcast_to(inverse, inverse_ref.shape)
    cube.upward(first, own=False, between=between)
    for a, out in enumerate((in_all, small_all)):
        await_bytes(out.at[pl.ds(0, cube.pieces)], pair_sem.at[a])
    keep_in = pltpu.make_async_copy(in_all, all_in, own_sem.at[1])
    keep_in.start()

    def unpack(d, carry):
        at = pl.ds(pl.multiple_of(d * per_device, per_device), per_device)
        x_s[at, :] = small_all[d, 0:per_device, 0:LANES].astype(jnp.float32)
        both = small_all[d, 0:per_device, LANES : 2 * LANES].astype(jnp.float32)
        own_lanes = lax.broadcasted_iota(jnp.int32, both.shape, 1) < DTRANK
        dt_s[at, :] = jnp.where(own_lanes, both, 0.0)
        return carry

    lax.fori_loop(0, cube.shards, unpack, 0)
    x_rows[...] = x_s[...].astype(jnp.bfloat16)
    dt_rows[...] = dt_s[...].astype(jnp.bfloat16)
    for d in range(cube.shards):
        block = small_all[d, 0:32, LANES : 2 * LANES].astype(jnp.float32)[:, DTRANK:]
        vec_ref[:, d * per_device : (d + 1) * per_device] = block[0:VECS, 0:per_device]
        gain_ref[:, d * gains : (d + 1) * gains] = block[GAIN : GAIN + 1, 0:gains]

    hidden_ref[...] = (normed_s[...] * gain_ref[...]).astype(jnp.bfloat16)
    span = 2 * x_s.shape[0] // CHUNKS
    group = cube.shards // CHUNKS

    def mixed_of(chunk, many):
        weights = in_all[pl.ds(chunk * group, many * group)].reshape(many * span, width)
        return contract(hidden_ref[...], weights, 1, 1)

    def x_block(i, carry):
        cols = pl.ds(pl.multiple_of(2 * i * span, 2 * span), 2 * span)
        xpart_ref[:, cols] = mixed_of(2 * i, 2)
        return carry

    lax.fori_loop(0, CHUNKS // 4, x_block, 0)

    def x_chunk(chunk):
        base = pl.multiple_of(chunk * span, span)
        for j in range(span // LANES):
            cols = pl.ds(pl.multiple_of(base + j * LANES, LANES), LANES)
            x = xpart_ref[:, cols]
            upre = vec_ref[CBIAS : CBIAS + 1, cols] + vec_ref[TAPS : TAPS + 1, cols] * x
            for k in range(1, KCONV):
                moved = pltpu.roll(x, k, 0) * mask_s[k - 1]
                upre = upre + vec_ref[TAPS + k : TAPS + k + 1, cols] * moved
            upre_ref[:, cols] = upre
            u_ref[:, cols] = (upre * jax.nn.sigmoid(upre)).astype(jnp.bfloat16)

    def gate_chunk(chunk):
        base = pl.multiple_of((chunk - CHUNKS // 2) * span, span)
        gate_ref[:, pl.ds(base, span)] = mixed_of(chunk, 1)

    away = [
        pltpu.make_async_copy(source, target, away_sem.at[k])
        for k, (source, target) in enumerate(
            ((xpart_ref, xpart_far), (upre_ref, upre_far), (u_ref, u_far), (gate_ref, gate_far))
        )
    ]
    away[0].start()
    seen = [0]

    def halfway():
        seen[0] += 1
        if seen[0] == cube.places:
            away[1].start()
            away[2].start()

    every = cube.pieces // CHUNKS

    def work(place, k):
        run = gate_chunk if place == cube.places - 1 else x_chunk
        if every == 1:
            run(k)
        else:

            @pl.when(lax.rem(k, every) == 0)
            def _():
                run(lax.div(k, every))

    work(-1, jnp.int32(0))
    cube.upward(later, work, own=False, between=halfway)
    away[3].start()
    proj_ref[...] = jnp.dot(u_ref[...], x_rows[...], preferred_element_type=jnp.float32)
    own.wait()
    keep_in.wait()
    for copy in away:
        copy.wait()
    await_bytes(all_out.at[pl.ds(0, cube.pieces)], pair_out.at[0])
    sent = [
        (in_all, send_sem.at[0], pair_send.at[0]),
        (small_all, send_sem.at[1], pair_send.at[1]),
        (all_out, send_out.at[0], give_out.at[0]),
    ]
    for ref, sems, pair in sent:
        await_bytes(ref.at[pl.ds(0, cube.pieces)], pair)
        for route, start, count in routes_of(ref.shape[2]):
            await_passed(cube, route, ref.at[:, :, pl.ds(start, count)], sems.at[route])


def small_rows(per_device):
    return -(-max(per_device, VECS) // 16) * 16


def gather_and_front(lengths, tokens, params, fsdp, ns):
    shards = fsdp * ns
    length, width = tokens.shape
    in_proj, out_proj, x_own, unused, unused, gain = params
    per_device, gains = x_own.shape[0], gain.shape[1]
    inner = per_device * shards
    small = (small_rows(per_device), SMALL_COLUMNS)
    f32, b16 = jnp.float32, jnp.bfloat16
    held = pl.BlockSpec(memory_space=pltpu.VMEM)
    far = pl.BlockSpec(memory_space=pl.ANY)

    def shape(*dims, dtype=f32):
        return jax.ShapeDtypeStruct(dims, dtype)

    return pl.pallas_call(
        functools.partial(front_kernel, fsdp, ns, per_device, gains),
        in_specs=[pl.BlockSpec(memory_space=pltpu.SMEM)] + [held] * 7,
        out_specs=[far] * 2 + [held] * 4 + [far] * 4 + [held] * 4,
        out_shape=[
            shape(shards, *in_proj.shape, dtype=b16),
            shape(shards, *out_proj.shape, dtype=b16),
            shape(inner, LANES, dtype=b16),
            shape(inner, LANES, dtype=b16),
            shape(VECS, inner),
            shape(1, width),
            shape(length, inner),
            shape(length, inner),
            shape(length, inner),
            shape(length, inner, dtype=b16),
            shape(length, LANES),
            shape(length, LANES),
            shape(length, width, dtype=b16),
            shape(length, LANES),
        ],
        scratch_shapes=[
            pltpu.VMEM((length, inner), f32),
            pltpu.VMEM((length, inner), f32),
            pltpu.VMEM((length, inner), f32),
            pltpu.VMEM((length, inner), b16),
            pltpu.SemaphoreType.DMA((4,)),
            pltpu.VMEM((length, width), f32),
            pltpu.VMEM((shards,) + in_proj.shape, b16),
            pltpu.VMEM((shards,) + small, b16),
            pltpu.VMEM(in_proj.shape, b16),
            pltpu.VMEM(out_proj.shape, b16),
            pltpu.VMEM(small, b16),
            pltpu.VMEM(small, f32),
            pltpu.VMEM((inner, LANES), f32),
            pltpu.VMEM((inner, LANES), f32),
            pltpu.VMEM((KCONV - 1, length, LANES), f32),
            pltpu.SemaphoreType.DMA((2,)),
            pltpu.SemaphoreType.DMA((2, ROUTES, 3)),
            pltpu.SemaphoreType.DMA((2, ROUTES, fsdp // 2, ns)),
            pltpu.SemaphoreType.DMA((2,)),
            pltpu.SemaphoreType.DMA((2,)),
            pltpu.SemaphoreType.DMA((1, ROUTES, 3)),
            pltpu.SemaphoreType.DMA((1, ROUTES, fsdp // 2, ns)),
            pltpu.SemaphoreType.DMA((1,)),
            pltpu.SemaphoreType.DMA((1,)),
        ],
        compiler_params=pltpu.CompilerParams(
            collective_id=0, has_side_effects=True, vmem_limit_bytes=56 * 1024 * 1024
        ),
    )(lengths, tokens, *params)


def slots_of(cube, route):
    if route == 2:

        def over(mask, col):
            if isinstance(mask, int):
                return (2 * cube.masks + mask // cube.ns, mask % cube.ns)
            return (2 * cube.masks + lax.div(mask, cube.ns), lax.rem(mask, cube.ns))

        below = lambda mask, col: (mask, col)
        above = lambda mask, col: (cube.masks + mask, col)
        return (below, above, over, cube.masks)
    return (
        lambda mask, col: (0, col),
        lambda mask, col: (1, col),
        lambda mask, col: (mask + 1, col),
        1,
    )


def slot_count(fsdp, ns, route):
    masks = fsdp // 2
    return 2 * masks + -(-masks // ns) if route == 2 else masks + 1


def clear_ends(cube, route, land):
    many = slots_of(cube, route)[3]

    def clear(first):
        ref = land.at[pl.ds(first, many)]
        ref[...] = jnp.zeros_like(ref)

    pl.when(jnp.logical_not(cube.has_below))(lambda: clear(0))
    pl.when(jnp.logical_not(cube.has_above))(lambda: clear(many))


def arrivals(cube, route, mask, col, lines, places, wait):
    below, above, over, unused = slots_of(cube, route)
    slots = [over(mask + (1 << p), col) for p in places]
    for slot in slots:
        wait(slot)
    if "below" in lines:
        pl.when(cube.has_below)(lambda: wait(below(mask, col)))
        slots.append(below(mask, col))
    if "above" in lines:
        pl.when(cube.has_above)(lambda: wait(above(mask, col)))
        slots.append(above(mask, col))
    return slots


def hand_on(cube, route, mask, col, to, give):
    below, above, over, unused = slots_of(cube, route)
    if to == "above":
        give(below(mask, col), cube.above)
    elif to == "below":
        give(above(mask, col), cube.below)
    elif to is not None:
        give(over(mask, col), cube.partner(route, to))


def scatter_steps(cube, parts, sums, pairs, lands, sems):
    send_sem, recv_sem, pair_sem = sems

    def pieces(routes):
        for a, part in enumerate(parts):
            for k, (route, first, count) in enumerate(routes_of(part.shape[2])):
                if route in routes:
                    yield (a, route, pl.ds(first, count), pairs[a][k], lands[a][k])

    def give_pair(routes, mask, col, to, lines, places):
        for a, route, cols, pair, unused in pieces(routes):
            index = cube.at(mask, col, route) + cube.sibling_step
            send(
                parts[a].at[index, :, cols],
                pair.at[mask, col],
                send_sem.at[a],
                pair_sem.at[a, route, mask, col],
                cube.sibling,
            )

    def step(routes, mask, col, to, lines, places):
        for a, route, cols, pair, land in pieces(routes):
            index = cube.at(mask, col, route)
            rows = parts[a].shape[1]
            await_bytes(pair.at[mask, col], pair_sem.at[a, route, mask, col])

            def wait(slot):
                await_bytes(land.at[slot], recv_sem.at[(a, route) + slot])

            slots = arrivals(cube, route, mask, col, lines, places, wait)
            deep = min(rows, 16)
            for r in range(0, rows, deep):
                at = pl.ds(r, deep)
                total = parts[a][index, at, cols].astype(jnp.float32)
                total = total + pair[mask, col, at, :].astype(jnp.float32)
                for slot in slots:
                    total = total + land[slot + (at, slice(None))].astype(jnp.float32)
                if to is not None:
                    pair[mask, col, at, :] = total.astype(jnp.bfloat16)
                else:
                    sums[a][at, cols] = total

            def give(slot, device):
                send(
                    pair.at[mask, col],
                    land.at[slot],
                    send_sem.at[a],
                    recv_sem.at[(a, route) + slot],
                    device,
                )

            hand_on(cube, route, mask, col, to, give)

    return (give_pair, step)


def back_kernel(
    fsdp,
    ns,
    per_device,
    far,
    inverse_ref,
    masks_ref,
    proj_ref,
    x_rows,
    dt_rows,
    vec_ref,
    gain_ref,
    gsum_ref,
    gamat_ref,
    dbc_ref,
    all_in,
    dtok_ref,
    ggain_ref,
    sum_in,
    sum_out,
    sum_small,
    sum_vec,
    near,
    near_sem,
    part_in,
    part_small,
    small_s,
    pair_in,
    pair_out,
    pair_small,
    land_in,
    land_out,
    land_small,
    dx_s,
    dhidden_s,
    weights,
    mask_s,
    dproj_s,
    dtin_s,
    du_s,
    gx_s,
    gdt_s,
    last_s,
    load_sem,
    send_first,
    recv_first,
    pair_first,
    send_sem,
    recv_sem,
    pair_sem,
):
    copies = [
        pltpu.make_async_copy(source, target, near_sem.at[k])
        for k, (source, target) in enumerate(zip(far, near))
    ]
    for copy in copies:
        copy.start()
    (
        gout_ref,
        dgate_ref,
        hidden_ref,
        ddt_ref,
        du_ref,
        u_ref,
        upre_ref,
        xpart_ref,
        tokens_ref,
        cot_ref,
    ) = near
    cube = Cube(fsdp, ns)
    length, width = tokens_ref.shape
    inner = x_rows.shape[0]
    cube.greet()
    give_out, step_out = scatter_steps(
        cube, (gout_ref,), (sum_out,), (pair_out,), (land_out,), (send_first, recv_first, pair_first)
    )
    give_in, step_in = scatter_steps(
        cube,
        (part_in, part_small),
        (sum_in, sum_small),
        (pair_in, pair_small),
        (land_in, land_small),
        (send_sem, recv_sem, pair_sem),
    )
    copies[0].wait()
    cube.downward(give_out)
    for part, land in ((gout_ref, land_out), (part_in, land_in), (part_small, land_small)):
        for (route, unused, unused), where in zip(routes_of(part.shape[2]), land):
            clear_ends(cube, route, where)

    group = BAND // part_in.shape[1]

    def into_part(first, source):
        def band(i, carry):
            cols = pl.ds(pl.multiple_of(i * BAND, BAND), BAND)
            gradient = contract(source[:, cols], hidden_ref[...], 0, 0).astype(jnp.bfloat16)
            at = pl.ds(first + i * group, group)
            part_in[at] = gradient.reshape(group, part_in.shape[1], width)
            return carry

        lax.fori_loop(0, inner // BAND, band, 0)

    for copy in copies[1:3]:
        copy.wait()
    into_part(cube.shards // 2, dgate_ref)
    for k in range(1, KCONV):
        mask_s[k - 1] = jnp.broadcast_to(masks_ref[:, k : k + 1], (length, LANES))
    for copy in copies[3:]:
        copy.wait()
    d_dtin = jnp.dot(ddt_ref[...], dt_rows[...], preferred_element_type=jnp.float32)
    dproj_s[...] = (d_dtin + dbc_ref[...]).astype(jnp.bfloat16)
    lane = lax.broadcasted_iota(jnp.int32, (length, LANES), 1)
    dtin_s[...] = jnp.where(lane < DTRANK, proj_ref[...], 0.0).astype(jnp.bfloat16)
    sub = lax.broadcasted_iota(jnp.int32, (SUBS, LANES), 0)

    def state_band(i, carry):
        at = pl.ds(pl.multiple_of(i * BAND, BAND), BAND)
        du_s[:, at] = du_ref[:, at] + contract(dproj_s[...], x_rows[at, :], 1, 1)
        gx_s[at, :] = contract(u_ref[:, at], dproj_s[...], 0, 0)
        gdt_s[at, :] = contract(ddt_ref[:, at], dtin_s[...], 0, 0)
        return carry

    lax.fori_loop(0, inner // BAND, state_band, 0)

    def x_chunk(chunk):
        cols = pl.ds(pl.multiple_of(chunk * LANES, LANES), LANES)
        x, upre = xpart_ref[:, cols], upre_ref[:, cols]
        sig = jax.nn.sigmoid(upre)
        dpre = du_s[:, cols] * sig * (1.0 + upre * (1.0 - sig))
        dx = vec_ref[TAPS : TAPS + 1, cols] * dpre
        sums = [jnp.sum(dpre * x, axis=0, keepdims=True)]
        for k in range(1, KCONV):
            masked = mask_s[k - 1] * dpre
            dx = dx + vec_ref[TAPS + k : TAPS + k + 1, cols] * pltpu.roll(masked, length - k, 0)
            sums.append(jnp.sum(masked * pltpu.roll(x, k, 0), axis=0, keepdims=True))
        sums.append(jnp.sum(dpre, axis=0, keepdims=True))
        sums.append(jnp.sum(gsum_ref[SUBS : 2 * SUBS, cols], axis=0, keepdims=True))
        sums.append(jnp.sum(gsum_ref[0:SUBS, cols], axis=0, keepdims=True))
        last = jnp.zeros((SUBS, LANES), jnp.float32)
        for k, value in enumerate(sums):
            last = jnp.where(sub == k, value, last)
        last_s[:, cols] = last
        dx_s[:, cols] = dx.astype(jnp.bfloat16)

    steps = ns << (cube.places - 1)
    many = max(CHUNKS // steps, 1)
    every = max(steps // CHUNKS, 1)

    def x_chunks(place, k):
        def run():
            for i in range(many):
                x_chunk((k if every == 1 else lax.div(k, every)) * many + i)

        if every == 1:
            run()
        else:
            pl.when(lax.rem(k, every) == 0)(run)

    cube.down_stage(0, step_out, x_chunks)
    into_part(0, dx_s)

    small_s[...] = jnp.zeros_like(small_s)
    owners = LANES // per_device

    def small_chunk(chunk, carry):
        cols = pl.ds(pl.multiple_of(chunk * LANES, LANES), LANES)
        shape = (owners, per_device, LANES)
        small_s[:, 0:per_device, 0:LANES] = gx_s[cols, :].reshape(shape)
        small_s[:, 0:per_device, LANES:VEC_AT] = gdt_s[cols, :].reshape(shape)[:, :, 0:DTRANK]
        rates, last = gamat_ref[:, cols], last_s[:, cols]
        for o in range(owners):
            mine = slice(o * per_device, (o + 1) * per_device)
            small_s[o, 0:DSTATE, VEC_AT : VEC_AT + per_device] = rates[:, mine]
            small_s[o, DSTATE:VECS, VEC_AT : VEC_AT + per_device] = last[:, mine]
        part_small[pl.ds(chunk * owners, owners)] = small_s[...].astype(jnp.bfloat16)
        return carry

    lax.fori_loop(0, inner // LANES, small_chunk, 0)
    cube.downward(give_in)

    share = cube.shards // CHUNKS
    span = 2 * inner // CHUNKS

    def load(chunk):
        slot = lax.rem(chunk, 2)
        return pltpu.make_async_copy(
            all_in.at[pl.ds(chunk * share, share)], weights.at[slot], load_sem.at[slot]
        )

    dhidden_s[...] = jnp.zeros_like(dhidden_s)
    load(jnp.int32(0)).start()

    def hidden_chunk(chunk, left, base):
        load(chunk).wait()
        pl.when(chunk + 1 < CHUNKS)(lambda: load(chunk + 1).start())
        cols = pl.ds(pl.multiple_of((chunk - base) * span, span), span)
        right = weights[lax.rem(chunk, 2)].reshape(span, width)
        dhidden_s[...] += jnp.dot(left[:, cols], right, preferred_element_type=jnp.float32)

    def tokens_rows(i, total):
        at = pl.ds(pl.multiple_of(i * 16, 16), 16)
        inverse = inverse_ref[at, 0:1]
        normed = tokens_ref[at, :].astype(jnp.float32) * inverse
        dhidden = dhidden_s[at, :]
        product = dhidden * normed
        scaled = dhidden * gain_ref[...]
        mean = jnp.mean(scaled * normed, axis=-1, keepdims=True)
        dtok_ref[at, :] = cot_ref[at, :].astype(jnp.float32) + inverse * (scaled - normed * mean)
        return total + product[0:8] + product[8:16]

    part = CHUNKS // 2

    def hidden_chunks(first, last, left, base):
        def body(chunk, carry):
            hidden_chunk(chunk, left, base)
            return carry

        lax.fori_loop(first, last, body, 0)

    for stage in range(cube.places + 2):
        if stage < cube.places + 1:
            cube.down_stage(stage + 1, step_out)
        cube.down_stage(stage, step_in)
        if stage == 0:
            hidden_chunks(0, part, dx_s, 0)
        if stage == 1:
            hidden_chunks(part, CHUNKS, dgate_ref, part)
        if stage == cube.places:
            zero = jnp.zeros((SUBS, width), jnp.float32)
            total = lax.fori_loop(0, length // 16, tokens_rows, zero)
            row = jnp.sum(total, axis=0, keepdims=True)
            ggain_ref[...] = jnp.zeros_like(ggain_ref)
            for k in range(width // LANES):
                ggain_ref[k : k + 1, :] = row[:, k * LANES : (k + 1) * LANES]
    vectors = sum_small[0:VECS, VEC_AT : VEC_AT + per_device]
    sum_vec[0 : KCONV + 3, :] = vectors[DSTATE:GAIN, :]
    sum_vec[KCONV + 3 :, :] = vectors[0:DSTATE, :]
    await_bytes(gout_ref.at[pl.ds(0, cube.shards - 1)], send_first.at[0])
    await_bytes(part_in.at[pl.ds(0, cube.shards - 1)], send_sem.at[0])
    await_bytes(part_small.at[pl.ds(0, cube.shards - 1)], send_sem.at[1])


def back_and_scatter(far, arrays, all_in, per_device, small, fsdp, ns):
    length, width = arrays[0].shape[0], all_in.shape[2]
    inner = per_device * fsdp * ns
    shards, masks = fsdp * ns, fsdp // 2
    f32, b16 = jnp.float32, jnp.bfloat16
    blocks = [(2 * per_device, width), (per_device, width), (small, SMALL_COLUMNS)]

    def inbox(slots):
        return [
            [
                pltpu.VMEM((slots(route), ns, rows, count), b16)
                for route, unused, count in routes_of(columns)
            ]
            for rows, columns in blocks
        ]

    most = slot_count(fsdp, ns, 2)
    return pl.pallas_call(
        functools.partial(back_kernel, fsdp, ns, per_device),
        in_specs=[
            [pl.BlockSpec(memory_space=pl.ANY)] * len(far),
            *[pl.BlockSpec(memory_space=pltpu.VMEM)] * len(arrays),
            pl.BlockSpec(memory_space=pl.ANY),
        ],
        out_specs=[pl.BlockSpec(memory_space=pltpu.VMEM)] * 6,
        out_shape=[
            jax.ShapeDtypeStruct((length, width), f32),
            jax.ShapeDtypeStruct((-(-width // LANES // 16) * 16, LANES), f32),
        ]
        + [jax.ShapeDtypeStruct(block, f32) for block in blocks]
        + [jax.ShapeDtypeStruct((GAIN, per_device), f32)],
        scratch_shapes=[
            [pltpu.VMEM(array.shape, array.dtype) for array in far],
            pltpu.SemaphoreType.DMA((len(far),)),
            pltpu.VMEM((shards,) + blocks[0], b16),
            pltpu.VMEM((shards,) + blocks[2], b16),
            pltpu.VMEM((LANES // per_device,) + blocks[2], f32),
        ]
        + inbox(lambda route: masks)
        + inbox(functools.partial(slot_count, fsdp, ns))
        + [
            pltpu.VMEM((length, inner), b16),
            pltpu.VMEM((length, width), f32),
            pltpu.VMEM((2, shards // CHUNKS) + blocks[0], b16),
            pltpu.VMEM((KCONV - 1, length, LANES), f32),
            pltpu.VMEM((length, LANES), b16),
            pltpu.VMEM((length, LANES), b16),
            pltpu.VMEM((length, inner), f32),
            pltpu.VMEM((inner, LANES), f32),
            pltpu.VMEM((inner, LANES), f32),
            pltpu.VMEM((SUBS, inner), f32),
            pltpu.SemaphoreType.DMA((2,)),
            pltpu.SemaphoreType.DMA((1,)),
            pltpu.SemaphoreType.DMA((1, ROUTES, most, ns)),
            pltpu.SemaphoreType.DMA((1, ROUTES, masks, ns)),
            pltpu.SemaphoreType.DMA((2,)),
            pltpu.SemaphoreType.DMA((2, ROUTES, most, ns)),
            pltpu.SemaphoreType.DMA((2, ROUTES, masks, ns)),
        ],
        compiler_params=pltpu.CompilerParams(
            collective_id=1, has_side_effects=True, vmem_limit_bytes=60 * 1024 * 1024
        ),
    )(far, *arrays, all_in)


def halves_of(deep, wide):
    if deep >= 32:
        return [(g, (g * (deep // 2), deep // 2), (0, wide)) for g in range(2)]
    return [(g, (0, deep), (first, count)) for g, first, count in routes_of(wide, wide)]


def muon_kernel(
    fsdp,
    ns,
    starts,
    sum_in,
    sum_out,
    in_moment,
    out_moment,
    low_ref,
    gain_ref,
    x_out,
    low_out,
    gain_out,
    rows_s,
    turn,
    back_s,
    mine,
    outbox,
    lands,
    pieces_s,
    gram,
    now,
    poly,
    small_now,
    small_land,
    small_gram,
    low_s,
    send_sem,
    gather_sem,
    recv_sem,
    came_sem,
    swap_sem,
    small_send,
    small_recv,
):
    cube = Cube(fsdp, ns)
    pieces, deep, wide = pieces_s.shape
    width = now.shape[0]
    rows = sum_in.shape[0]
    blocks = width // LANES
    each = LANES // deep
    split = halves_of(deep, wide)
    ways = [cube.sibling] + [cube.partner(0, place) for place in range(cube.places)]
    ways += [(cube.row, flipped(cube.col, 1 << k)) for k in range(ns.bit_length() - 1)]
    stages = len(ways)
    cube.greet(ways[cube.places + 2 :])

    short = sum_out.shape[0]
    rows_s[0] = (MOMENTUM * in_moment[...] + sum_in[...]).astype(jnp.bfloat16)
    rows_s[1, 0:short, :] = (MOMENTUM * out_moment[...] + sum_out[...]).astype(jnp.bfloat16)
    rows_s[1, short:, :] = jnp.zeros((rows - short, width), jnp.bfloat16)

    def swap(source, target, which):
        return pltpu.make_async_remote_copy(
            src_ref=source,
            dst_ref=target,
            send_sem=swap_sem.at[which, 0],
            recv_sem=swap_sem.at[which, 1],
            device_id=cube.sibling,
            device_id_type=MESH,
        )

    there = swap(rows_s.at[1 - cube.core], turn.at[pl.ds(rows, rows)], 0)
    there.start()
    turn[0:rows] = rows_s[cube.core]

    def small_copy(k):
        return pltpu.make_async_remote_copy(
            src_ref=small_now.at[k],
            dst_ref=small_land.at[k],
            send_sem=small_send.at[k],
            recv_sem=small_recv.at[k],
            device_id=ways[k],
            device_id_type=MESH,
        )

    def inverse(total):
        return 1.0 / (jnp.sqrt(jnp.full((1, 1), total, jnp.float32)) + FROB_EPS)

    def diagonal(block):
        on = lax.broadcasted_iota(jnp.int32, block.shape, 0) == lax.broadcasted_iota(
            jnp.int32, block.shape, 1
        )
        return jnp.sum(jnp.where(on, block, 0.0))

    def small_step(k):
        small_copy(k).wait()
        total = small_now[k].astype(jnp.float32) + small_land[k].astype(jnp.float32)
        if k + 1 < stages:
            small_now[k + 1] = total.astype(jnp.bfloat16)
            small_copy(k + 1).start()
            return
        gain_out[...] = total[starts[2] :]
        for which in range(2):
            deep = starts[which + 1] - starts[which]
            whole = jnp.pad(total[starts[which] : starts[which + 1]], ((0, LANES - deep), (0, 0)))
            scale = inverse(diagonal(whole))
            small_gram[which] = whole * (scale * scale)
            low_s[which] = (low_ref[which] * scale).astype(jnp.bfloat16)

    for which in range(2):
        low = low_ref[which].astype(jnp.bfloat16)
        term = contract(low, low, 0, 0)[0 : starts[which + 1] - starts[which]]
        small_now[0, starts[which] : starts[which + 1], :] = term.astype(jnp.bfloat16)
    small_now[0, starts[2] :, :] = gain_ref[...].astype(jnp.bfloat16)
    small_copy(0).start()
    left = list(range(stages))

    def between():
        if left:
            small_step(left.pop(0))

    for (route, unused, unused), land in zip(split, lands):
        clear_ends(cube, route, land)

    there.wait()
    for b in range(blocks):
        if b % 2 == 0:
            band = contract(turn[:, b * LANES : (b + 2) * LANES], turn[...], 0, 0)
        block = band[b % 2 * LANES : (b % 2 + 1) * LANES]
        for c in range(wide // LANES):
            at = (b + c) % blocks * LANES
            for r in range(each):
                strip = block[r * deep : (r + 1) * deep, at : at + LANES]
                mine[b * each + r, :, c * LANES : (c + 1) * LANES] = strip

    def step(routes, mask, col, to, lines, places):
        for (route, rows_at, cols_at), land in zip(split, lands):
            if route not in routes:
                continue
            at = (cube.spot(mask, col, route), pl.ds(*rows_at), pl.ds(*cols_at))

            def wait(slot):
                await_bytes(land.at[slot], recv_sem.at[(route,) + slot])

            total = mine[at]
            for slot in arrivals(cube, route, mask, col, lines, places, wait):
                total = total + land[slot].astype(jnp.float32)
            if to is not None:
                outbox[at] = total.astype(jnp.bfloat16)
            else:
                pieces_s[at] = total.astype(jnp.bfloat16)

            def give(slot, device):
                send(
                    outbox.at[at],
                    land.at[slot],
                    send_sem,
                    recv_sem.at[(route,) + slot],
                    device,
                )

            hand_on(cube, route, mask, col, to, give)

    for stage in range(cube.places + 2):
        cube.down_stage(stage, step, third=False)
        if stage <= cube.places:
            between()

    def spread(routes, mask, col, ways, places, own):
        for route, rows_at, cols_at in split:
            if route not in routes:
                continue
            block = pieces_s.at[cube.spot(mask, col, route), pl.ds(*rows_at), pl.ds(*cols_at)]

            def sem_of(mask, col):
                return came_sem.at[route, mask, col]

            if not own:
                await_bytes(block, sem_of(mask, col))
            sems = gather_sem.at[route]
            pass_on(cube, route, mask, col, ways, places, block, block, sems, sem_of)

    def small_newton():
        for which in range(2):
            whole = small_gram[which]
            low = whole.astype(jnp.bfloat16)
            power = jnp.dot(low, low, preferred_element_type=jnp.float32)
            mixed = (COEF_B * whole + COEF_C * power).astype(jnp.bfloat16)
            block = low_s[which]
            low_s[which] = (
                COEF_A * block.astype(jnp.float32)
                + jnp.dot(block, mixed, preferred_element_type=jnp.float32)
            ).astype(jnp.bfloat16)
            half = COEF_A * whole + jnp.dot(low, mixed, preferred_element_type=jnp.float32)
            small_gram[which] = COEF_A * half + jnp.dot(
                half.astype(jnp.bfloat16), mixed, preferred_element_type=jnp.float32
            )

    def after(place, k):
        if place == cube.places - 1:
            pl.when(k - (ns << place) < NS_STEPS)(small_newton)

    cube.upward(spread, after=after, between=between, third=False)
    low_out[...] = low_s[...]

    for b in range(blocks):
        for c in range(wide // LANES):
            at = (b + c) % blocks * LANES
            for r in range(each):
                now[b * LANES + r * deep : b * LANES + (r + 1) * deep, at : at + LANES] = pieces_s[
                    b * each + r, :, c * LANES : (c + 1) * LANES
                ]
    for b in range(blocks):
        for c in range(wide // LANES, blocks):
            other = (b + c) % blocks
            block = now[other * LANES : (other + 1) * LANES, b * LANES : (b + 1) * LANES]
            flip = block.astype(jnp.float32).T.astype(jnp.bfloat16)
            now[b * LANES : (b + 1) * LANES, other * LANES : (other + 1) * LANES] = flip

    total = jnp.zeros((), jnp.float32)
    for b in range(0, width, LANES):
        total = total + diagonal(now[b : b + LANES, b : b + LANES].astype(jnp.float32))
    factor = inverse(total)
    square = factor * factor
    strip = min(BAND, width)

    def turned(block, k):
        moved = COEF_A * block.astype(jnp.float32) + jnp.dot(
            block, poly[...], preferred_element_type=jnp.float32
        )
        if k == 0:
            moved = moved * factor
        return moved.astype(jnp.bfloat16)

    for k in range(NS_STEPS):

        def poly_strip(i, carry, k=k):
            at = pl.ds(pl.multiple_of(i * strip, strip), strip)
            low = now[at, :]
            power = jnp.dot(low, now[...], preferred_element_type=jnp.float32)
            if k == 0:
                mixed = COEF_B * square * low.astype(jnp.float32) + (COEF_C * square * square) * power
            else:
                mixed = COEF_B * gram[at, :] + COEF_C * power
            poly[at, :] = mixed.astype(jnp.bfloat16)
            return carry

        lax.fori_loop(0, width // strip, poly_strip, 0)
        if k + 1 == NS_STEPS:
            break
        turn[...] = turned(turn[...], k)

        def gram_strip(i, carry, k=k):
            at = pl.ds(pl.multiple_of(i * strip, strip), strip)
            low = now[at, :]
            full = low.astype(jnp.float32) if k == 0 else gram[at, :]
            half = COEF_A * full + jnp.dot(low, poly[...], preferred_element_type=jnp.float32)
            if k == 0:
                half = half * square
            renewed = COEF_A * half + jnp.dot(
                half.astype(jnp.bfloat16), poly[...], preferred_element_type=jnp.float32
            )
            gram[at, :] = renewed
            now[at, :] = renewed.astype(jnp.bfloat16)
            return carry

        lax.fori_loop(0, width // strip, gram_strip, 0)
    turn[rows:] = turned(turn[rows:], NS_STEPS - 1)
    home = swap(turn.at[pl.ds(rows, rows)], back_s, 1)
    home.start()
    x_out[cube.core] = turned(turn[0:rows], NS_STEPS - 1)
    home.wait()
    x_out[1 - cube.core] = back_s[...]
    await_bytes(outbox.at[pl.ds(0, pieces - 1)], send_sem)
    for route, rows_at, cols_at in split:
        sent = pieces_s.at[:, pl.ds(*rows_at), pl.ds(*cols_at)]
        await_passed(cube, route, sent, gather_sem.at[route])


def muon_rows(sum_in, sum_out, in_moment, out_moment, low, columns, gain, fsdp, ns):
    pieces = fsdp * ns // 2
    rows, width = sum_in.shape
    wide = (width // LANES // 2 + 1) * LANES
    deep = width // pieces
    block = (pieces, deep, wide)
    stages = (fsdp * ns).bit_length() - 1
    starts = (0, columns[0], sum(columns))
    small = (sum(columns) + gain.shape[0], LANES)
    f32, b16 = jnp.float32, jnp.bfloat16
    landing = [
        pltpu.VMEM((slot_count(fsdp, ns, route), ns, rows_at[1], cols_at[1]), b16)
        for route, rows_at, cols_at in halves_of(deep, wide)
    ]
    held = pl.BlockSpec(memory_space=pltpu.VMEM)
    return pl.pallas_call(
        functools.partial(muon_kernel, fsdp, ns, starts),
        in_specs=[held] * 6,
        out_specs=[held] * 3,
        out_shape=[
            jax.ShapeDtypeStruct((2, rows, width), b16),
            jax.ShapeDtypeStruct(low.shape, b16),
            jax.ShapeDtypeStruct(gain.shape, f32),
        ],
        scratch_shapes=[
            pltpu.VMEM((2, rows, width), b16),
            pltpu.VMEM((2 * rows, width), b16),
            pltpu.VMEM((rows, width), b16),
            pltpu.VMEM(block, f32),
            pltpu.VMEM(block, b16),
        ]
        + [
            landing,
            pltpu.VMEM(block, b16),
            pltpu.VMEM((width, width), f32),
            pltpu.VMEM((width, width), b16),
            pltpu.VMEM((width, width), b16),
            pltpu.VMEM((stages,) + small, b16),
            pltpu.VMEM((stages,) + small, b16),
            pltpu.VMEM((2, LANES, LANES), f32),
            pltpu.VMEM(low.shape, b16),
            pltpu.SemaphoreType.DMA,
            pltpu.SemaphoreType.DMA((ROUTES, 3)),
            pltpu.SemaphoreType.DMA((ROUTES, slot_count(fsdp, ns, 2), ns)),
            pltpu.SemaphoreType.DMA((ROUTES, fsdp // 2, ns)),
            pltpu.SemaphoreType.DMA((2, 2)),
            pltpu.SemaphoreType.DMA((stages,)),
            pltpu.SemaphoreType.DMA((stages,)),
        ],
        compiler_params=pltpu.CompilerParams(
            collective_id=2, has_side_effects=True, vmem_limit_bytes=48 * 1024 * 1024
        ),
    )(sum_in, sum_out, in_moment, out_moment, low, gain)


def layer(tokens, out_grad, lengths, params, fsdp, ns):
    flat_low, grad_flat = tokens[0], out_grad[0]
    length, width = flat_low.shape
    (
        all_in,
        all_out,
        x_rows,
        dt_rows,
        vecs,
        gain,
        x_part,
        gate_in,
        conv_flat,
        u_low,
        proj,
        masks,
        hidden,
        inverse,
    ) = gather_and_front(lengths, flat_low, params, fsdp, ns)
    per_device = params[2].shape[0]
    inner = x_rows.shape[0]
    out_low = all_out.reshape(inner, width)
    d_gate, d_u, d_dtlow, vec_parts, grad_amat, d_bc, grad_out, block_out = scan_both(
        proj, masks, dt_rows, u_low, gate_in, flat_low, grad_flat, out_low, vecs
    )
    d_tokens, grad_gain, sum_in, sum_out, sum_small, sum_vec = back_and_scatter(
        [
            grad_out.reshape(fsdp * ns, per_device, width),
            d_gate,
            hidden,
            d_dtlow,
            d_u,
            u_low,
            conv_flat,
            x_part,
            flat_low,
            grad_flat,
        ],
        (inverse, masks, proj, x_rows, dt_rows, vecs, gain, vec_parts, grad_amat, d_bc),
        all_in,
        per_device,
        small_rows(per_device),
        fsdp,
        ns,
    )
    return (block_out[None], d_tokens[None], grad_gain, sum_in, sum_out, sum_small, sum_vec)


def adamw_update(param, first, second, grad):
    first_new = FIRST_MOMENT_BETA * first + (1.0 - FIRST_MOMENT_BETA) * grad
    second_new = BETA_SECOND * second + (1.0 - BETA_SECOND) * grad * grad
    first_hat = first_new / (1.0 - FIRST_MOMENT_BETA**STEP_NO)
    second_hat = second_new / (1.0 - BETA_SECOND**STEP_NO)
    param_new = param * (1.0 - ADAM_RATE * ADAM_DECAY) - ADAM_RATE * first_hat / (
        jnp.sqrt(second_hat) + ADAM_EPS
    )
    return (param_new, first_new, second_new)


def on_device(
    tokens,
    out_grad,
    doc_lengths,
    in_proj,
    inner_projection_weight,
    dt_proj,
    out_proj,
    in_moment,
    x_moment,
    dt_moment,
    out_moment,
    vectors,
    vector_first,
    vector_second,
    norm_gain,
    gain_first,
    gain_second,
):
    fsdp, ns = lax.axis_size("fsdp"), lax.axis_size("ns")
    shards = fsdp * ns
    per_device, columns = inner_projection_weight.shape
    rank, gains = dt_proj.shape[1], norm_gain.shape[0]
    block_out, grad_tokens, grad_gain, sum_in, sum_out, sum_small, sum_vec = layer(
        tokens,
        out_grad,
        doc_lengths,
        (
            in_proj,
            out_proj,
            inner_projection_weight,
            dt_proj,
            vectors,
            norm_gain[None],
        ),
        fsdp,
        ns,
    )
    sum_x = sum_small[:per_device, :columns]
    sum_dt = sum_small[:per_device, LANES : LANES + rank]
    summed = (sum_in, sum_x, sum_dt, sum_out, sum_vec)
    old_moments = (in_moment, x_moment, dt_moment, out_moment)
    moments = tuple((MOMENTUM * moment + grad for moment, grad in zip(old_moments, summed[:4])))
    gap = -per_device % 16
    low = jnp.stack(
        [
            jnp.pad(moments[1], ((0, gap), (0, LANES - columns))),
            jnp.pad(moments[2], ((0, gap), (0, LANES - rank))),
        ]
    )
    big, low, sum_gain = muon_rows(
        sum_in, sum_out, in_moment, out_moment, low, (columns, rank), grad_gain, fsdp, ns
    )
    place = lax.axis_index("fsdp") * ns + lax.axis_index("ns")
    sum_gain = lax.dynamic_slice_in_dim(sum_gain.reshape(-1), place * gains, gains, 0)
    own_blocks = (
        big[0],
        low[0, :per_device, :columns],
        low[1, :per_device, :rank],
        big[1, :per_device],
    )
    weights = (in_proj, inner_projection_weight, dt_proj, out_proj)
    fans = (DMODEL, DINNER, DTRANK, DINNER // 8)
    results = []
    for weight, moment, block, fan in zip(weights, moments, own_blocks, fans):
        rate = 0.5 * math.sqrt(weight.shape[0] * shards / fan)
        results.append((1.0 - SHRINK) * weight - rate * block.astype(jnp.float32))
        results.append(moment)
    vec_new, vec_first, vec_second = adamw_update(vectors, vector_first, vector_second, summed[4])
    gain_new, gain_m, gain_v = adamw_update(norm_gain, gain_first, gain_second, sum_gain)
    return (
        block_out,
        grad_tokens,
        results[0],
        results[1],
        results[2],
        results[3],
        results[4],
        results[5],
        results[6],
        results[7],
        vec_new,
        vec_first,
        vec_second,
        gain_new,
        gain_m,
        gain_v,
    )


def solution(mesh):
    placed = (
        P(("fsdp", "ns"), None, None),
        P(("fsdp", "ns"), None, None),
        P(("fsdp", "ns"), None),
        P(("fsdp", "ns"), None),
        P(("fsdp", "ns"), None),
        P(("fsdp", "ns"), None),
        P(("fsdp", "ns"), None),
        P(("fsdp", "ns"), None),
        P(("fsdp", "ns"), None),
        P(("fsdp", "ns"), None),
        P(("fsdp", "ns"), None),
        P(None, ("fsdp", "ns")),
        P(None, ("fsdp", "ns")),
        P(None, ("fsdp", "ns")),
        P(("fsdp", "ns")),
        P(("fsdp", "ns")),
        P(("fsdp", "ns")),
    )
    return jax.shard_map(
        on_device,
        mesh=mesh,
        in_specs=placed,
        out_specs=(
            P(("fsdp", "ns"), None, None),
            P(("fsdp", "ns"), None, None),
            P(("fsdp", "ns"), None),
            P(("fsdp", "ns"), None),
            P(("fsdp", "ns"), None),
            P(("fsdp", "ns"), None),
            P(("fsdp", "ns"), None),
            P(("fsdp", "ns"), None),
            P(("fsdp", "ns"), None),
            P(("fsdp", "ns"), None),
            P(None, ("fsdp", "ns")),
            P(None, ("fsdp", "ns")),
            P(None, ("fsdp", "ns")),
            P(("fsdp", "ns")),
            P(("fsdp", "ns")),
            P(("fsdp", "ns")),
        ),
        check_vma=False,
    )
```

```python
import functools
import math

import jax
import jax.numpy as jnp
from jax import lax
from jax.experimental import pallas as pl
from jax.experimental.pallas import tpu as pltpu
from jax.sharding import PartitionSpec as P

DMODEL = 1024
DINNER = 2048
DSTATE = 16
DTRANK = 64
KCONV = 4
NS_STEPS = 4
STEP_NO = 10


NORM_EPS = 1e-05
FROB_EPS = 1e-07
COEF_A = 3.4445
COEF_B = -4.775
COEF_C = 2.0315
MOMENTUM = 0.95
SHRINK = 0.001
FIRST_MOMENT_BETA = 0.9
BETA_SECOND = 0.95
ADAM_EPS = 1e-08
ADAM_RATE = 1.0
ADAM_DECAY = 0.001


def contract(left, right, left_dim, right_dim):
    return lax.dot_general(
        left, right, (((left_dim,), (right_dim,)), ((), ())), preferred_element_type=jnp.float32
    )


MESH = pl.DeviceIdType.MESH
LANES = 128
SUBS = 8
PASS = LANES * SUBS
STEPS = 4
RESET = 1.0e4
LOG2E = math.log2(math.e)
LN2 = math.log(2.0)
TAPS = DSTATE
CBIAS = TAPS + KCONV
DTBIAS = CBIAS + 1
SKIP = CBIAS + 2
GAIN = CBIAS + 3
VECS = CBIAS + 4
CHUNKS = 16
BAND = 512
SMALL_COLUMNS = 2 * LANES
VEC_AT = LANES + DTRANK


def lane_tile(j):
    return pl.ds(j * LANES, LANES)


def scan_kernel(
    bc_ref,
    proj_ref,
    masks_ref,
    dtw_ref,
    u_ref,
    gate_ref,
    tokens_ref,
    cot_ref,
    outw_ref,
    vec_ref,
    dgate_ref,
    du_ref,
    ddt_ref,
    gsum_ref,
    gamat_ref,
    dbc_ref,
    gout_ref,
    block_ref,
    gated_s,
    amat_s,
    gamat_s,
    pre_s,
    dg_s,
    delta_s,
    dec_s,
    drive_s,
    dstate_s,
    y_s,
    pull_s,
    ddelta_s,
    states,
    prod_a,
    prod_b,
    sums_b,
    sums_c,
):
    length = u_ref.shape[0]
    half = pl.program_id(0)
    bias_row = vec_ref[DTBIAS : DTBIAS + 1, :]

    pre_s[...] = contract(proj_ref[...].astype(jnp.bfloat16), dtw_ref[...], 1, 1) + bias_row
    dg_s[...] = contract(cot_ref[...], outw_ref[...], 1, 1)

    for j in range(SUBS):
        rates = -LOG2E * jnp.exp(vec_ref[0:DSTATE, j * LANES : (j + 1) * LANES])
        amat_s[pl.ds(j, DSTATE, stride=SUBS), :] = rates

    def amat_of(n):
        return amat_s[n * SUBS : (n + 1) * SUBS, :]

    rows = 16

    def prepare(i, carry):
        r = pl.multiple_of(i * rows, rows)
        keep = masks_ref[pl.ds(r, rows), 1:2] > 0.0
        for j in range(SUBS):
            at = (pl.ds(r, rows), lane_tile(j))
            delta = jax.nn.softplus(pre_s[at])
            u = u_ref[at].astype(jnp.float32)
            gate = gate_ref[at]
            delta_s[at] = delta
            to = (pl.ds(r * SUBS + j, rows, stride=SUBS), slice(None))
            dec_s[to] = jnp.where(keep, delta, RESET)
            drive_s[to] = delta * u
            dstate_s[to] = dg_s[at] * (gate * jax.nn.sigmoid(gate))
        return carry

    lax.fori_loop(0, length // rows, prepare, 0)

    for n in range(DSTATE):
        states[n] = jnp.zeros((SUBS, LANES), jnp.float32)

    def tile_of(ref, t):
        return ref[pl.ds(pl.multiple_of(t * SUBS, SUBS), SUBS), :]

    def put_tile(ref, t, value):
        ref[pl.ds(pl.multiple_of(t * SUBS, SUBS), SUBS), :] = value

    def ahead(i, carry):
        state = list(carry)
        for k in range(STEPS):
            t = i * STEPS + k
            dec, drive = tile_of(dec_s, t), tile_of(drive_s, t)
            parts = [None, None]
            for n in range(DSTATE):
                s = jnp.exp2(dec * amat_of(n)) * state[n] + drive * bc_ref[t, DTRANK + n]
                state[n] = s
                states[(t + 1) * DSTATE + n] = s
                term = s * bc_ref[t, DTRANK + DSTATE + n]
                parts[n % 2] = term if parts[n % 2] is None else parts[n % 2] + term
            put_tile(y_s, t, parts[0] + parts[1])
        return tuple(state)

    zero = jnp.zeros((SUBS, LANES), jnp.float32)
    lax.fori_loop(0, length // STEPS, ahead, (zero,) * DSTATE)

    fold = SUBS // 2
    span = DSTATE * fold
    pick = (
        lax.broadcasted_iota(jnp.int32, (STEPS * DSTATE, STEPS * span), 1) // fold
        == lax.broadcasted_iota(jnp.int32, (STEPS * DSTATE, STEPS * span), 0)
    ).astype(jnp.bfloat16)
    upper = lax.broadcasted_iota(jnp.int32, (SUBS, LANES), 0) < fold

    def folded(one, two):
        crossed = pltpu.roll(jnp.where(upper, two, one), fold, 0)
        return jnp.where(upper, one, two) + crossed

    def channel_sums(products, t0):
        row = pl.multiple_of(t0 * DSTATE, STEPS * DSTATE)
        both = jnp.dot(pick, products[...], preferred_element_type=jnp.float32)
        sums_b[pl.ds(row, STEPS * DSTATE), :] = both[:, 0:LANES]
        sums_c[pl.ds(row, STEPS * DSTATE), :] = both[:, LANES : 2 * LANES]

    def behind_steps(t0, products, flow, g_amat):
        for k in reversed(range(STEPS)):
            t = t0 + k
            dec, drive, dstate = tile_of(dec_s, t), tile_of(drive_s, t), tile_of(dstate_s, t)
            pull, back = [None, None], [None, None]
            pend_b, pend_c = None, None
            for n in range(DSTATE):
                amat = amat_of(n)
                adj = dstate * bc_ref[t, DTRANK + DSTATE + n] + flow[n]
                term = adj * bc_ref[t, DTRANK + n]
                pull[n % 2] = term if pull[n % 2] is None else pull[n % 2] + term
                flow[n] = jnp.exp2(dec * amat) * adj
                weighted = flow[n] * states[t * DSTATE + n]
                g_amat[n] = g_amat[n] + weighted * dec
                term = weighted * amat
                back[n % 2] = term if back[n % 2] is None else back[n % 2] + term
                prod_b_n = adj * drive
                prod_c_n = states[(t + 1) * DSTATE + n] * dstate
                if n % 2:
                    pair_b, pair_c = folded(pend_b, prod_b_n), folded(pend_c, prod_c_n)
                if n % 4 == 1:
                    half_b, half_c = pair_b, pair_c
                if n % 4 == 3:
                    row = k * span + (n - 3) * fold
                    products[row : row + 2 * SUBS, 0:LANES] = jnp.concatenate(
                        [half_b, pair_b], axis=0
                    ).astype(jnp.bfloat16)
                    products[row : row + 2 * SUBS, LANES : 2 * LANES] = jnp.concatenate(
                        [half_c, pair_c], axis=0
                    ).astype(jnp.bfloat16)
                pend_b, pend_c = prod_b_n, prod_c_n
            put_tile(pull_s, t, pull[0] + pull[1])
            put_tile(ddelta_s, t, back[0] + back[1])

    groups = length // (2 * STEPS)

    def behind(i, carry):
        flow, g_amat = list(carry[0]), list(carry[1])
        t1 = length - (2 * i + 1) * STEPS
        channel_sums(prod_b, t1 + STEPS)
        behind_steps(t1, prod_a, flow, g_amat)
        channel_sums(prod_a, t1)
        behind_steps(t1 - STEPS, prod_b, flow, g_amat)
        return (tuple(flow), tuple(g_amat))

    unused, g_amat = lax.fori_loop(0, groups, behind, ((zero,) * DSTATE, (zero,) * DSTATE))
    channel_sums(prod_b, 0)
    for n in range(DSTATE):
        gamat_s[n * SUBS : (n + 1) * SUBS, :] = g_amat[n]
    for j in range(SUBS):
        cols = slice(j * LANES, (j + 1) * LANES)
        of_rates = gamat_s[pl.ds(j, DSTATE, stride=SUBS), :]
        gamat_ref[:, cols] = of_rates * -jnp.exp(vec_ref[0:DSTATE, cols])

    line = lax.broadcasted_iota(jnp.int32, (2 * LANES, LANES), 0)
    column = lax.broadcasted_iota(jnp.int32, (2 * LANES, LANES), 1)
    first = line < LANES
    total = jnp.zeros((length, LANES), jnp.float32)
    for n in range(DSTATE):
        goes = jnp.where(first, DTRANK + n, DTRANK + DSTATE + n) == column
        at = (pl.ds(n, length, stride=DSTATE), slice(None))
        both = jnp.concatenate([sums_b[at], sums_c[at]], axis=1).astype(jnp.bfloat16)
        total = total + jnp.dot(
            both, goes.astype(jnp.bfloat16), preferred_element_type=jnp.float32
        )

    @pl.when(half == 0)
    def _():
        dbc_ref[...] = total

    @pl.when(half > 0)
    def _():
        dbc_ref[...] += total

    gsum_ref[...] = jnp.zeros_like(gsum_ref)

    def finish(i, carry):
        r = pl.multiple_of(i * rows, rows)
        for j in range(SUBS):
            at = (pl.ds(r, rows), lane_tile(j))
            of = (pl.ds(r * SUBS + j, rows, stride=SUBS), slice(None))
            skip = vec_ref[SKIP : SKIP + 1, j * LANES : (j + 1) * LANES]
            u = u_ref[at].astype(jnp.float32)
            gate = gate_ref[at]
            sig = jax.nn.sigmoid(gate)
            act = gate * sig
            dg = dg_s[at]
            y = y_s[of] + skip * u
            gated_s[at] = (y * act).astype(jnp.bfloat16)
            dgate_ref[at] = (dg * y * sig * (1.0 + gate * (1.0 - sig))).astype(jnp.bfloat16)
            dstate = dg * act
            pull = pull_s[of]
            du_ref[at] = dstate * skip + pull * delta_s[at]
            ddt = (ddelta_s[of] * LN2 + pull * u) * jax.nn.sigmoid(pre_s[at])
            ddt_ref[at] = ddt.astype(jnp.bfloat16)
            cols = slice(j * LANES, (j + 1) * LANES)
            g_skip = dstate * u
            gsum_ref[0:8, cols] += g_skip[0:8] + g_skip[8:16]
            gsum_ref[8:16, cols] += ddt[0:8] + ddt[8:16]
        return carry

    lax.fori_loop(0, length // rows, finish, 0)

    for b in range(0, PASS, BAND):
        strip = slice(b, b + BAND)
        gout_ref[strip, :] = contract(gated_s[:, strip], cot_ref[...], 0, 0).astype(jnp.bfloat16)
    through = jnp.dot(gated_s[...], outw_ref[...], preferred_element_type=jnp.float32)

    @pl.when(half == 0)
    def _():
        block_ref[...] = tokens_ref[...].astype(jnp.float32) + through

    @pl.when(half > 0)
    def _():
        block_ref[...] += through


def scan_both(proj, masks, dt_rows, u_low, gate_in, tokens, cotangent, out_low, vecs):
    length, inner = u_low.shape
    width = out_low.shape[1]
    by_channel = lambda h: (0, h)
    whole = lambda h: (0, 0)
    rows_of = lambda h: (h, 0)
    f32, b16 = jnp.float32, jnp.bfloat16
    return pl.pallas_call(
        scan_kernel,
        grid=(inner // PASS,),
        in_specs=[
            pl.BlockSpec(memory_space=pltpu.SMEM),
            pl.BlockSpec((length, LANES), whole),
            pl.BlockSpec((length, LANES), whole),
            pl.BlockSpec((PASS, LANES), rows_of),
            pl.BlockSpec((length, PASS), by_channel),
            pl.BlockSpec((length, PASS), by_channel),
            pl.BlockSpec((length, width), whole),
            pl.BlockSpec((length, width), whole),
            pl.BlockSpec((PASS, width), rows_of),
            pl.BlockSpec((VECS, PASS), by_channel),
        ],
        out_specs=[
            pl.BlockSpec((length, PASS), by_channel),
            pl.BlockSpec((length, PASS), by_channel),
            pl.BlockSpec((length, PASS), by_channel),
            pl.BlockSpec((16, PASS), by_channel),
            pl.BlockSpec((DSTATE, PASS), by_channel),
            pl.BlockSpec((length, LANES), whole),
            pl.BlockSpec((PASS, width), rows_of),
            pl.BlockSpec((length, width), whole),
        ],
        out_shape=[
            jax.ShapeDtypeStruct((length, inner), b16),
            jax.ShapeDtypeStruct((length, inner), f32),
            jax.ShapeDtypeStruct((length, inner), b16),
            jax.ShapeDtypeStruct((16, inner), f32),
            jax.ShapeDtypeStruct((DSTATE, inner), f32),
            jax.ShapeDtypeStruct((length, LANES), f32),
            jax.ShapeDtypeStruct((inner, width), b16),
            jax.ShapeDtypeStruct((length, width), f32),
        ],
        scratch_shapes=[
            pltpu.VMEM((length, PASS), b16),
            pltpu.VMEM((DSTATE * SUBS, LANES), f32),
            pltpu.VMEM((DSTATE * SUBS, LANES), f32),
        ]
        + [pltpu.VMEM((length, PASS), f32)] * 3
        + [pltpu.VMEM((length * SUBS, LANES), f32)] * 6
        + [
            pltpu.VMEM(((length + 1) * DSTATE, SUBS, LANES), f32),
            pltpu.VMEM((STEPS * DSTATE * SUBS // 2, 2 * LANES), b16),
            pltpu.VMEM((STEPS * DSTATE * SUBS // 2, 2 * LANES), b16),
            pltpu.VMEM(((length + STEPS) * DSTATE, LANES), f32),
            pltpu.VMEM(((length + STEPS) * DSTATE, LANES), f32),
        ],
        compiler_params=pltpu.CompilerParams(vmem_limit_bytes=60 * 1024 * 1024),
        cost_estimate=pl.CostEstimate(
            flops=24 * length * inner * DSTATE,
            bytes_accessed=24 * length * inner,
            transcendentals=2 * length * inner * DSTATE,
        ),
    )(proj, proj, masks, dt_rows, u_low, gate_in, tokens, cotangent, out_low, vecs)


def flipped(index, bit):
    return index + bit * (1 - 2 * lax.rem(lax.div(index, bit), 2))


ROUTES = 3


def each_mask(first, last, body):
    count = abs(last - first)
    sign = 1 if last > first else -1
    if count <= 4:
        for k in range(count):
            body(first + sign * k)
        return

    def step(k, carry):
        body(first + sign * k)
        return carry

    lax.fori_loop(0, count, step, 0)


def routes_of(width, share=4):
    tiles = width // LANES
    last = tiles // share
    counts = ((tiles - last + 1) // 2, (tiles - last) // 2, last)
    firsts = (0, counts[0], counts[0] + counts[1])
    return [(g, firsts[g] * LANES, counts[g] * LANES) for g in range(ROUTES) if counts[g]]


class Cube:
    def __init__(self, fsdp, ns):
        self.fsdp, self.ns = fsdp, ns
        self.shards, self.pieces, self.masks = fsdp * ns, fsdp * ns // 2, fsdp // 2
        order = [2 << k for k in range(fsdp.bit_length() - 2)]
        self.orders = (order, order[:-2] + [order[-1], order[-2]], order)
        self.places = len(order)
        self.row, self.col = lax.axis_index("fsdp"), lax.axis_index("ns")
        self.me = self.row * ns + self.col
        self.sibling = (flipped(self.row, 1), self.col)
        self.sibling_step = (flipped(self.row, 1) - self.row) * ns
        self.core = lax.rem(self.row, 2)
        self.above, self.below = (self.row, self.col + 1), (self.row, self.col - 1)
        self.has_above, self.has_below = self.col < ns - 1, self.col > 0
        self.half_row = lax.div(self.row, 2)
        moves = {bit: flipped(self.row, bit) - self.row for bit in order}
        halves = {bit: flipped(self.half_row, bit // 2) - self.half_row for bit in order}
        self.steps = [[moves[bit] for bit in bits] for bits in self.orders]
        self.half_steps = [[halves[bit] for bit in bits] for bits in self.orders]

    def partner(self, route, place):
        return (self.row + self.steps[route][place], self.col)

    def flips(self, mask, steps, start):
        for place, step in enumerate(steps):
            if isinstance(mask, int):
                start = start + step if mask >> place & 1 else start
            else:
                start = start + lax.rem(lax.div(mask, 1 << place), 2) * step
        return start

    def at(self, mask, col, route):
        return self.flips(mask, self.steps[route], self.row) * self.ns + col

    def spot(self, mask, col, route):
        return self.flips(mask, self.half_steps[route], self.half_row) * self.ns + col

    def wrapped(self, distance):
        col = self.col + distance
        return jnp.where(col < self.ns, col, col - self.ns)

    def greet(self, others=()):
        barrier = pltpu.get_barrier_semaphore()

        def signal(device):
            pl.semaphore_signal(barrier, inc=1, device_id=device, device_id_type=MESH)

        for place in range(self.places):
            signal(self.partner(0, place))
        signal(self.sibling)
        for other in others:
            signal(other)
        pl.when(self.has_above)(lambda: signal(self.above))
        pl.when(self.has_below)(lambda: signal(self.below))
        ends = jnp.where(self.has_above, 1, 0) + jnp.where(self.has_below, 1, 0)
        pl.semaphore_wait(barrier, self.places + 1 + len(others) + ends)

    def along_line(self, distance, step_to):
        pl.when(self.col - distance >= 0)(lambda: step_to(self.col - distance, "above"))
        pl.when(self.col + distance < self.ns)(lambda: step_to(self.col + distance, "below"))

    def upward(self, step, after=None, own=True, between=lambda: None, third=True):
        after = after or (lambda place, k: None)
        nothing, every, both = 0, range(self.places), ("above", "below")
        if own:
            step((0, 1, 2), nothing, self.col, both, every, True)
            after(-1, nothing)

        def along(d, carry):
            self.along_line(
                d, lambda col, way: step((0, 1), nothing, col, (way,), every, False)
            )
            after(-1, d)
            return carry

        lax.fori_loop(1, self.ns, along, 0)
        for place in every if third else ():
            later = range(place + 1, self.places)
            each_mask(
                1 << place,
                2 << place,
                lambda mask: step((2,), mask, self.col, both, later, False),
            )
        done = 1
        for place in every:
            between()
            later = range(place + 1, self.places)

            def of_mask(mask):
                def across(k, carry):
                    step((0, 1), mask, self.wrapped(k), (), later, False)
                    after(place, mask * self.ns + k)
                    return carry

                lax.fori_loop(0, self.ns, across, 0)

            each_mask(1 << place, 2 << place, of_mask)
            until = self.ns if place == self.places - 1 else min(done + 1, self.ns)
            if not third:
                continue

            def last(distance, carry):
                def of_mask(mask):
                    self.along_line(
                        distance, lambda col, way: step((2,), mask, col, (way,), (), False)
                    )

                each_mask(0, self.masks, of_mask)
                return carry

            lax.fori_loop(done, until, last, 0)
            done = until

    def down_stage(self, stage, step, after=None, third=True):
        after = after or (lambda place, k: None)
        nothing, every, both = 0, range(self.places), ("below", "above")
        source = {"above": ("below",), "below": ("above",)}
        if stage > self.places:
            step((0, 1, 2), nothing, self.col, None, both, every)
            return
        if stage == self.places:

            def along(k, carry):
                self.along_line(
                    self.ns - 1 - k,
                    lambda col, way: step((0, 1), nothing, col, other(way), source[other(way)], every),
                )
                after(-1, k)
                return carry

            lax.fori_loop(0, self.ns - 1, along, 0)
            for place in reversed(every if third else ()):
                later = range(place + 1, self.places)
                each_mask(
                    (2 << place) - 1,
                    (1 << place) - 1,
                    lambda mask: step((2,), mask, self.col, place, both, later),
                )
            return
        place = self.places - 1 - stage
        later = range(place + 1, self.places)

        def of_mask(mask):
            def across(i, carry):
                far = jnp.where(2 * self.col < self.ns, self.ns - 1 - i, 1 + i)
                far = jnp.where(far == self.ns, 0, far)
                step((0, 1), mask, self.wrapped(far), place, (), later)
                after(place, ((2 << place) - 1 - mask) * self.ns + i)
                return carry

            lax.fori_loop(0, self.ns, across, 0)

        each_mask((2 << place) - 1, (1 << place) - 1, of_mask)
        first = self.ns - 1 if stage == 0 else 1
        last = 2 if stage == 0 and self.places > 1 else 1

        def line_first(k, carry):
            def of_mask(mask):
                self.along_line(
                    first - k,
                    lambda col, way: step((2,), mask, col, other(way), source[other(way)], ()),
                )

            each_mask(self.masks - 1, -1, of_mask)
            return carry

        if stage < 2 and third:
            lax.fori_loop(0, first - last + 1, line_first, 0)

    def downward(self, step):
        for stage in range(self.places + 2):
            self.down_stage(stage, step)


def other(way):
    return "below" if way == "above" else "above"


def send(src, dst, send_sem, recv_sem, device):
    pltpu.make_async_remote_copy(
        src_ref=src,
        dst_ref=dst,
        send_sem=send_sem,
        recv_sem=recv_sem,
        device_id=device,
        device_id_type=MESH,
    ).start()


def await_bytes(ref, sem):
    pltpu.make_async_copy(ref, ref, sem).wait()


def pass_on(cube, route, mask, col, ways, places, source, target, send_sem, sem_of):
    if "above" in ways:
        pl.when(cube.has_above)(
            lambda: send(source, target, send_sem.at[1], sem_of(mask, col), cube.above)
        )
    if "below" in ways:
        pl.when(cube.has_below)(
            lambda: send(source, target, send_sem.at[2], sem_of(mask, col), cube.below)
        )
    for p in places:
        partner = cube.partner(route, p)
        send(source, target, send_sem.at[0], sem_of(mask + (1 << p), col), partner)


def await_passed(cube, route, ref, send_sem):
    many = cube.masks if route == 2 else 1
    crossed = cube.masks - 1 if route == 2 else cube.pieces - cube.ns
    await_bytes(ref.at[pl.ds(0, crossed)], send_sem.at[0])
    for col in range(cube.ns):

        @pl.when(cube.col == col)
        def _():
            if col + 1 < cube.ns:
                await_bytes(ref.at[pl.ds(0, many * (col + 1))], send_sem.at[1])
            if col:
                await_bytes(ref.at[pl.ds(0, many * (cube.ns - col))], send_sem.at[2])


def gather_step(cube, ins, outs, sems):
    send_sem, recv_sem, pair_send, pair_sem = sems

    def step(routes, mask, col, ways, places, own):
        for a, (mine, out) in enumerate(zip(ins, outs)):
            for route, first, count in routes_of(mine.shape[1]):
                if route not in routes:
                    continue
                cols = pl.ds(first, count)
                block = out.at[cube.at(mask, col, route), :, cols]

                def sem_of(mask, col):
                    return recv_sem.at[a, route, mask, col]

                if not own:
                    await_bytes(block, sem_of(mask, col))
                source = mine.at[:, cols] if own else block
                pass_on(
                    cube, route, mask, col, ways, places, source, block, send_sem.at[a, route], sem_of
                )
                send(source, block, pair_send.at[a], pair_sem.at[a], cube.sibling)

    return step


def own_step(cube, step):
    step((0, 1, 2), 0, cube.col, ("above", "below"), range(cube.places), True)


def front_kernel(
    fsdp,
    ns,
    per_device,
    gains,
    lengths_ref,
    tokens_ref,
    in_ref,
    out_ref,
    x_own,
    dt_own,
    vectors_own,
    gain_own,
    all_in,
    all_out,
    x_rows,
    dt_rows,
    vec_ref,
    gain_ref,
    xpart_far,
    gate_far,
    upre_far,
    u_far,
    proj_ref,
    masks_ref,
    hidden_ref,
    inverse_ref,
    xpart_ref,
    gate_ref,
    upre_ref,
    u_ref,
    away_sem,
    normed_s,
    in_all,
    small_all,
    in_low,
    out_low,
    small_ref,
    small_s,
    x_s,
    dt_s,
    mask_s,
    own_sem,
    send_sem,
    recv_sem,
    pair_send,
    pair_sem,
    send_out,
    recv_out,
    give_out,
    pair_out,
):
    cube = Cube(fsdp, ns)
    length, width = tokens_ref.shape
    in_low[...] = in_ref[...].astype(jnp.bfloat16)
    out_low[...] = out_ref[...].astype(jnp.bfloat16)
    small_s[...] = jnp.zeros_like(small_s)
    small_s[0:per_device, 0 : x_own.shape[1]] = x_own[...]
    small_s[0:per_device, LANES : LANES + dt_own.shape[1]] = dt_own[...]
    small_s[0:DSTATE, VEC_AT : VEC_AT + per_device] = vectors_own[KCONV + 3 :, :]
    small_s[DSTATE:GAIN, VEC_AT : VEC_AT + per_device] = vectors_own[0 : KCONV + 3, :]
    small_s[GAIN:VECS, VEC_AT : VEC_AT + gains] = gain_own[...]
    small_ref[...] = small_s[...].astype(jnp.bfloat16)
    cube.greet()
    first = gather_step(
        cube, (in_low, small_ref), (in_all, small_all), (send_sem, recv_sem, pair_send, pair_sem)
    )
    later = gather_step(cube, (out_low,), (all_out,), (send_out, recv_out, give_out, pair_out))
    own_step(cube, first)
    in_all[cube.me] = in_low[...]
    small_all[cube.me] = small_ref[...]
    own = pltpu.make_async_copy(out_low, all_out.at[cube.me], own_sem.at[0])
    own.start()

    place = lax.broadcasted_iota(jnp.int32, (length, LANES), 0)
    lane = lax.broadcasted_iota(jnp.int32, (length, LANES), 1)
    masks = jnp.ones((length, LANES), jnp.float32)
    for k in range(1, KCONV):
        same = place >= k
        start = jnp.int32(0)
        for d in range(lengths_ref.shape[1]):
            inside = jnp.logical_and(place >= start, place - k < start)
            same = jnp.logical_and(same, jnp.logical_not(inside))
            start = start + lengths_ref[0, d]
        mask_s[k - 1] = jnp.where(same, 1.0, 0.0)
        masks = jnp.where(lane == k, mask_s[k - 1], masks)
    masks_ref[...] = masks

    stage = [0]

    def between():
        stage[0] += 1
        if stage[0] == cube.places:
            own_step(cube, later)

    tokens = tokens_ref[...].astype(jnp.float32)
    inverse = lax.rsqrt(jnp.mean(tokens * tokens, axis=-1, keepdims=True) + NORM_EPS)
    normed_s[...] = tokens * inverse
    inverse_ref[...] = jnp.broadcast_to(inverse, inverse_ref.shape)
    cube.upward(first, own=False, between=between)
    for a, out in enumerate((in_all, small_all)):
        await_bytes(out.at[pl.ds(0, cube.pieces)], pair_sem.at[a])
    keep_in = pltpu.make_async_copy(in_all, all_in, own_sem.at[1])
    keep_in.start()

    def unpack(d, carry):
        at = pl.ds(pl.multiple_of(d * per_device, per_device), per_device)
        x_s[at, :] = small_all[d, 0:per_device, 0:LANES].astype(jnp.float32)
        both = small_all[d, 0:per_device, LANES : 2 * LANES].astype(jnp.float32)
        own_lanes = lax.broadcasted_iota(jnp.int32, both.shape, 1) < DTRANK
        dt_s[at, :] = jnp.where(own_lanes, both, 0.0)
        return carry

    lax.fori_loop(0, cube.shards, unpack, 0)
    x_rows[...] = x_s[...].astype(jnp.bfloat16)
    dt_rows[...] = dt_s[...].astype(jnp.bfloat16)
    for d in range(cube.shards):
        block = small_all[d, 0:32, LANES : 2 * LANES].astype(jnp.float32)[:, DTRANK:]
        vec_ref[:, d * per_device : (d + 1) * per_device] = block[0:VECS, 0:per_device]
        gain_ref[:, d * gains : (d + 1) * gains] = block[GAIN : GAIN + 1, 0:gains]

    hidden_ref[...] = (normed_s[...] * gain_ref[...]).astype(jnp.bfloat16)
    span = 2 * x_s.shape[0] // CHUNKS
    group = cube.shards // CHUNKS

    def mixed_of(chunk, many):
        weights = in_all[pl.ds(chunk * group, many * group)].reshape(many * span, width)
        return contract(hidden_ref[...], weights, 1, 1)

    def x_block(i, carry):
        cols = pl.ds(pl.multiple_of(2 * i * span, 2 * span), 2 * span)
        xpart_ref[:, cols] = mixed_of(2 * i, 2)
        return carry

    lax.fori_loop(0, CHUNKS // 4, x_block, 0)

    def x_chunk(chunk):
        base = pl.multiple_of(chunk * span, span)
        for j in range(span // LANES):
            cols = pl.ds(pl.multiple_of(base + j * LANES, LANES), LANES)
            x = xpart_ref[:, cols]
            upre = vec_ref[CBIAS : CBIAS + 1, cols] + vec_ref[TAPS : TAPS + 1, cols] * x
            for k in range(1, KCONV):
                moved = pltpu.roll(x, k, 0) * mask_s[k - 1]
                upre = upre + vec_ref[TAPS + k : TAPS + k + 1, cols] * moved
            upre_ref[:, cols] = upre
            u_ref[:, cols] = (upre * jax.nn.sigmoid(upre)).astype(jnp.bfloat16)

    def gate_chunk(chunk):
        base = pl.multiple_of((chunk - CHUNKS // 2) * span, span)
        gate_ref[:, pl.ds(base, span)] = mixed_of(chunk, 1)

    away = [
        pltpu.make_async_copy(source, target, away_sem.at[k])
        for k, (source, target) in enumerate(
            ((xpart_ref, xpart_far), (upre_ref, upre_far), (u_ref, u_far), (gate_ref, gate_far))
        )
    ]
    away[0].start()
    seen = [0]

    def halfway():
        seen[0] += 1
        if seen[0] == cube.places:
            away[1].start()
            away[2].start()

    every = cube.pieces // CHUNKS

    def work(place, k):
        run = gate_chunk if place == cube.places - 1 else x_chunk
        if every == 1:
            run(k)
        else:

            @pl.when(lax.rem(k, every) == 0)
            def _():
                run(lax.div(k, every))

    work(-1, jnp.int32(0))
    cube.upward(later, work, own=False, between=halfway)
    away[3].start()
    proj_ref[...] = jnp.dot(u_ref[...], x_rows[...], preferred_element_type=jnp.float32)
    own.wait()
    keep_in.wait()
    for copy in away:
        copy.wait()
    await_bytes(all_out.at[pl.ds(0, cube.pieces)], pair_out.at[0])
    sent = [
        (in_all, send_sem.at[0], pair_send.at[0]),
        (small_all, send_sem.at[1], pair_send.at[1]),
        (all_out, send_out.at[0], give_out.at[0]),
    ]
    for ref, sems, pair in sent:
        await_bytes(ref.at[pl.ds(0, cube.pieces)], pair)
        for route, start, count in routes_of(ref.shape[2]):
            await_passed(cube, route, ref.at[:, :, pl.ds(start, count)], sems.at[route])


def small_rows(per_device):
    return -(-max(per_device, VECS) // 16) * 16


def gather_and_front(lengths, tokens, params, fsdp, ns):
    shards = fsdp * ns
    length, width = tokens.shape
    in_proj, out_proj, x_own, unused, unused, gain = params
    per_device, gains = x_own.shape[0], gain.shape[1]
    inner = per_device * shards
    small = (small_rows(per_device), SMALL_COLUMNS)
    f32, b16 = jnp.float32, jnp.bfloat16
    held = pl.BlockSpec(memory_space=pltpu.VMEM)
    far = pl.BlockSpec(memory_space=pl.ANY)

    def shape(*dims, dtype=f32):
        return jax.ShapeDtypeStruct(dims, dtype)

    return pl.pallas_call(
        functools.partial(front_kernel, fsdp, ns, per_device, gains),
        in_specs=[pl.BlockSpec(memory_space=pltpu.SMEM)] + [held] * 7,
        out_specs=[far] * 2 + [held] * 4 + [far] * 4 + [held] * 4,
        out_shape=[
            shape(shards, *in_proj.shape, dtype=b16),
            shape(shards, *out_proj.shape, dtype=b16),
            shape(inner, LANES, dtype=b16),
            shape(inner, LANES, dtype=b16),
            shape(VECS, inner),
            shape(1, width),
            shape(length, inner),
            shape(length, inner),
            shape(length, inner),
            shape(length, inner, dtype=b16),
            shape(length, LANES),
            shape(length, LANES),
            shape(length, width, dtype=b16),
            shape(length, LANES),
        ],
        scratch_shapes=[
            pltpu.VMEM((length, inner), f32),
            pltpu.VMEM((length, inner), f32),
            pltpu.VMEM((length, inner), f32),
            pltpu.VMEM((length, inner), b16),
            pltpu.SemaphoreType.DMA((4,)),
            pltpu.VMEM((length, width), f32),
            pltpu.VMEM((shards,) + in_proj.shape, b16),
            pltpu.VMEM((shards,) + small, b16),
            pltpu.VMEM(in_proj.shape, b16),
            pltpu.VMEM(out_proj.shape, b16),
            pltpu.VMEM(small, b16),
            pltpu.VMEM(small, f32),
            pltpu.VMEM((inner, LANES), f32),
            pltpu.VMEM((inner, LANES), f32),
            pltpu.VMEM((KCONV - 1, length, LANES), f32),
            pltpu.SemaphoreType.DMA((2,)),
            pltpu.SemaphoreType.DMA((2, ROUTES, 3)),
            pltpu.SemaphoreType.DMA((2, ROUTES, fsdp // 2, ns)),
            pltpu.SemaphoreType.DMA((2,)),
            pltpu.SemaphoreType.DMA((2,)),
            pltpu.SemaphoreType.DMA((1, ROUTES, 3)),
            pltpu.SemaphoreType.DMA((1, ROUTES, fsdp // 2, ns)),
            pltpu.SemaphoreType.DMA((1,)),
            pltpu.SemaphoreType.DMA((1,)),
        ],
        compiler_params=pltpu.CompilerParams(
            collective_id=0, has_side_effects=True, vmem_limit_bytes=56 * 1024 * 1024
        ),
    )(lengths, tokens, *params)


def slots_of(cube, route):
    if route == 2:

        def over(mask, col):
            if isinstance(mask, int):
                return (2 * cube.masks + mask // cube.ns, mask % cube.ns)
            return (2 * cube.masks + lax.div(mask, cube.ns), lax.rem(mask, cube.ns))

        below = lambda mask, col: (mask, col)
        above = lambda mask, col: (cube.masks + mask, col)
        return (below, above, over, cube.masks)
    return (
        lambda mask, col: (0, col),
        lambda mask, col: (1, col),
        lambda mask, col: (mask + 1, col),
        1,
    )


def slot_count(fsdp, ns, route):
    masks = fsdp // 2
    return 2 * masks + -(-masks // ns) if route == 2 else masks + 1


def clear_ends(cube, route, land):
    many = slots_of(cube, route)[3]

    def clear(first):
        ref = land.at[pl.ds(first, many)]
        ref[...] = jnp.zeros_like(ref)

    pl.when(jnp.logical_not(cube.has_below))(lambda: clear(0))
    pl.when(jnp.logical_not(cube.has_above))(lambda: clear(many))


def arrivals(cube, route, mask, col, lines, places, wait):
    below, above, over, unused = slots_of(cube, route)
    slots = [over(mask + (1 << p), col) for p in places]
    for slot in slots:
        wait(slot)
    if "below" in lines:
        pl.when(cube.has_below)(lambda: wait(below(mask, col)))
        slots.append(below(mask, col))
    if "above" in lines:
        pl.when(cube.has_above)(lambda: wait(above(mask, col)))
        slots.append(above(mask, col))
    return slots


def hand_on(cube, route, mask, col, to, give):
    below, above, over, unused = slots_of(cube, route)
    if to == "above":
        give(below(mask, col), cube.above)
    elif to == "below":
        give(above(mask, col), cube.below)
    elif to is not None:
        give(over(mask, col), cube.partner(route, to))


def scatter_steps(cube, parts, sums, pairs, lands, sems):
    send_sem, recv_sem, pair_sem = sems

    def pieces(routes):
        for a, part in enumerate(parts):
            for k, (route, first, count) in enumerate(routes_of(part.shape[2])):
                if route in routes:
                    yield (a, route, pl.ds(first, count), pairs[a][k], lands[a][k])

    def give_pair(routes, mask, col, to, lines, places):
        for a, route, cols, pair, unused in pieces(routes):
            index = cube.at(mask, col, route) + cube.sibling_step
            send(
                parts[a].at[index, :, cols],
                pair.at[mask, col],
                send_sem.at[a],
                pair_sem.at[a, route, mask, col],
                cube.sibling,
            )

    def step(routes, mask, col, to, lines, places):
        for a, route, cols, pair, land in pieces(routes):
            index = cube.at(mask, col, route)
            rows = parts[a].shape[1]
            await_bytes(pair.at[mask, col], pair_sem.at[a, route, mask, col])

            def wait(slot):
                await_bytes(land.at[slot], recv_sem.at[(a, route) + slot])

            slots = arrivals(cube, route, mask, col, lines, places, wait)
            deep = min(rows, 16)
            for r in range(0, rows, deep):
                at = pl.ds(r, deep)
                total = parts[a][index, at, cols].astype(jnp.float32)
                total = total + pair[mask, col, at, :].astype(jnp.float32)
                for slot in slots:
                    total = total + land[slot + (at, slice(None))].astype(jnp.float32)
                if to is not None:
                    pair[mask, col, at, :] = total.astype(jnp.bfloat16)
                else:
                    sums[a][at, cols] = total

            def give(slot, device):
                send(
                    pair.at[mask, col],
                    land.at[slot],
                    send_sem.at[a],
                    recv_sem.at[(a, route) + slot],
                    device,
                )

            hand_on(cube, route, mask, col, to, give)

    return (give_pair, step)


def back_kernel(
    fsdp,
    ns,
    per_device,
    far,
    inverse_ref,
    masks_ref,
    proj_ref,
    x_rows,
    dt_rows,
    vec_ref,
    gain_ref,
    gsum_ref,
    gamat_ref,
    dbc_ref,
    all_in,
    dtok_ref,
    ggain_ref,
    sum_in,
    sum_out,
    sum_small,
    sum_vec,
    near,
    near_sem,
    part_in,
    part_small,
    small_s,
    pair_in,
    pair_out,
    pair_small,
    land_in,
    land_out,
    land_small,
    dx_s,
    dhidden_s,
    weights,
    mask_s,
    dproj_s,
    dtin_s,
    du_s,
    gx_s,
    gdt_s,
    last_s,
    load_sem,
    send_first,
    recv_first,
    pair_first,
    send_sem,
    recv_sem,
    pair_sem,
):
    copies = [
        pltpu.make_async_copy(source, target, near_sem.at[k])
        for k, (source, target) in enumerate(zip(far, near))
    ]
    for copy in copies:
        copy.start()
    (
        gout_ref,
        dgate_ref,
        hidden_ref,
        ddt_ref,
        du_ref,
        u_ref,
        upre_ref,
        xpart_ref,
        tokens_ref,
        cot_ref,
    ) = near
    cube = Cube(fsdp, ns)
    length, width = tokens_ref.shape
    inner = x_rows.shape[0]
    cube.greet()
    give_out, step_out = scatter_steps(
        cube, (gout_ref,), (sum_out,), (pair_out,), (land_out,), (send_first, recv_first, pair_first)
    )
    give_in, step_in = scatter_steps(
        cube,
        (part_in, part_small),
        (sum_in, sum_small),
        (pair_in, pair_small),
        (land_in, land_small),
        (send_sem, recv_sem, pair_sem),
    )
    copies[0].wait()
    cube.downward(give_out)
    for part, land in ((gout_ref, land_out), (part_in, land_in), (part_small, land_small)):
        for (route, unused, unused), where in zip(routes_of(part.shape[2]), land):
            clear_ends(cube, route, where)

    group = BAND // part_in.shape[1]

    def into_part(first, source):
        def band(i, carry):
            cols = pl.ds(pl.multiple_of(i * BAND, BAND), BAND)
            gradient = contract(source[:, cols], hidden_ref[...], 0, 0).astype(jnp.bfloat16)
            at = pl.ds(first + i * group, group)
            part_in[at] = gradient.reshape(group, part_in.shape[1], width)
            return carry

        lax.fori_loop(0, inner // BAND, band, 0)

    for copy in copies[1:3]:
        copy.wait()
    into_part(cube.shards // 2, dgate_ref)
    for k in range(1, KCONV):
        mask_s[k - 1] = jnp.broadcast_to(masks_ref[:, k : k + 1], (length, LANES))
    for copy in copies[3:]:
        copy.wait()
    d_dtin = jnp.dot(ddt_ref[...], dt_rows[...], preferred_element_type=jnp.float32)
    dproj_s[...] = (d_dtin + dbc_ref[...]).astype(jnp.bfloat16)
    lane = lax.broadcasted_iota(jnp.int32, (length, LANES), 1)
    dtin_s[...] = jnp.where(lane < DTRANK, proj_ref[...], 0.0).astype(jnp.bfloat16)
    sub = lax.broadcasted_iota(jnp.int32, (SUBS, LANES), 0)

    def state_band(i, carry):
        at = pl.ds(pl.multiple_of(i * BAND, BAND), BAND)
        du_s[:, at] = du_ref[:, at] + contract(dproj_s[...], x_rows[at, :], 1, 1)
        gx_s[at, :] = contract(u_ref[:, at], dproj_s[...], 0, 0)
        gdt_s[at, :] = contract(ddt_ref[:, at], dtin_s[...], 0, 0)
        return carry

    lax.fori_loop(0, inner // BAND, state_band, 0)

    def x_chunk(chunk):
        cols = pl.ds(pl.multiple_of(chunk * LANES, LANES), LANES)
        x, upre = xpart_ref[:, cols], upre_ref[:, cols]
        sig = jax.nn.sigmoid(upre)
        dpre = du_s[:, cols] * sig * (1.0 + upre * (1.0 - sig))
        dx = vec_ref[TAPS : TAPS + 1, cols] * dpre
        sums = [jnp.sum(dpre * x, axis=0, keepdims=True)]
        for k in range(1, KCONV):
            masked = mask_s[k - 1] * dpre
            dx = dx + vec_ref[TAPS + k : TAPS + k + 1, cols] * pltpu.roll(masked, length - k, 0)
            sums.append(jnp.sum(masked * pltpu.roll(x, k, 0), axis=0, keepdims=True))
        sums.append(jnp.sum(dpre, axis=0, keepdims=True))
        sums.append(jnp.sum(gsum_ref[SUBS : 2 * SUBS, cols], axis=0, keepdims=True))
        sums.append(jnp.sum(gsum_ref[0:SUBS, cols], axis=0, keepdims=True))
        last = jnp.zeros((SUBS, LANES), jnp.float32)
        for k, value in enumerate(sums):
            last = jnp.where(sub == k, value, last)
        last_s[:, cols] = last
        dx_s[:, cols] = dx.astype(jnp.bfloat16)

    steps = ns << (cube.places - 1)
    many = max(CHUNKS // steps, 1)
    every = max(steps // CHUNKS, 1)

    def x_chunks(place, k):
        def run():
            for i in range(many):
                x_chunk((k if every == 1 else lax.div(k, every)) * many + i)

        if every == 1:
            run()
        else:
            pl.when(lax.rem(k, every) == 0)(run)

    cube.down_stage(0, step_out, x_chunks)
    into_part(0, dx_s)

    small_s[...] = jnp.zeros_like(small_s)
    owners = LANES // per_device

    def small_chunk(chunk, carry):
        cols = pl.ds(pl.multiple_of(chunk * LANES, LANES), LANES)
        shape = (owners, per_device, LANES)
        small_s[:, 0:per_device, 0:LANES] = gx_s[cols, :].reshape(shape)
        small_s[:, 0:per_device, LANES:VEC_AT] = gdt_s[cols, :].reshape(shape)[:, :, 0:DTRANK]
        rates, last = gamat_ref[:, cols], last_s[:, cols]
        for o in range(owners):
            mine = slice(o * per_device, (o + 1) * per_device)
            small_s[o, 0:DSTATE, VEC_AT : VEC_AT + per_device] = rates[:, mine]
            small_s[o, DSTATE:VECS, VEC_AT : VEC_AT + per_device] = last[:, mine]
        part_small[pl.ds(chunk * owners, owners)] = small_s[...].astype(jnp.bfloat16)
        return carry

    lax.fori_loop(0, inner // LANES, small_chunk, 0)
    cube.downward(give_in)

    share = cube.shards // CHUNKS
    span = 2 * inner // CHUNKS

    def load(chunk):
        slot = lax.rem(chunk, 2)
        return pltpu.make_async_copy(
            all_in.at[pl.ds(chunk * share, share)], weights.at[slot], load_sem.at[slot]
        )

    dhidden_s[...] = jnp.zeros_like(dhidden_s)
    load(jnp.int32(0)).start()

    def hidden_chunk(chunk, left, base):
        load(chunk).wait()
        pl.when(chunk + 1 < CHUNKS)(lambda: load(chunk + 1).start())
        cols = pl.ds(pl.multiple_of((chunk - base) * span, span), span)
        right = weights[lax.rem(chunk, 2)].reshape(span, width)
        dhidden_s[...] += jnp.dot(left[:, cols], right, preferred_element_type=jnp.float32)

    def tokens_rows(i, total):
        at = pl.ds(pl.multiple_of(i * 16, 16), 16)
        inverse = inverse_ref[at, 0:1]
        normed = tokens_ref[at, :].astype(jnp.float32) * inverse
        dhidden = dhidden_s[at, :]
        product = dhidden * normed
        scaled = dhidden * gain_ref[...]
        mean = jnp.mean(scaled * normed, axis=-1, keepdims=True)
        dtok_ref[at, :] = cot_ref[at, :].astype(jnp.float32) + inverse * (scaled - normed * mean)
        return total + product[0:8] + product[8:16]

    part = CHUNKS // 2

    def hidden_chunks(first, last, left, base):
        def body(chunk, carry):
            hidden_chunk(chunk, left, base)
            return carry

        lax.fori_loop(first, last, body, 0)

    for stage in range(cube.places + 2):
        if stage < cube.places + 1:
            cube.down_stage(stage + 1, step_out)
        cube.down_stage(stage, step_in)
        if stage == 0:
            hidden_chunks(0, part, dx_s, 0)
        if stage == 1:
            hidden_chunks(part, CHUNKS, dgate_ref, part)
        if stage == cube.places:
            zero = jnp.zeros((SUBS, width), jnp.float32)
            total = lax.fori_loop(0, length // 16, tokens_rows, zero)
            row = jnp.sum(total, axis=0, keepdims=True)
            ggain_ref[...] = jnp.zeros_like(ggain_ref)
            for k in range(width // LANES):
                ggain_ref[k : k + 1, :] = row[:, k * LANES : (k + 1) * LANES]
    vectors = sum_small[0:VECS, VEC_AT : VEC_AT + per_device]
    sum_vec[0 : KCONV + 3, :] = vectors[DSTATE:GAIN, :]
    sum_vec[KCONV + 3 :, :] = vectors[0:DSTATE, :]
    await_bytes(gout_ref.at[pl.ds(0, cube.shards - 1)], send_first.at[0])
    await_bytes(part_in.at[pl.ds(0, cube.shards - 1)], send_sem.at[0])
    await_bytes(part_small.at[pl.ds(0, cube.shards - 1)], send_sem.at[1])


def back_and_scatter(far, arrays, all_in, per_device, small, fsdp, ns):
    length, width = arrays[0].shape[0], all_in.shape[2]
    inner = per_device * fsdp * ns
    shards, masks = fsdp * ns, fsdp // 2
    f32, b16 = jnp.float32, jnp.bfloat16
    blocks = [(2 * per_device, width), (per_device, width), (small, SMALL_COLUMNS)]

    def inbox(slots):
        return [
            [
                pltpu.VMEM((slots(route), ns, rows, count), b16)
                for route, unused, count in routes_of(columns)
            ]
            for rows, columns in blocks
        ]

    most = slot_count(fsdp, ns, 2)
    return pl.pallas_call(
        functools.partial(back_kernel, fsdp, ns, per_device),
        in_specs=[
            [pl.BlockSpec(memory_space=pl.ANY)] * len(far),
            *[pl.BlockSpec(memory_space=pltpu.VMEM)] * len(arrays),
            pl.BlockSpec(memory_space=pl.ANY),
        ],
        out_specs=[pl.BlockSpec(memory_space=pltpu.VMEM)] * 6,
        out_shape=[
            jax.ShapeDtypeStruct((length, width), f32),
            jax.ShapeDtypeStruct((-(-width // LANES // 16) * 16, LANES), f32),
        ]
        + [jax.ShapeDtypeStruct(block, f32) for block in blocks]
        + [jax.ShapeDtypeStruct((GAIN, per_device), f32)],
        scratch_shapes=[
            [pltpu.VMEM(array.shape, array.dtype) for array in far],
            pltpu.SemaphoreType.DMA((len(far),)),
            pltpu.VMEM((shards,) + blocks[0], b16),
            pltpu.VMEM((shards,) + blocks[2], b16),
            pltpu.VMEM((LANES // per_device,) + blocks[2], f32),
        ]
        + inbox(lambda route: masks)
        + inbox(functools.partial(slot_count, fsdp, ns))
        + [
            pltpu.VMEM((length, inner), b16),
            pltpu.VMEM((length, width), f32),
            pltpu.VMEM((2, shards // CHUNKS) + blocks[0], b16),
            pltpu.VMEM((KCONV - 1, length, LANES), f32),
            pltpu.VMEM((length, LANES), b16),
            pltpu.VMEM((length, LANES), b16),
            pltpu.VMEM((length, inner), f32),
            pltpu.VMEM((inner, LANES), f32),
            pltpu.VMEM((inner, LANES), f32),
            pltpu.VMEM((SUBS, inner), f32),
            pltpu.SemaphoreType.DMA((2,)),
            pltpu.SemaphoreType.DMA((1,)),
            pltpu.SemaphoreType.DMA((1, ROUTES, most, ns)),
            pltpu.SemaphoreType.DMA((1, ROUTES, masks, ns)),
            pltpu.SemaphoreType.DMA((2,)),
            pltpu.SemaphoreType.DMA((2, ROUTES, most, ns)),
            pltpu.SemaphoreType.DMA((2, ROUTES, masks, ns)),
        ],
        compiler_params=pltpu.CompilerParams(
            collective_id=1, has_side_effects=True, vmem_limit_bytes=60 * 1024 * 1024
        ),
    )(far, *arrays, all_in)


def halves_of(deep, wide):
    if deep >= 32:
        return [(g, (g * (deep // 2), deep // 2), (0, wide)) for g in range(2)]
    return [(g, (0, deep), (first, count)) for g, first, count in routes_of(wide, wide)]


def muon_kernel(
    fsdp,
    ns,
    starts,
    sum_in,
    sum_out,
    in_moment,
    out_moment,
    low_ref,
    gain_ref,
    x_out,
    low_out,
    gain_out,
    rows_s,
    turn,
    back_s,
    mine,
    outbox,
    lands,
    pieces_s,
    gram,
    now,
    poly,
    small_now,
    small_land,
    small_gram,
    low_s,
    send_sem,
    gather_sem,
    recv_sem,
    came_sem,
    swap_sem,
    small_send,
    small_recv,
):
    cube = Cube(fsdp, ns)
    pieces, deep, wide = pieces_s.shape
    width = now.shape[0]
    rows = sum_in.shape[0]
    blocks = width // LANES
    each = LANES // deep
    split = halves_of(deep, wide)
    ways = [cube.sibling] + [cube.partner(0, place) for place in range(cube.places)]
    ways += [(cube.row, flipped(cube.col, 1 << k)) for k in range(ns.bit_length() - 1)]
    stages = len(ways)
    cube.greet(ways[cube.places + 2 :])

    short = sum_out.shape[0]
    rows_s[0] = (MOMENTUM * in_moment[...] + sum_in[...]).astype(jnp.bfloat16)
    rows_s[1, 0:short, :] = (MOMENTUM * out_moment[...] + sum_out[...]).astype(jnp.bfloat16)
    rows_s[1, short:, :] = jnp.zeros((rows - short, width), jnp.bfloat16)

    def swap(source, target, which):
        return pltpu.make_async_remote_copy(
            src_ref=source,
            dst_ref=target,
            send_sem=swap_sem.at[which, 0],
            recv_sem=swap_sem.at[which, 1],
            device_id=cube.sibling,
            device_id_type=MESH,
        )

    there = swap(rows_s.at[1 - cube.core], turn.at[pl.ds(rows, rows)], 0)
    there.start()
    turn[0:rows] = rows_s[cube.core]

    def small_copy(k):
        return pltpu.make_async_remote_copy(
            src_ref=small_now.at[k],
            dst_ref=small_land.at[k],
            send_sem=small_send.at[k],
            recv_sem=small_recv.at[k],
            device_id=ways[k],
            device_id_type=MESH,
        )

    def inverse(total):
        return 1.0 / (jnp.sqrt(jnp.full((1, 1), total, jnp.float32)) + FROB_EPS)

    def diagonal(block):
        on = lax.broadcasted_iota(jnp.int32, block.shape, 0) == lax.broadcasted_iota(
            jnp.int32, block.shape, 1
        )
        return jnp.sum(jnp.where(on, block, 0.0))

    def small_step(k):
        small_copy(k).wait()
        total = small_now[k].astype(jnp.float32) + small_land[k].astype(jnp.float32)
        if k + 1 < stages:
            small_now[k + 1] = total.astype(jnp.bfloat16)
            small_copy(k + 1).start()
            return
        gain_out[...] = total[starts[2] :]
        for which in range(2):
            deep = starts[which + 1] - starts[which]
            whole = jnp.pad(total[starts[which] : starts[which + 1]], ((0, LANES - deep), (0, 0)))
            scale = inverse(diagonal(whole))
            small_gram[which] = whole * (scale * scale)
            low_s[which] = (low_ref[which] * scale).astype(jnp.bfloat16)

    for which in range(2):
        low = low_ref[which].astype(jnp.bfloat16)
        term = contract(low, low, 0, 0)[0 : starts[which + 1] - starts[which]]
        small_now[0, starts[which] : starts[which + 1], :] = term.astype(jnp.bfloat16)
    small_now[0, starts[2] :, :] = gain_ref[...].astype(jnp.bfloat16)
    small_copy(0).start()
    left = list(range(stages))

    def between():
        if left:
            small_step(left.pop(0))

    for (route, unused, unused), land in zip(split, lands):
        clear_ends(cube, route, land)

    there.wait()
    for b in range(blocks):
        if b % 2 == 0:
            band = contract(turn[:, b * LANES : (b + 2) * LANES], turn[...], 0, 0)
        block = band[b % 2 * LANES : (b % 2 + 1) * LANES]
        for c in range(wide // LANES):
            at = (b + c) % blocks * LANES
            for r in range(each):
                strip = block[r * deep : (r + 1) * deep, at : at + LANES]
                mine[b * each + r, :, c * LANES : (c + 1) * LANES] = strip

    def step(routes, mask, col, to, lines, places):
        for (route, rows_at, cols_at), land in zip(split, lands):
            if route not in routes:
                continue
            at = (cube.spot(mask, col, route), pl.ds(*rows_at), pl.ds(*cols_at))

            def wait(slot):
                await_bytes(land.at[slot], recv_sem.at[(route,) + slot])

            total = mine[at]
            for slot in arrivals(cube, route, mask, col, lines, places, wait):
                total = total + land[slot].astype(jnp.float32)
            if to is not None:
                outbox[at] = total.astype(jnp.bfloat16)
            else:
                pieces_s[at] = total.astype(jnp.bfloat16)

            def give(slot, device):
                send(
                    outbox.at[at],
                    land.at[slot],
                    send_sem,
                    recv_sem.at[(route,) + slot],
                    device,
                )

            hand_on(cube, route, mask, col, to, give)

    for stage in range(cube.places + 2):
        cube.down_stage(stage, step, third=False)
        if stage <= cube.places:
            between()

    def spread(routes, mask, col, ways, places, own):
        for route, rows_at, cols_at in split:
            if route not in routes:
                continue
            block = pieces_s.at[cube.spot(mask, col, route), pl.ds(*rows_at), pl.ds(*cols_at)]

            def sem_of(mask, col):
                return came_sem.at[route, mask, col]

            if not own:
                await_bytes(block, sem_of(mask, col))
            sems = gather_sem.at[route]
            pass_on(cube, route, mask, col, ways, places, block, block, sems, sem_of)

    def small_newton():
        for which in range(2):
            whole = small_gram[which]
            low = whole.astype(jnp.bfloat16)
            power = jnp.dot(low, low, preferred_element_type=jnp.float32)
            mixed = (COEF_B * whole + COEF_C * power).astype(jnp.bfloat16)
            block = low_s[which]
            low_s[which] = (
                COEF_A * block.astype(jnp.float32)
                + jnp.dot(block, mixed, preferred_element_type=jnp.float32)
            ).astype(jnp.bfloat16)
            half = COEF_A * whole + jnp.dot(low, mixed, preferred_element_type=jnp.float32)
            small_gram[which] = COEF_A * half + jnp.dot(
                half.astype(jnp.bfloat16), mixed, preferred_element_type=jnp.float32
            )

    def after(place, k):
        if place == cube.places - 1:
            pl.when(k - (ns << place) < NS_STEPS)(small_newton)

    cube.upward(spread, after=after, between=between, third=False)
    low_out[...] = low_s[...]

    for b in range(blocks):
        for c in range(wide // LANES):
            at = (b + c) % blocks * LANES
            for r in range(each):
                now[b * LANES + r * deep : b * LANES + (r + 1) * deep, at : at + LANES] = pieces_s[
                    b * each + r, :, c * LANES : (c + 1) * LANES
                ]
    for b in range(blocks):
        for c in range(wide // LANES, blocks):
            other = (b + c) % blocks
            block = now[other * LANES : (other + 1) * LANES, b * LANES : (b + 1) * LANES]
            flip = block.astype(jnp.float32).T.astype(jnp.bfloat16)
            now[b * LANES : (b + 1) * LANES, other * LANES : (other + 1) * LANES] = flip

    total = jnp.zeros((), jnp.float32)
    for b in range(0, width, LANES):
        total = total + diagonal(now[b : b + LANES, b : b + LANES].astype(jnp.float32))
    factor = inverse(total)
    square = factor * factor
    strip = min(BAND, width)

    def turned(block, k):
        moved = COEF_A * block.astype(jnp.float32) + jnp.dot(
            block, poly[...], preferred_element_type=jnp.float32
        )
        if k == 0:
            moved = moved * factor
        return moved.astype(jnp.bfloat16)

    for k in range(NS_STEPS):

        def poly_strip(i, carry, k=k):
            at = pl.ds(pl.multiple_of(i * strip, strip), strip)
            low = now[at, :]
            power = jnp.dot(low, now[...], preferred_element_type=jnp.float32)
            if k == 0:
                mixed = COEF_B * square * low.astype(jnp.float32) + (COEF_C * square * square) * power
            else:
                mixed = COEF_B * gram[at, :] + COEF_C * power
            poly[at, :] = mixed.astype(jnp.bfloat16)
            return carry

        lax.fori_loop(0, width // strip, poly_strip, 0)
        if k + 1 == NS_STEPS:
            break
        turn[...] = turned(turn[...], k)

        def gram_strip(i, carry, k=k):
            at = pl.ds(pl.multiple_of(i * strip, strip), strip)
            low = now[at, :]
            full = low.astype(jnp.float32) if k == 0 else gram[at, :]
            half = COEF_A * full + jnp.dot(low, poly[...], preferred_element_type=jnp.float32)
            if k == 0:
                half = half * square
            renewed = COEF_A * half + jnp.dot(
                half.astype(jnp.bfloat16), poly[...], preferred_element_type=jnp.float32
            )
            gram[at, :] = renewed
            now[at, :] = renewed.astype(jnp.bfloat16)
            return carry

        lax.fori_loop(0, width // strip, gram_strip, 0)
    turn[rows:] = turned(turn[rows:], NS_STEPS - 1)
    home = swap(turn.at[pl.ds(rows, rows)], back_s, 1)
    home.start()
    x_out[cube.core] = turned(turn[0:rows], NS_STEPS - 1)
    home.wait()
    x_out[1 - cube.core] = back_s[...]
    await_bytes(outbox.at[pl.ds(0, pieces - 1)], send_sem)
    for route, rows_at, cols_at in split:
        sent = pieces_s.at[:, pl.ds(*rows_at), pl.ds(*cols_at)]
        await_passed(cube, route, sent, gather_sem.at[route])


def muon_rows(sum_in, sum_out, in_moment, out_moment, low, columns, gain, fsdp, ns):
    pieces = fsdp * ns // 2
    rows, width = sum_in.shape
    wide = (width // LANES // 2 + 1) * LANES
    deep = width // pieces
    block = (pieces, deep, wide)
    stages = (fsdp * ns).bit_length() - 1
    starts = (0, columns[0], sum(columns))
    small = (sum(columns) + gain.shape[0], LANES)
    f32, b16 = jnp.float32, jnp.bfloat16
    landing = [
        pltpu.VMEM((slot_count(fsdp, ns, route), ns, rows_at[1], cols_at[1]), b16)
        for route, rows_at, cols_at in halves_of(deep, wide)
    ]
    held = pl.BlockSpec(memory_space=pltpu.VMEM)
    return pl.pallas_call(
        functools.partial(muon_kernel, fsdp, ns, starts),
        in_specs=[held] * 6,
        out_specs=[held] * 3,
        out_shape=[
            jax.ShapeDtypeStruct((2, rows, width), b16),
            jax.ShapeDtypeStruct(low.shape, b16),
            jax.ShapeDtypeStruct(gain.shape, f32),
        ],
        scratch_shapes=[
            pltpu.VMEM((2, rows, width), b16),
            pltpu.VMEM((2 * rows, width), b16),
            pltpu.VMEM((rows, width), b16),
            pltpu.VMEM(block, f32),
            pltpu.VMEM(block, b16),
        ]
        + [
            landing,
            pltpu.VMEM(block, b16),
            pltpu.VMEM((width, width), f32),
            pltpu.VMEM((width, width), b16),
            pltpu.VMEM((width, width), b16),
            pltpu.VMEM((stages,) + small, b16),
            pltpu.VMEM((stages,) + small, b16),
            pltpu.VMEM((2, LANES, LANES), f32),
            pltpu.VMEM(low.shape, b16),
            pltpu.SemaphoreType.DMA,
            pltpu.SemaphoreType.DMA((ROUTES, 3)),
            pltpu.SemaphoreType.DMA((ROUTES, slot_count(fsdp, ns, 2), ns)),
            pltpu.SemaphoreType.DMA((ROUTES, fsdp // 2, ns)),
            pltpu.SemaphoreType.DMA((2, 2)),
            pltpu.SemaphoreType.DMA((stages,)),
            pltpu.SemaphoreType.DMA((stages,)),
        ],
        compiler_params=pltpu.CompilerParams(
            collective_id=2, has_side_effects=True, vmem_limit_bytes=48 * 1024 * 1024
        ),
    )(sum_in, sum_out, in_moment, out_moment, low, gain)


def layer(tokens, out_grad, lengths, params, fsdp, ns):
    flat_low, grad_flat = tokens[0], out_grad[0]
    length, width = flat_low.shape
    (
        all_in,
        all_out,
        x_rows,
        dt_rows,
        vecs,
        gain,
        x_part,
        gate_in,
        conv_flat,
        u_low,
        proj,
        masks,
        hidden,
        inverse,
    ) = gather_and_front(lengths, flat_low, params, fsdp, ns)
    per_device = params[2].shape[0]
    inner = x_rows.shape[0]
    out_low = all_out.reshape(inner, width)
    d_gate, d_u, d_dtlow, vec_parts, grad_amat, d_bc, grad_out, block_out = scan_both(
        proj, masks, dt_rows, u_low, gate_in, flat_low, grad_flat, out_low, vecs
    )
    d_tokens, grad_gain, sum_in, sum_out, sum_small, sum_vec = back_and_scatter(
        [
            grad_out.reshape(fsdp * ns, per_device, width),
            d_gate,
            hidden,
            d_dtlow,
            d_u,
            u_low,
            conv_flat,
            x_part,
            flat_low,
            grad_flat,
        ],
        (inverse, masks, proj, x_rows, dt_rows, vecs, gain, vec_parts, grad_amat, d_bc),
        all_in,
        per_device,
        small_rows(per_device),
        fsdp,
        ns,
    )
    return (block_out[None], d_tokens[None], grad_gain, sum_in, sum_out, sum_small, sum_vec)


def adamw_update(param, first, second, grad):
    first_new = FIRST_MOMENT_BETA * first + (1.0 - FIRST_MOMENT_BETA) * grad
    second_new = BETA_SECOND * second + (1.0 - BETA_SECOND) * grad * grad
    first_hat = first_new / (1.0 - FIRST_MOMENT_BETA**STEP_NO)
    second_hat = second_new / (1.0 - BETA_SECOND**STEP_NO)
    param_new = param * (1.0 - ADAM_RATE * ADAM_DECAY) - ADAM_RATE * first_hat / (
        jnp.sqrt(second_hat) + ADAM_EPS
    )
    return (param_new, first_new, second_new)


def on_device(
    tokens,
    out_grad,
    doc_lengths,
    in_proj,
    inner_projection_weight,
    dt_proj,
    out_proj,
    in_moment,
    x_moment,
    dt_moment,
    out_moment,
    vectors,
    vector_first,
    vector_second,
    norm_gain,
    gain_first,
    gain_second,
):
    fsdp, ns = lax.axis_size("fsdp"), lax.axis_size("ns")
    shards = fsdp * ns
    per_device, columns = inner_projection_weight.shape
    rank, gains = dt_proj.shape[1], norm_gain.shape[0]
    block_out, grad_tokens, grad_gain, sum_in, sum_out, sum_small, sum_vec = layer(
        tokens,
        out_grad,
        doc_lengths,
        (
            in_proj,
            out_proj,
            inner_projection_weight,
            dt_proj,
            vectors,
            norm_gain[None],
        ),
        fsdp,
        ns,
    )
    sum_x = sum_small[:per_device, :columns]
    sum_dt = sum_small[:per_device, LANES : LANES + rank]
    summed = (sum_in, sum_x, sum_dt, sum_out, sum_vec)
    old_moments = (in_moment, x_moment, dt_moment, out_moment)
    moments = tuple((MOMENTUM * moment + grad for moment, grad in zip(old_moments, summed[:4])))
    gap = -per_device % 16
    low = jnp.stack(
        [
            jnp.pad(moments[1], ((0, gap), (0, LANES - columns))),
            jnp.pad(moments[2], ((0, gap), (0, LANES - rank))),
        ]
    )
    big, low, sum_gain = muon_rows(
        sum_in, sum_out, in_moment, out_moment, low, (columns, rank), grad_gain, fsdp, ns
    )
    place = lax.axis_index("fsdp") * ns + lax.axis_index("ns")
    sum_gain = lax.dynamic_slice_in_dim(sum_gain.reshape(-1), place * gains, gains, 0)
    own_blocks = (
        big[0],
        low[0, :per_device, :columns],
        low[1, :per_device, :rank],
        big[1, :per_device],
    )
    weights = (in_proj, inner_projection_weight, dt_proj, out_proj)
    fans = (DMODEL, DINNER, DTRANK, DINNER // 8)
    results = []
    for weight, moment, block, fan in zip(weights, moments, own_blocks, fans):
        rate = 0.5 * math.sqrt(weight.shape[0] * shards / fan)
        results.append((1.0 - SHRINK) * weight - rate * block.astype(jnp.float32))
        results.append(moment)
    vec_new, vec_first, vec_second = adamw_update(vectors, vector_first, vector_second, summed[4])
    gain_new, gain_m, gain_v = adamw_update(norm_gain, gain_first, gain_second, sum_gain)
    return (
        block_out,
        grad_tokens,
        results[0],
        results[1],
        results[2],
        results[3],
        results[4],
        results[5],
        results[6],
        results[7],
        vec_new,
        vec_first,
        vec_second,
        gain_new,
        gain_m,
        gain_v,
    )


def solution(mesh):
    placed = (
        P(("fsdp", "ns"), None, None),
        P(("fsdp", "ns"), None, None),
        P(("fsdp", "ns"), None),
        P(("fsdp", "ns"), None),
        P(("fsdp", "ns"), None),
        P(("fsdp", "ns"), None),
        P(("fsdp", "ns"), None),
        P(("fsdp", "ns"), None),
        P(("fsdp", "ns"), None),
        P(("fsdp", "ns"), None),
        P(("fsdp", "ns"), None),
        P(None, ("fsdp", "ns")),
        P(None, ("fsdp", "ns")),
        P(None, ("fsdp", "ns")),
        P(("fsdp", "ns")),
        P(("fsdp", "ns")),
        P(("fsdp", "ns")),
    )
    return jax.shard_map(
        on_device,
        mesh=mesh,
        in_specs=placed,
        out_specs=(
            P(("fsdp", "ns"), None, None),
            P(("fsdp", "ns"), None, None),
            P(("fsdp", "ns"), None),
            P(("fsdp", "ns"), None),
            P(("fsdp", "ns"), None),
            P(("fsdp", "ns"), None),
            P(("fsdp", "ns"), None),
            P(("fsdp", "ns"), None),
            P(("fsdp", "ns"), None),
            P(("fsdp", "ns"), None),
            P(None, ("fsdp", "ns")),
            P(None, ("fsdp", "ns")),
            P(None, ("fsdp", "ns")),
            P(("fsdp", "ns")),
            P(("fsdp", "ns")),
            P(("fsdp", "ns")),
        ),
        check_vma=False,
    )
```

```python
import functools
import math

import jax
import jax.numpy as jnp
from jax import lax
from jax.experimental import pallas as pl
from jax.experimental.pallas import tpu as pltpu
from jax.sharding import PartitionSpec as P

DMODEL = 1024
DINNER = 2048
DSTATE = 16
DTRANK = 64
KCONV = 4
NS_STEPS = 4
STEP_NO = 10


NORM_EPS = 1e-05
FROB_EPS = 1e-07
COEF_A = 3.4445
COEF_B = -4.775
COEF_C = 2.0315
MOMENTUM = 0.95
SHRINK = 0.001
FIRST_MOMENT_BETA = 0.9
BETA_SECOND = 0.95
ADAM_EPS = 1e-08
ADAM_RATE = 1.0
ADAM_DECAY = 0.001


def contract(left, right, left_dim, right_dim):
    return lax.dot_general(
        left, right, (((left_dim,), (right_dim,)), ((), ())), preferred_element_type=jnp.float32
    )


MESH = pl.DeviceIdType.MESH
LANES = 128
SUBS = 8
PASS = LANES * SUBS
STEPS = 4
RESET = 1.0e4
LOG2E = math.log2(math.e)
LN2 = math.log(2.0)
TAPS = DSTATE
CBIAS = TAPS + KCONV
DTBIAS = CBIAS + 1
SKIP = CBIAS + 2
GAIN = CBIAS + 3
VECS = CBIAS + 4
CHUNKS = 16
BAND = 512
SMALL_COLUMNS = 2 * LANES
VEC_AT = LANES + DTRANK


def lane_tile(j):
    return pl.ds(j * LANES, LANES)


def scan_kernel(
    bc_ref,
    proj_ref,
    masks_ref,
    dtw_ref,
    u_ref,
    gate_ref,
    tokens_ref,
    cot_ref,
    outw_ref,
    vec_ref,
    dgate_ref,
    du_ref,
    ddt_ref,
    gsum_ref,
    gamat_ref,
    dbc_ref,
    gout_ref,
    block_ref,
    gated_s,
    amat_s,
    gamat_s,
    pre_s,
    dg_s,
    delta_s,
    sig_s,
    dec_s,
    drive_s,
    dstate_s,
    y_s,
    pull_s,
    ddelta_s,
    states,
    prod_a,
    prod_b,
    sums_b,
    sums_c,
):
    length = u_ref.shape[0]
    half = pl.program_id(0)
    bias_row = vec_ref[DTBIAS : DTBIAS + 1, :]

    pre_s[...] = contract(proj_ref[...].astype(jnp.bfloat16), dtw_ref[...], 1, 1) + bias_row
    dg_s[...] = contract(cot_ref[...], outw_ref[...], 1, 1)

    for j in range(SUBS):
        rates = -LOG2E * jnp.exp(vec_ref[0:DSTATE, j * LANES : (j + 1) * LANES])
        amat_s[pl.ds(j, DSTATE, stride=SUBS), :] = rates

    def amat_of(n):
        return amat_s[n * SUBS : (n + 1) * SUBS, :]

    rows = 16

    def prepare(i, carry):
        r = pl.multiple_of(i * rows, rows)
        keep = masks_ref[pl.ds(r, rows), 1:2] > 0.0
        for j in range(SUBS):
            at = (pl.ds(r, rows), lane_tile(j))
            pre = pre_s[at]
            z = jnp.exp(-jnp.abs(pre))
            tail = jnp.where(z < 2.0**-10, z * (1.0 - 0.5 * z), jnp.log(1.0 + z))
            delta = jnp.maximum(pre, 0.0) + tail
            u = u_ref[at].astype(jnp.float32)
            gate = gate_ref[at]
            delta_s[at] = delta
            to = (pl.ds(r * SUBS + j, rows, stride=SUBS), slice(None))
            dec_s[to] = jnp.where(keep, delta, RESET)
            drive_s[to] = delta * u
            sig = jax.nn.sigmoid(gate)
            sig_s[at] = sig
            dstate_s[to] = dg_s[at] * (gate * sig)
        return carry

    lax.fori_loop(0, length // rows, prepare, 0)

    for n in range(DSTATE):
        states[n] = jnp.zeros((SUBS, LANES), jnp.float32)

    def tile_of(ref, t):
        return ref[pl.ds(pl.multiple_of(t * SUBS, SUBS), SUBS), :]

    def put_tile(ref, t, value):
        ref[pl.ds(pl.multiple_of(t * SUBS, SUBS), SUBS), :] = value

    def ahead(i, carry):
        state = list(carry)
        for k in range(STEPS):
            t = i * STEPS + k
            dec, drive = tile_of(dec_s, t), tile_of(drive_s, t)
            parts = [None, None]
            for n in range(DSTATE):
                s = jnp.exp2(dec * amat_of(n)) * state[n] + drive * bc_ref[t, DTRANK + n]
                state[n] = s
                states[(t + 1) * DSTATE + n] = s
                term = s * bc_ref[t, DTRANK + DSTATE + n]
                parts[n % 2] = term if parts[n % 2] is None else parts[n % 2] + term
            put_tile(y_s, t, parts[0] + parts[1])
        return tuple(state)

    zero = jnp.zeros((SUBS, LANES), jnp.float32)
    lax.fori_loop(0, length // STEPS, ahead, (zero,) * DSTATE)

    pick = (
        lax.broadcasted_iota(jnp.int32, (2 * DSTATE, 2 * LANES), 1) // SUBS
        == lax.broadcasted_iota(jnp.int32, (2 * DSTATE, 2 * LANES), 0)
    ).astype(jnp.bfloat16)
    span = DSTATE * SUBS

    def channel_sums(products, t0):
        for k in range(0, STEPS, 2):
            block = products[k * span : (k + 2) * span, :]
            row = pl.multiple_of((t0 + k) * DSTATE, 2 * DSTATE)
            both = jnp.dot(pick, block, preferred_element_type=jnp.float32)
            sums_b[pl.ds(row, 2 * DSTATE), :] = both[:, 0:LANES]
            sums_c[pl.ds(row, 2 * DSTATE), :] = both[:, LANES : 2 * LANES]

    def behind_steps(t0, products, flow, g_amat):
        for k in reversed(range(STEPS)):
            t = t0 + k
            dec, drive, dstate = tile_of(dec_s, t), tile_of(drive_s, t), tile_of(dstate_s, t)
            pull, back = [None, None], [None, None]
            pend_b, pend_c = None, None
            for n in range(DSTATE):
                amat = amat_of(n)
                adj = dstate * bc_ref[t, DTRANK + DSTATE + n] + flow[n]
                term = adj * bc_ref[t, DTRANK + n]
                pull[n % 2] = term if pull[n % 2] is None else pull[n % 2] + term
                flow[n] = jnp.exp2(dec * amat) * adj
                weighted = flow[n] * states[t * DSTATE + n]
                g_amat[n] = g_amat[n] + weighted * dec
                term = weighted * amat
                back[n % 2] = term if back[n % 2] is None else back[n % 2] + term
                prod_b_n = adj * drive
                prod_c_n = states[(t + 1) * DSTATE + n] * dstate
                if n % 2:
                    row = k * span + (n - 1) * SUBS
                    products[row : row + 2 * SUBS, 0:LANES] = jnp.concatenate(
                        [pend_b, prod_b_n], axis=0
                    ).astype(jnp.bfloat16)
                    products[row : row + 2 * SUBS, LANES : 2 * LANES] = jnp.concatenate(
                        [pend_c, prod_c_n], axis=0
                    ).astype(jnp.bfloat16)
                pend_b, pend_c = prod_b_n, prod_c_n
            put_tile(pull_s, t, pull[0] + pull[1])
            put_tile(ddelta_s, t, back[0] + back[1])

    groups = length // (2 * STEPS)

    def behind(i, carry):
        flow, g_amat = list(carry[0]), list(carry[1])
        t1 = length - (2 * i + 1) * STEPS
        channel_sums(prod_b, t1 + STEPS)
        behind_steps(t1, prod_a, flow, g_amat)
        channel_sums(prod_a, t1)
        behind_steps(t1 - STEPS, prod_b, flow, g_amat)
        return (tuple(flow), tuple(g_amat))

    unused, g_amat = lax.fori_loop(0, groups, behind, ((zero,) * DSTATE, (zero,) * DSTATE))
    channel_sums(prod_b, 0)
    for n in range(DSTATE):
        gamat_s[n * SUBS : (n + 1) * SUBS, :] = g_amat[n]
    for j in range(SUBS):
        cols = slice(j * LANES, (j + 1) * LANES)
        of_rates = gamat_s[pl.ds(j, DSTATE, stride=SUBS), :]
        gamat_ref[:, cols] = of_rates * -jnp.exp(vec_ref[0:DSTATE, cols])

    line = lax.broadcasted_iota(jnp.int32, (2 * LANES, LANES), 0)
    column = lax.broadcasted_iota(jnp.int32, (2 * LANES, LANES), 1)
    first = line < LANES
    total = jnp.zeros((length, LANES), jnp.float32)
    for n in range(DSTATE):
        goes = jnp.where(first, DTRANK + n, DTRANK + DSTATE + n) == column
        at = (pl.ds(n, length, stride=DSTATE), slice(None))
        both = jnp.concatenate([sums_b[at], sums_c[at]], axis=1).astype(jnp.bfloat16)
        total = total + jnp.dot(
            both, goes.astype(jnp.bfloat16), preferred_element_type=jnp.float32
        )

    @pl.when(half == 0)
    def _():
        dbc_ref[...] = total

    @pl.when(half > 0)
    def _():
        dbc_ref[...] += total

    gsum_ref[...] = jnp.zeros_like(gsum_ref)

    def finish(i, carry):
        r = pl.multiple_of(i * rows, rows)
        for j in range(SUBS):
            at = (pl.ds(r, rows), lane_tile(j))
            of = (pl.ds(r * SUBS + j, rows, stride=SUBS), slice(None))
            skip = vec_ref[SKIP : SKIP + 1, j * LANES : (j + 1) * LANES]
            u = u_ref[at].astype(jnp.float32)
            gate = gate_ref[at]
            sig = sig_s[at]
            act = gate * sig
            dg = dg_s[at]
            y = y_s[of] + skip * u
            gated_s[at] = (y * act).astype(jnp.bfloat16)
            dgate_ref[at] = (dg * y * sig * (1.0 + gate * (1.0 - sig))).astype(jnp.bfloat16)
            dstate = dg * act
            pull = pull_s[of]
            du_ref[at] = dstate * skip + pull * delta_s[at]
            ddt = (ddelta_s[of] * LN2 + pull * u) * jax.nn.sigmoid(pre_s[at])
            ddt_ref[at] = ddt.astype(jnp.bfloat16)
            cols = slice(j * LANES, (j + 1) * LANES)
            g_skip = dstate * u
            gsum_ref[0:8, cols] += g_skip[0:8] + g_skip[8:16]
            gsum_ref[8:16, cols] += ddt[0:8] + ddt[8:16]
        return carry

    lax.fori_loop(0, length // rows, finish, 0)

    for b in range(0, PASS, BAND):
        strip = slice(b, b + BAND)
        gout_ref[strip, :] = contract(gated_s[:, strip], cot_ref[...], 0, 0).astype(jnp.bfloat16)
    through = jnp.dot(gated_s[...], outw_ref[...], preferred_element_type=jnp.float32)

    @pl.when(half == 0)
    def _():
        block_ref[...] = tokens_ref[...].astype(jnp.float32) + through

    @pl.when(half > 0)
    def _():
        block_ref[...] += through


def scan_both(proj, masks, dt_rows, u_low, gate_in, tokens, cotangent, out_low, vecs):
    length, inner = u_low.shape
    width = out_low.shape[1]
    by_channel = lambda h: (0, h)
    whole = lambda h: (0, 0)
    rows_of = lambda h: (h, 0)
    f32, b16 = jnp.float32, jnp.bfloat16
    return pl.pallas_call(
        scan_kernel,
        grid=(inner // PASS,),
        in_specs=[
            pl.BlockSpec(memory_space=pltpu.SMEM),
            pl.BlockSpec((length, LANES), whole),
            pl.BlockSpec((length, LANES), whole),
            pl.BlockSpec((PASS, LANES), rows_of),
            pl.BlockSpec((length, PASS), by_channel),
            pl.BlockSpec((length, PASS), by_channel),
            pl.BlockSpec((length, width), whole),
            pl.BlockSpec((length, width), whole),
            pl.BlockSpec((PASS, width), rows_of),
            pl.BlockSpec((VECS, PASS), by_channel),
        ],
        out_specs=[
            pl.BlockSpec((length, PASS), by_channel),
            pl.BlockSpec((length, PASS), by_channel),
            pl.BlockSpec((length, PASS), by_channel),
            pl.BlockSpec((16, PASS), by_channel),
            pl.BlockSpec((DSTATE, PASS), by_channel),
            pl.BlockSpec((length, LANES), whole),
            pl.BlockSpec((PASS, width), rows_of),
            pl.BlockSpec((length, width), whole),
        ],
        out_shape=[
            jax.ShapeDtypeStruct((length, inner), b16),
            jax.ShapeDtypeStruct((length, inner), f32),
            jax.ShapeDtypeStruct((length, inner), b16),
            jax.ShapeDtypeStruct((16, inner), f32),
            jax.ShapeDtypeStruct((DSTATE, inner), f32),
            jax.ShapeDtypeStruct((length, LANES), f32),
            jax.ShapeDtypeStruct((inner, width), b16),
            jax.ShapeDtypeStruct((length, width), f32),
        ],
        scratch_shapes=[
            pltpu.VMEM((length, PASS), b16),
            pltpu.VMEM((DSTATE * SUBS, LANES), f32),
            pltpu.VMEM((DSTATE * SUBS, LANES), f32),
        ]
        + [pltpu.VMEM((length, PASS), f32)] * 4
        + [pltpu.VMEM((length * SUBS, LANES), f32)] * 6
        + [
            pltpu.VMEM(((length + 1) * DSTATE, SUBS, LANES), f32),
            pltpu.VMEM((STEPS * DSTATE * SUBS, 2 * LANES), b16),
            pltpu.VMEM((STEPS * DSTATE * SUBS, 2 * LANES), b16),
            pltpu.VMEM(((length + STEPS) * DSTATE, LANES), f32),
            pltpu.VMEM(((length + STEPS) * DSTATE, LANES), f32),
        ],
        compiler_params=pltpu.CompilerParams(vmem_limit_bytes=60 * 1024 * 1024),
        cost_estimate=pl.CostEstimate(
            flops=24 * length * inner * DSTATE,
            bytes_accessed=24 * length * inner,
            transcendentals=2 * length * inner * DSTATE,
        ),
    )(proj, proj, masks, dt_rows, u_low, gate_in, tokens, cotangent, out_low, vecs)


def flipped(index, bit):
    return index + bit * (1 - 2 * lax.rem(lax.div(index, bit), 2))


ROUTES = 3


def each_mask(first, last, body):
    count = abs(last - first)
    sign = 1 if last > first else -1
    if count <= 4:
        for k in range(count):
            body(first + sign * k)
        return

    def step(k, carry):
        body(first + sign * k)
        return carry

    lax.fori_loop(0, count, step, 0)


def routes_of(width, share=4):
    tiles = width // LANES
    last = tiles // share
    counts = ((tiles - last + 1) // 2, (tiles - last) // 2, last)
    firsts = (0, counts[0], counts[0] + counts[1])
    return [(g, firsts[g] * LANES, counts[g] * LANES) for g in range(ROUTES) if counts[g]]


class Cube:
    def __init__(self, fsdp, ns):
        self.fsdp, self.ns = fsdp, ns
        self.shards, self.pieces, self.masks = fsdp * ns, fsdp * ns // 2, fsdp // 2
        order = [2 << k for k in range(fsdp.bit_length() - 2)]
        self.orders = (order, order[:-2] + [order[-1], order[-2]], order)
        self.places = len(order)
        self.row, self.col = lax.axis_index("fsdp"), lax.axis_index("ns")
        self.me = self.row * ns + self.col
        self.sibling = (flipped(self.row, 1), self.col)
        self.sibling_step = (flipped(self.row, 1) - self.row) * ns
        self.core = lax.rem(self.row, 2)
        self.above, self.below = (self.row, self.col + 1), (self.row, self.col - 1)
        self.has_above, self.has_below = self.col < ns - 1, self.col > 0
        self.half_row = lax.div(self.row, 2)
        moves = {bit: flipped(self.row, bit) - self.row for bit in order}
        halves = {bit: flipped(self.half_row, bit // 2) - self.half_row for bit in order}
        self.steps = [[moves[bit] for bit in bits] for bits in self.orders]
        self.half_steps = [[halves[bit] for bit in bits] for bits in self.orders]

    def partner(self, route, place):
        return (self.row + self.steps[route][place], self.col)

    def flips(self, mask, steps, start):
        for place, step in enumerate(steps):
            if isinstance(mask, int):
                start = start + step if mask >> place & 1 else start
            else:
                start = start + lax.rem(lax.div(mask, 1 << place), 2) * step
        return start

    def at(self, mask, col, route):
        return self.flips(mask, self.steps[route], self.row) * self.ns + col

    def spot(self, mask, col, route):
        return self.flips(mask, self.half_steps[route], self.half_row) * self.ns + col

    def wrapped(self, distance):
        col = self.col + distance
        return jnp.where(col < self.ns, col, col - self.ns)

    def greet(self, others=()):
        barrier = pltpu.get_barrier_semaphore()

        def signal(device):
            pl.semaphore_signal(barrier, inc=1, device_id=device, device_id_type=MESH)

        for place in range(self.places):
            signal(self.partner(0, place))
        signal(self.sibling)
        for other in others:
            signal(other)
        pl.when(self.has_above)(lambda: signal(self.above))
        pl.when(self.has_below)(lambda: signal(self.below))
        ends = jnp.where(self.has_above, 1, 0) + jnp.where(self.has_below, 1, 0)
        pl.semaphore_wait(barrier, self.places + 1 + len(others) + ends)

    def along_line(self, distance, step_to):
        pl.when(self.col - distance >= 0)(lambda: step_to(self.col - distance, "above"))
        pl.when(self.col + distance < self.ns)(lambda: step_to(self.col + distance, "below"))

    def upward(self, step, after=None, own=True, between=lambda: None, third=True):
        after = after or (lambda place, k: None)
        nothing, every, both = 0, range(self.places), ("above", "below")
        if own:
            step((0, 1, 2), nothing, self.col, both, every, True)
            after(-1, nothing)

        def along(d, carry):
            self.along_line(
                d, lambda col, way: step((0, 1), nothing, col, (way,), every, False)
            )
            after(-1, d)
            return carry

        lax.fori_loop(1, self.ns, along, 0)
        for place in every if third else ():
            later = range(place + 1, self.places)
            each_mask(
                1 << place,
                2 << place,
                lambda mask: step((2,), mask, self.col, both, later, False),
            )
        done = 1
        for place in every:
            between()
            later = range(place + 1, self.places)

            def of_mask(mask):
                def across(k, carry):
                    step((0, 1), mask, self.wrapped(k), (), later, False)
                    after(place, mask * self.ns + k)
                    return carry

                lax.fori_loop(0, self.ns, across, 0)

            each_mask(1 << place, 2 << place, of_mask)
            until = self.ns if place == self.places - 1 else min(done + 1, self.ns)
            if not third:
                continue

            def last(distance, carry):
                def of_mask(mask):
                    self.along_line(
                        distance, lambda col, way: step((2,), mask, col, (way,), (), False)
                    )

                each_mask(0, self.masks, of_mask)
                return carry

            lax.fori_loop(done, until, last, 0)
            done = until

    def down_stage(self, stage, step, after=None, third=True):
        after = after or (lambda place, k: None)
        nothing, every, both = 0, range(self.places), ("below", "above")
        source = {"above": ("below",), "below": ("above",)}
        if stage > self.places:
            step((0, 1, 2), nothing, self.col, None, both, every)
            return
        if stage == self.places:

            def along(k, carry):
                self.along_line(
                    self.ns - 1 - k,
                    lambda col, way: step((0, 1), nothing, col, other(way), source[other(way)], every),
                )
                after(-1, k)
                return carry

            lax.fori_loop(0, self.ns - 1, along, 0)
            for place in reversed(every if third else ()):
                later = range(place + 1, self.places)
                each_mask(
                    (2 << place) - 1,
                    (1 << place) - 1,
                    lambda mask: step((2,), mask, self.col, place, both, later),
                )
            return
        place = self.places - 1 - stage
        later = range(place + 1, self.places)

        def of_mask(mask):
            def across(i, carry):
                far = jnp.where(2 * self.col < self.ns, self.ns - 1 - i, 1 + i)
                far = jnp.where(far == self.ns, 0, far)
                step((0, 1), mask, self.wrapped(far), place, (), later)
                after(place, ((2 << place) - 1 - mask) * self.ns + i)
                return carry

            lax.fori_loop(0, self.ns, across, 0)

        each_mask((2 << place) - 1, (1 << place) - 1, of_mask)
        first = self.ns - 1 if stage == 0 else 1
        last = 2 if stage == 0 and self.places > 1 else 1

        def line_first(k, carry):
            def of_mask(mask):
                self.along_line(
                    first - k,
                    lambda col, way: step((2,), mask, col, other(way), source[other(way)], ()),
                )

            each_mask(self.masks - 1, -1, of_mask)
            return carry

        if stage < 2 and third:
            lax.fori_loop(0, first - last + 1, line_first, 0)

    def downward(self, step):
        for stage in range(self.places + 2):
            self.down_stage(stage, step)


def other(way):
    return "below" if way == "above" else "above"


def send(src, dst, send_sem, recv_sem, device):
    pltpu.make_async_remote_copy(
        src_ref=src,
        dst_ref=dst,
        send_sem=send_sem,
        recv_sem=recv_sem,
        device_id=device,
        device_id_type=MESH,
    ).start()


def await_bytes(ref, sem):
    pltpu.make_async_copy(ref, ref, sem).wait()


def pass_on(cube, route, mask, col, ways, places, source, target, send_sem, sem_of):
    if "above" in ways:
        pl.when(cube.has_above)(
            lambda: send(source, target, send_sem.at[1], sem_of(mask, col), cube.above)
        )
    if "below" in ways:
        pl.when(cube.has_below)(
            lambda: send(source, target, send_sem.at[2], sem_of(mask, col), cube.below)
        )
    for p in places:
        partner = cube.partner(route, p)
        send(source, target, send_sem.at[0], sem_of(mask + (1 << p), col), partner)


def await_passed(cube, route, ref, send_sem):
    many = cube.masks if route == 2 else 1
    crossed = cube.masks - 1 if route == 2 else cube.pieces - cube.ns
    await_bytes(ref.at[pl.ds(0, crossed)], send_sem.at[0])
    for col in range(cube.ns):

        @pl.when(cube.col == col)
        def _():
            if col + 1 < cube.ns:
                await_bytes(ref.at[pl.ds(0, many * (col + 1))], send_sem.at[1])
            if col:
                await_bytes(ref.at[pl.ds(0, many * (cube.ns - col))], send_sem.at[2])


def gather_step(cube, ins, outs, sems):
    send_sem, recv_sem, pair_send, pair_sem = sems

    def step(routes, mask, col, ways, places, own):
        for a, (mine, out) in enumerate(zip(ins, outs)):
            for route, first, count in routes_of(mine.shape[1]):
                if route not in routes:
                    continue
                cols = pl.ds(first, count)
                block = out.at[cube.at(mask, col, route), :, cols]

                def sem_of(mask, col):
                    return recv_sem.at[a, route, mask, col]

                if not own:
                    await_bytes(block, sem_of(mask, col))
                source = mine.at[:, cols] if own else block
                pass_on(
                    cube, route, mask, col, ways, places, source, block, send_sem.at[a, route], sem_of
                )
                send(source, block, pair_send.at[a], pair_sem.at[a], cube.sibling)

    return step


def own_step(cube, step):
    step((0, 1, 2), 0, cube.col, ("above", "below"), range(cube.places), True)


def front_kernel(
    fsdp,
    ns,
    per_device,
    gains,
    lengths_ref,
    tokens_ref,
    in_ref,
    out_ref,
    x_own,
    dt_own,
    vectors_own,
    gain_own,
    all_in,
    all_out,
    x_rows,
    dt_rows,
    vec_ref,
    gain_ref,
    xpart_far,
    gate_far,
    upre_far,
    u_far,
    proj_ref,
    masks_ref,
    hidden_ref,
    inverse_ref,
    xpart_ref,
    gate_ref,
    upre_ref,
    u_ref,
    away_sem,
    normed_s,
    in_all,
    small_all,
    in_low,
    out_low,
    small_ref,
    small_s,
    x_s,
    dt_s,
    mask_s,
    own_sem,
    send_sem,
    recv_sem,
    pair_send,
    pair_sem,
    send_out,
    recv_out,
    give_out,
    pair_out,
):
    cube = Cube(fsdp, ns)
    length, width = tokens_ref.shape
    in_low[...] = in_ref[...].astype(jnp.bfloat16)
    out_low[...] = out_ref[...].astype(jnp.bfloat16)
    small_s[...] = jnp.zeros_like(small_s)
    small_s[0:per_device, 0 : x_own.shape[1]] = x_own[...]
    small_s[0:per_device, LANES : LANES + dt_own.shape[1]] = dt_own[...]
    small_s[0:DSTATE, VEC_AT : VEC_AT + per_device] = vectors_own[KCONV + 3 :, :]
    small_s[DSTATE:GAIN, VEC_AT : VEC_AT + per_device] = vectors_own[0 : KCONV + 3, :]
    small_s[GAIN:VECS, VEC_AT : VEC_AT + gains] = gain_own[...]
    small_ref[...] = small_s[...].astype(jnp.bfloat16)
    cube.greet()
    first = gather_step(
        cube, (in_low, small_ref), (in_all, small_all), (send_sem, recv_sem, pair_send, pair_sem)
    )
    later = gather_step(cube, (out_low,), (all_out,), (send_out, recv_out, give_out, pair_out))
    own_step(cube, first)
    in_all[cube.me] = in_low[...]
    small_all[cube.me] = small_ref[...]
    own = pltpu.make_async_copy(out_low, all_out.at[cube.me], own_sem.at[0])
    own.start()

    place = lax.broadcasted_iota(jnp.int32, (length, LANES), 0)
    lane = lax.broadcasted_iota(jnp.int32, (length, LANES), 1)
    masks = jnp.ones((length, LANES), jnp.float32)
    for k in range(1, KCONV):
        same = place >= k
        start = jnp.int32(0)
        for d in range(lengths_ref.shape[1]):
            inside = jnp.logical_and(place >= start, place - k < start)
            same = jnp.logical_and(same, jnp.logical_not(inside))
            start = start + lengths_ref[0, d]
        mask_s[k - 1] = jnp.where(same, 1.0, 0.0)
        masks = jnp.where(lane == k, mask_s[k - 1], masks)
    masks_ref[...] = masks

    stage = [0]

    def between():
        stage[0] += 1
        if stage[0] == cube.places:
            own_step(cube, later)

    tokens = tokens_ref[...].astype(jnp.float32)
    inverse = lax.rsqrt(jnp.mean(tokens * tokens, axis=-1, keepdims=True) + NORM_EPS)
    normed_s[...] = tokens * inverse
    inverse_ref[...] = jnp.broadcast_to(inverse, inverse_ref.shape)
    cube.upward(first, own=False, between=between)
    for a, out in enumerate((in_all, small_all)):
        await_bytes(out.at[pl.ds(0, cube.pieces)], pair_sem.at[a])
    keep_in = pltpu.make_async_copy(in_all, all_in, own_sem.at[1])
    keep_in.start()

    def unpack(d, carry):
        at = pl.ds(pl.multiple_of(d * per_device, per_device), per_device)
        x_s[at, :] = small_all[d, 0:per_device, 0:LANES].astype(jnp.float32)
        both = small_all[d, 0:per_device, LANES : 2 * LANES].astype(jnp.float32)
        own_lanes = lax.broadcasted_iota(jnp.int32, both.shape, 1) < DTRANK
        dt_s[at, :] = jnp.where(own_lanes, both, 0.0)
        return carry

    lax.fori_loop(0, cube.shards, unpack, 0)
    x_rows[...] = x_s[...].astype(jnp.bfloat16)
    dt_rows[...] = dt_s[...].astype(jnp.bfloat16)
    for d in range(cube.shards):
        block = small_all[d, 0:32, LANES : 2 * LANES].astype(jnp.float32)[:, DTRANK:]
        vec_ref[:, d * per_device : (d + 1) * per_device] = block[0:VECS, 0:per_device]
        gain_ref[:, d * gains : (d + 1) * gains] = block[GAIN : GAIN + 1, 0:gains]

    hidden_ref[...] = (normed_s[...] * gain_ref[...]).astype(jnp.bfloat16)
    span = 2 * x_s.shape[0] // CHUNKS
    group = cube.shards // CHUNKS

    def mixed_of(chunk, many):
        weights = in_all[pl.ds(chunk * group, many * group)].reshape(many * span, width)
        return contract(hidden_ref[...], weights, 1, 1)

    def x_block(i, carry):
        cols = pl.ds(pl.multiple_of(2 * i * span, 2 * span), 2 * span)
        xpart_ref[:, cols] = mixed_of(2 * i, 2)
        return carry

    lax.fori_loop(0, CHUNKS // 4, x_block, 0)

    def x_chunk(chunk):
        base = pl.multiple_of(chunk * span, span)
        for j in range(span // LANES):
            cols = pl.ds(pl.multiple_of(base + j * LANES, LANES), LANES)
            x = xpart_ref[:, cols]
            upre = vec_ref[CBIAS : CBIAS + 1, cols] + vec_ref[TAPS : TAPS + 1, cols] * x
            for k in range(1, KCONV):
                moved = pltpu.roll(x, k, 0) * mask_s[k - 1]
                upre = upre + vec_ref[TAPS + k : TAPS + k + 1, cols] * moved
            upre_ref[:, cols] = upre
            u_ref[:, cols] = (upre * jax.nn.sigmoid(upre)).astype(jnp.bfloat16)

    def gate_chunk(chunk):
        base = pl.multiple_of((chunk - CHUNKS // 2) * span, span)
        gate_ref[:, pl.ds(base, span)] = mixed_of(chunk, 1)

    away = [
        pltpu.make_async_copy(source, target, away_sem.at[k])
        for k, (source, target) in enumerate(
            ((xpart_ref, xpart_far), (upre_ref, upre_far), (u_ref, u_far), (gate_ref, gate_far))
        )
    ]
    away[0].start()
    seen = [0]

    def halfway():
        seen[0] += 1
        if seen[0] == cube.places:
            away[1].start()
            away[2].start()

    every = cube.pieces // CHUNKS

    def work(place, k):
        run = gate_chunk if place == cube.places - 1 else x_chunk
        if every == 1:
            run(k)
        else:

            @pl.when(lax.rem(k, every) == 0)
            def _():
                run(lax.div(k, every))

    work(-1, jnp.int32(0))
    cube.upward(later, work, own=False, between=halfway)
    away[3].start()
    proj_ref[...] = jnp.dot(u_ref[...], x_rows[...], preferred_element_type=jnp.float32)
    own.wait()
    keep_in.wait()
    for copy in away:
        copy.wait()
    await_bytes(all_out.at[pl.ds(0, cube.pieces)], pair_out.at[0])
    sent = [
        (in_all, send_sem.at[0], pair_send.at[0]),
        (small_all, send_sem.at[1], pair_send.at[1]),
        (all_out, send_out.at[0], give_out.at[0]),
    ]
    for ref, sems, pair in sent:
        await_bytes(ref.at[pl.ds(0, cube.pieces)], pair)
        for route, start, count in routes_of(ref.shape[2]):
            await_passed(cube, route, ref.at[:, :, pl.ds(start, count)], sems.at[route])


def small_rows(per_device):
    return -(-max(per_device, VECS) // 16) * 16


def gather_and_front(lengths, tokens, params, fsdp, ns):
    shards = fsdp * ns
    length, width = tokens.shape
    in_proj, out_proj, x_own, unused, unused, gain = params
    per_device, gains = x_own.shape[0], gain.shape[1]
    inner = per_device * shards
    small = (small_rows(per_device), SMALL_COLUMNS)
    f32, b16 = jnp.float32, jnp.bfloat16
    held = pl.BlockSpec(memory_space=pltpu.VMEM)
    far = pl.BlockSpec(memory_space=pl.ANY)

    def shape(*dims, dtype=f32):
        return jax.ShapeDtypeStruct(dims, dtype)

    return pl.pallas_call(
        functools.partial(front_kernel, fsdp, ns, per_device, gains),
        in_specs=[pl.BlockSpec(memory_space=pltpu.SMEM)] + [held] * 7,
        out_specs=[far] * 2 + [held] * 4 + [far] * 4 + [held] * 4,
        out_shape=[
            shape(shards, *in_proj.shape, dtype=b16),
            shape(shards, *out_proj.shape, dtype=b16),
            shape(inner, LANES, dtype=b16),
            shape(inner, LANES, dtype=b16),
            shape(VECS, inner),
            shape(1, width),
            shape(length, inner),
            shape(length, inner),
            shape(length, inner),
            shape(length, inner, dtype=b16),
            shape(length, LANES),
            shape(length, LANES),
            shape(length, width, dtype=b16),
            shape(length, LANES),
        ],
        scratch_shapes=[
            pltpu.VMEM((length, inner), f32),
            pltpu.VMEM((length, inner), f32),
            pltpu.VMEM((length, inner), f32),
            pltpu.VMEM((length, inner), b16),
            pltpu.SemaphoreType.DMA((4,)),
            pltpu.VMEM((length, width), f32),
            pltpu.VMEM((shards,) + in_proj.shape, b16),
            pltpu.VMEM((shards,) + small, b16),
            pltpu.VMEM(in_proj.shape, b16),
            pltpu.VMEM(out_proj.shape, b16),
            pltpu.VMEM(small, b16),
            pltpu.VMEM(small, f32),
            pltpu.VMEM((inner, LANES), f32),
            pltpu.VMEM((inner, LANES), f32),
            pltpu.VMEM((KCONV - 1, length, LANES), f32),
            pltpu.SemaphoreType.DMA((2,)),
            pltpu.SemaphoreType.DMA((2, ROUTES, 3)),
            pltpu.SemaphoreType.DMA((2, ROUTES, fsdp // 2, ns)),
            pltpu.SemaphoreType.DMA((2,)),
            pltpu.SemaphoreType.DMA((2,)),
            pltpu.SemaphoreType.DMA((1, ROUTES, 3)),
            pltpu.SemaphoreType.DMA((1, ROUTES, fsdp // 2, ns)),
            pltpu.SemaphoreType.DMA((1,)),
            pltpu.SemaphoreType.DMA((1,)),
        ],
        compiler_params=pltpu.CompilerParams(
            collective_id=0, has_side_effects=True, vmem_limit_bytes=56 * 1024 * 1024
        ),
    )(lengths, tokens, *params)


def slots_of(cube, route):
    if route == 2:

        def over(mask, col):
            if isinstance(mask, int):
                return (2 * cube.masks + mask // cube.ns, mask % cube.ns)
            return (2 * cube.masks + lax.div(mask, cube.ns), lax.rem(mask, cube.ns))

        below = lambda mask, col: (mask, col)
        above = lambda mask, col: (cube.masks + mask, col)
        return (below, above, over, cube.masks)
    return (
        lambda mask, col: (0, col),
        lambda mask, col: (1, col),
        lambda mask, col: (mask + 1, col),
        1,
    )


def slot_count(fsdp, ns, route):
    masks = fsdp // 2
    return 2 * masks + -(-masks // ns) if route == 2 else masks + 1


def clear_ends(cube, route, land):
    many = slots_of(cube, route)[3]

    def clear(first):
        ref = land.at[pl.ds(first, many)]
        ref[...] = jnp.zeros_like(ref)

    pl.when(jnp.logical_not(cube.has_below))(lambda: clear(0))
    pl.when(jnp.logical_not(cube.has_above))(lambda: clear(many))


def arrivals(cube, route, mask, col, lines, places, wait):
    below, above, over, unused = slots_of(cube, route)
    slots = [over(mask + (1 << p), col) for p in places]
    for slot in slots:
        wait(slot)
    if "below" in lines:
        pl.when(cube.has_below)(lambda: wait(below(mask, col)))
        slots.append(below(mask, col))
    if "above" in lines:
        pl.when(cube.has_above)(lambda: wait(above(mask, col)))
        slots.append(above(mask, col))
    return slots


def hand_on(cube, route, mask, col, to, give):
    below, above, over, unused = slots_of(cube, route)
    if to == "above":
        give(below(mask, col), cube.above)
    elif to == "below":
        give(above(mask, col), cube.below)
    elif to is not None:
        give(over(mask, col), cube.partner(route, to))


def scatter_steps(cube, parts, sums, pairs, lands, sems):
    send_sem, recv_sem, pair_sem = sems

    def pieces(routes):
        for a, part in enumerate(parts):
            for k, (route, first, count) in enumerate(routes_of(part.shape[2])):
                if route in routes:
                    yield (a, route, pl.ds(first, count), pairs[a][k], lands[a][k])

    def give_pair(routes, mask, col, to, lines, places):
        for a, route, cols, pair, unused in pieces(routes):
            index = cube.at(mask, col, route) + cube.sibling_step
            send(
                parts[a].at[index, :, cols],
                pair.at[mask, col],
                send_sem.at[a],
                pair_sem.at[a, route, mask, col],
                cube.sibling,
            )

    def step(routes, mask, col, to, lines, places):
        for a, route, cols, pair, land in pieces(routes):
            index = cube.at(mask, col, route)
            rows = parts[a].shape[1]
            await_bytes(pair.at[mask, col], pair_sem.at[a, route, mask, col])

            def wait(slot):
                await_bytes(land.at[slot], recv_sem.at[(a, route) + slot])

            slots = arrivals(cube, route, mask, col, lines, places, wait)
            deep = min(rows, 16)
            for r in range(0, rows, deep):
                at = pl.ds(r, deep)
                total = parts[a][index, at, cols].astype(jnp.float32)
                total = total + pair[mask, col, at, :].astype(jnp.float32)
                for slot in slots:
                    total = total + land[slot + (at, slice(None))].astype(jnp.float32)
                if to is not None:
                    pair[mask, col, at, :] = total.astype(jnp.bfloat16)
                else:
                    sums[a][at, cols] = total

            def give(slot, device):
                send(
                    pair.at[mask, col],
                    land.at[slot],
                    send_sem.at[a],
                    recv_sem.at[(a, route) + slot],
                    device,
                )

            hand_on(cube, route, mask, col, to, give)

    return (give_pair, step)


def back_kernel(
    fsdp,
    ns,
    per_device,
    far,
    inverse_ref,
    masks_ref,
    proj_ref,
    x_rows,
    dt_rows,
    vec_ref,
    gain_ref,
    gsum_ref,
    gamat_ref,
    dbc_ref,
    all_in,
    dtok_ref,
    ggain_ref,
    sum_in,
    sum_out,
    sum_small,
    sum_vec,
    near,
    near_sem,
    part_in,
    part_small,
    small_s,
    pair_in,
    pair_out,
    pair_small,
    land_in,
    land_out,
    land_small,
    dx_s,
    dhidden_s,
    weights,
    mask_s,
    dproj_s,
    dtin_s,
    du_s,
    gx_s,
    gdt_s,
    last_s,
    load_sem,
    send_first,
    recv_first,
    pair_first,
    send_sem,
    recv_sem,
    pair_sem,
):
    copies = [
        pltpu.make_async_copy(source, target, near_sem.at[k])
        for k, (source, target) in enumerate(zip(far, near))
    ]
    for copy in copies:
        copy.start()
    (
        gout_ref,
        dgate_ref,
        hidden_ref,
        ddt_ref,
        du_ref,
        u_ref,
        upre_ref,
        xpart_ref,
        tokens_ref,
        cot_ref,
    ) = near
    cube = Cube(fsdp, ns)
    length, width = tokens_ref.shape
    inner = x_rows.shape[0]
    cube.greet()
    give_out, step_out = scatter_steps(
        cube, (gout_ref,), (sum_out,), (pair_out,), (land_out,), (send_first, recv_first, pair_first)
    )
    give_in, step_in = scatter_steps(
        cube,
        (part_in, part_small),
        (sum_in, sum_small),
        (pair_in, pair_small),
        (land_in, land_small),
        (send_sem, recv_sem, pair_sem),
    )
    copies[0].wait()
    cube.downward(give_out)
    for part, land in ((gout_ref, land_out), (part_in, land_in), (part_small, land_small)):
        for (route, unused, unused), where in zip(routes_of(part.shape[2]), land):
            clear_ends(cube, route, where)

    group = BAND // part_in.shape[1]

    def into_part(first, source):
        def band(i, carry):
            cols = pl.ds(pl.multiple_of(i * BAND, BAND), BAND)
            gradient = contract(source[:, cols], hidden_ref[...], 0, 0).astype(jnp.bfloat16)
            at = pl.ds(first + i * group, group)
            part_in[at] = gradient.reshape(group, part_in.shape[1], width)
            return carry

        lax.fori_loop(0, inner // BAND, band, 0)

    for copy in copies[1:3]:
        copy.wait()
    into_part(cube.shards // 2, dgate_ref)
    for k in range(1, KCONV):
        mask_s[k - 1] = jnp.broadcast_to(masks_ref[:, k : k + 1], (length, LANES))
    for copy in copies[3:]:
        copy.wait()
    d_dtin = jnp.dot(ddt_ref[...], dt_rows[...], preferred_element_type=jnp.float32)
    dproj_s[...] = (d_dtin + dbc_ref[...]).astype(jnp.bfloat16)
    lane = lax.broadcasted_iota(jnp.int32, (length, LANES), 1)
    dtin_s[...] = jnp.where(lane < DTRANK, proj_ref[...], 0.0).astype(jnp.bfloat16)
    sub = lax.broadcasted_iota(jnp.int32, (SUBS, LANES), 0)

    def state_band(i, carry):
        at = pl.ds(pl.multiple_of(i * BAND, BAND), BAND)
        du_s[:, at] = du_ref[:, at] + contract(dproj_s[...], x_rows[at, :], 1, 1)
        gx_s[at, :] = contract(u_ref[:, at], dproj_s[...], 0, 0)
        gdt_s[at, :] = contract(ddt_ref[:, at], dtin_s[...], 0, 0)
        return carry

    lax.fori_loop(0, inner // BAND, state_band, 0)

    def x_chunk(chunk):
        cols = pl.ds(pl.multiple_of(chunk * LANES, LANES), LANES)
        x, upre = xpart_ref[:, cols], upre_ref[:, cols]
        sig = jax.nn.sigmoid(upre)
        dpre = du_s[:, cols] * sig * (1.0 + upre * (1.0 - sig))
        dx = vec_ref[TAPS : TAPS + 1, cols] * dpre
        sums = [jnp.sum(dpre * x, axis=0, keepdims=True)]
        for k in range(1, KCONV):
            masked = mask_s[k - 1] * dpre
            dx = dx + vec_ref[TAPS + k : TAPS + k + 1, cols] * pltpu.roll(masked, length - k, 0)
            sums.append(jnp.sum(masked * pltpu.roll(x, k, 0), axis=0, keepdims=True))
        sums.append(jnp.sum(dpre, axis=0, keepdims=True))
        sums.append(jnp.sum(gsum_ref[SUBS : 2 * SUBS, cols], axis=0, keepdims=True))
        sums.append(jnp.sum(gsum_ref[0:SUBS, cols], axis=0, keepdims=True))
        last = jnp.zeros((SUBS, LANES), jnp.float32)
        for k, value in enumerate(sums):
            last = jnp.where(sub == k, value, last)
        last_s[:, cols] = last
        dx_s[:, cols] = dx.astype(jnp.bfloat16)

    steps = ns << (cube.places - 1)
    many = max(CHUNKS // steps, 1)
    every = max(steps // CHUNKS, 1)

    def x_chunks(place, k):
        def run():
            for i in range(many):
                x_chunk((k if every == 1 else lax.div(k, every)) * many + i)

        if every == 1:
            run()
        else:
            pl.when(lax.rem(k, every) == 0)(run)

    cube.down_stage(0, step_out, x_chunks)
    into_part(0, dx_s)

    small_s[...] = jnp.zeros_like(small_s)
    owners = LANES // per_device

    def small_chunk(chunk, carry):
        cols = pl.ds(pl.multiple_of(chunk * LANES, LANES), LANES)
        shape = (owners, per_device, LANES)
        small_s[:, 0:per_device, 0:LANES] = gx_s[cols, :].reshape(shape)
        small_s[:, 0:per_device, LANES:VEC_AT] = gdt_s[cols, :].reshape(shape)[:, :, 0:DTRANK]
        rates, last = gamat_ref[:, cols], last_s[:, cols]
        for o in range(owners):
            mine = slice(o * per_device, (o + 1) * per_device)
            small_s[o, 0:DSTATE, VEC_AT : VEC_AT + per_device] = rates[:, mine]
            small_s[o, DSTATE:VECS, VEC_AT : VEC_AT + per_device] = last[:, mine]
        part_small[pl.ds(chunk * owners, owners)] = small_s[...].astype(jnp.bfloat16)
        return carry

    lax.fori_loop(0, inner // LANES, small_chunk, 0)
    cube.downward(give_in)

    share = cube.shards // CHUNKS
    span = 2 * inner // CHUNKS

    def load(chunk):
        slot = lax.rem(chunk, 2)
        return pltpu.make_async_copy(
            all_in.at[pl.ds(chunk * share, share)], weights.at[slot], load_sem.at[slot]
        )

    dhidden_s[...] = jnp.zeros_like(dhidden_s)
    load(jnp.int32(0)).start()

    def hidden_chunk(chunk, left, base):
        load(chunk).wait()
        pl.when(chunk + 1 < CHUNKS)(lambda: load(chunk + 1).start())
        cols = pl.ds(pl.multiple_of((chunk - base) * span, span), span)
        right = weights[lax.rem(chunk, 2)].reshape(span, width)
        dhidden_s[...] += jnp.dot(left[:, cols], right, preferred_element_type=jnp.float32)

    def tokens_rows(i, total):
        at = pl.ds(pl.multiple_of(i * 16, 16), 16)
        inverse = inverse_ref[at, 0:1]
        normed = tokens_ref[at, :].astype(jnp.float32) * inverse
        dhidden = dhidden_s[at, :]
        product = dhidden * normed
        scaled = dhidden * gain_ref[...]
        mean = jnp.mean(scaled * normed, axis=-1, keepdims=True)
        dtok_ref[at, :] = cot_ref[at, :].astype(jnp.float32) + inverse * (scaled - normed * mean)
        return total + product[0:8] + product[8:16]

    part = CHUNKS // 2

    def hidden_chunks(first, last, left, base):
        def body(chunk, carry):
            hidden_chunk(chunk, left, base)
            return carry

        lax.fori_loop(first, last, body, 0)

    for stage in range(cube.places + 2):
        if stage < cube.places + 1:
            cube.down_stage(stage + 1, step_out)
        cube.down_stage(stage, step_in)
        if stage == 0:
            hidden_chunks(0, part, dx_s, 0)
        if stage == 1:
            hidden_chunks(part, CHUNKS, dgate_ref, part)
        if stage == cube.places:
            zero = jnp.zeros((SUBS, width), jnp.float32)
            total = lax.fori_loop(0, length // 16, tokens_rows, zero)
            row = jnp.sum(total, axis=0, keepdims=True)
            ggain_ref[...] = jnp.zeros_like(ggain_ref)
            for k in range(width // LANES):
                ggain_ref[k : k + 1, :] = row[:, k * LANES : (k + 1) * LANES]
    vectors = sum_small[0:VECS, VEC_AT : VEC_AT + per_device]
    sum_vec[0 : KCONV + 3, :] = vectors[DSTATE:GAIN, :]
    sum_vec[KCONV + 3 :, :] = vectors[0:DSTATE, :]
    await_bytes(gout_ref.at[pl.ds(0, cube.shards - 1)], send_first.at[0])
    await_bytes(part_in.at[pl.ds(0, cube.shards - 1)], send_sem.at[0])
    await_bytes(part_small.at[pl.ds(0, cube.shards - 1)], send_sem.at[1])


def back_and_scatter(far, arrays, all_in, per_device, small, fsdp, ns):
    length, width = arrays[0].shape[0], all_in.shape[2]
    inner = per_device * fsdp * ns
    shards, masks = fsdp * ns, fsdp // 2
    f32, b16 = jnp.float32, jnp.bfloat16
    blocks = [(2 * per_device, width), (per_device, width), (small, SMALL_COLUMNS)]

    def inbox(slots):
        return [
            [
                pltpu.VMEM((slots(route), ns, rows, count), b16)
                for route, unused, count in routes_of(columns)
            ]
            for rows, columns in blocks
        ]

    most = slot_count(fsdp, ns, 2)
    return pl.pallas_call(
        functools.partial(back_kernel, fsdp, ns, per_device),
        in_specs=[
            [pl.BlockSpec(memory_space=pl.ANY)] * len(far),
            *[pl.BlockSpec(memory_space=pltpu.VMEM)] * len(arrays),
            pl.BlockSpec(memory_space=pl.ANY),
        ],
        out_specs=[pl.BlockSpec(memory_space=pltpu.VMEM)] * 6,
        out_shape=[
            jax.ShapeDtypeStruct((length, width), f32),
            jax.ShapeDtypeStruct((-(-width // LANES // 16) * 16, LANES), f32),
        ]
        + [jax.ShapeDtypeStruct(block, f32) for block in blocks]
        + [jax.ShapeDtypeStruct((GAIN, per_device), f32)],
        scratch_shapes=[
            [pltpu.VMEM(array.shape, array.dtype) for array in far],
            pltpu.SemaphoreType.DMA((len(far),)),
            pltpu.VMEM((shards,) + blocks[0], b16),
            pltpu.VMEM((shards,) + blocks[2], b16),
            pltpu.VMEM((LANES // per_device,) + blocks[2], f32),
        ]
        + inbox(lambda route: masks)
        + inbox(functools.partial(slot_count, fsdp, ns))
        + [
            pltpu.VMEM((length, inner), b16),
            pltpu.VMEM((length, width), f32),
            pltpu.VMEM((2, shards // CHUNKS) + blocks[0], b16),
            pltpu.VMEM((KCONV - 1, length, LANES), f32),
            pltpu.VMEM((length, LANES), b16),
            pltpu.VMEM((length, LANES), b16),
            pltpu.VMEM((length, inner), f32),
            pltpu.VMEM((inner, LANES), f32),
            pltpu.VMEM((inner, LANES), f32),
            pltpu.VMEM((SUBS, inner), f32),
            pltpu.SemaphoreType.DMA((2,)),
            pltpu.SemaphoreType.DMA((1,)),
            pltpu.SemaphoreType.DMA((1, ROUTES, most, ns)),
            pltpu.SemaphoreType.DMA((1, ROUTES, masks, ns)),
            pltpu.SemaphoreType.DMA((2,)),
            pltpu.SemaphoreType.DMA((2, ROUTES, most, ns)),
            pltpu.SemaphoreType.DMA((2, ROUTES, masks, ns)),
        ],
        compiler_params=pltpu.CompilerParams(
            collective_id=1, has_side_effects=True, vmem_limit_bytes=60 * 1024 * 1024
        ),
    )(far, *arrays, all_in)


def halves_of(deep, wide):
    if deep >= 32:
        return [(g, (g * (deep // 2), deep // 2), (0, wide)) for g in range(2)]
    return [(g, (0, deep), (first, count)) for g, first, count in routes_of(wide, wide)]


def muon_kernel(
    fsdp,
    ns,
    starts,
    sum_in,
    sum_out,
    in_moment,
    out_moment,
    low_ref,
    gain_ref,
    x_out,
    low_out,
    gain_out,
    rows_s,
    turn,
    back_s,
    mine,
    outbox,
    lands,
    pieces_s,
    gram,
    now,
    poly,
    small_now,
    small_land,
    small_gram,
    low_s,
    send_sem,
    gather_sem,
    recv_sem,
    came_sem,
    swap_sem,
    small_send,
    small_recv,
):
    cube = Cube(fsdp, ns)
    pieces, deep, wide = pieces_s.shape
    width = now.shape[0]
    rows = sum_in.shape[0]
    blocks = width // LANES
    each = LANES // deep
    split = halves_of(deep, wide)
    ways = [cube.sibling] + [cube.partner(0, place) for place in range(cube.places)]
    ways += [(cube.row, flipped(cube.col, 1 << k)) for k in range(ns.bit_length() - 1)]
    stages = len(ways)
    cube.greet(ways[cube.places + 2 :])

    short = sum_out.shape[0]
    rows_s[0] = (MOMENTUM * in_moment[...] + sum_in[...]).astype(jnp.bfloat16)
    rows_s[1, 0:short, :] = (MOMENTUM * out_moment[...] + sum_out[...]).astype(jnp.bfloat16)
    rows_s[1, short:, :] = jnp.zeros((rows - short, width), jnp.bfloat16)

    def swap(source, target, which):
        return pltpu.make_async_remote_copy(
            src_ref=source,
            dst_ref=target,
            send_sem=swap_sem.at[which, 0],
            recv_sem=swap_sem.at[which, 1],
            device_id=cube.sibling,
            device_id_type=MESH,
        )

    there = swap(rows_s.at[1 - cube.core], turn.at[pl.ds(rows, rows)], 0)
    there.start()
    turn[0:rows] = rows_s[cube.core]

    def small_copy(k):
        return pltpu.make_async_remote_copy(
            src_ref=small_now.at[k],
            dst_ref=small_land.at[k],
            send_sem=small_send.at[k],
            recv_sem=small_recv.at[k],
            device_id=ways[k],
            device_id_type=MESH,
        )

    def inverse(total):
        return 1.0 / (jnp.sqrt(jnp.full((1, 1), total, jnp.float32)) + FROB_EPS)

    def diagonal(block):
        on = lax.broadcasted_iota(jnp.int32, block.shape, 0) == lax.broadcasted_iota(
            jnp.int32, block.shape, 1
        )
        return jnp.sum(jnp.where(on, block, 0.0))

    def small_step(k):
        small_copy(k).wait()
        total = small_now[k].astype(jnp.float32) + small_land[k].astype(jnp.float32)
        if k + 1 < stages:
            small_now[k + 1] = total.astype(jnp.bfloat16)
            small_copy(k + 1).start()
            return
        gain_out[...] = total[starts[2] :]
        for which in range(2):
            deep = starts[which + 1] - starts[which]
            whole = jnp.pad(total[starts[which] : starts[which + 1]], ((0, LANES - deep), (0, 0)))
            scale = inverse(diagonal(whole))
            small_gram[which] = whole * (scale * scale)
            low_s[which] = (low_ref[which] * scale).astype(jnp.bfloat16)

    for which in range(2):
        low = low_ref[which].astype(jnp.bfloat16)
        term = contract(low, low, 0, 0)[0 : starts[which + 1] - starts[which]]
        small_now[0, starts[which] : starts[which + 1], :] = term.astype(jnp.bfloat16)
    small_now[0, starts[2] :, :] = gain_ref[...].astype(jnp.bfloat16)
    small_copy(0).start()
    left = list(range(stages))

    def between():
        if left:
            small_step(left.pop(0))

    for (route, unused, unused), land in zip(split, lands):
        clear_ends(cube, route, land)

    there.wait()
    for b in range(blocks):
        if b % 2 == 0:
            band = contract(turn[:, b * LANES : (b + 2) * LANES], turn[...], 0, 0)
        block = band[b % 2 * LANES : (b % 2 + 1) * LANES]
        for c in range(wide // LANES):
            at = (b + c) % blocks * LANES
            for r in range(each):
                strip = block[r * deep : (r + 1) * deep, at : at + LANES]
                mine[b * each + r, :, c * LANES : (c + 1) * LANES] = strip

    def step(routes, mask, col, to, lines, places):
        for (route, rows_at, cols_at), land in zip(split, lands):
            if route not in routes:
                continue
            at = (cube.spot(mask, col, route), pl.ds(*rows_at), pl.ds(*cols_at))

            def wait(slot):
                await_bytes(land.at[slot], recv_sem.at[(route,) + slot])

            total = mine[at]
            for slot in arrivals(cube, route, mask, col, lines, places, wait):
                total = total + land[slot].astype(jnp.float32)
            if to is not None:
                outbox[at] = total.astype(jnp.bfloat16)
            else:
                pieces_s[at] = total.astype(jnp.bfloat16)

            def give(slot, device):
                send(
                    outbox.at[at],
                    land.at[slot],
                    send_sem,
                    recv_sem.at[(route,) + slot],
                    device,
                )

            hand_on(cube, route, mask, col, to, give)

    for stage in range(cube.places + 2):
        cube.down_stage(stage, step, third=False)
        if stage <= cube.places:
            between()

    def spread(routes, mask, col, ways, places, own):
        for route, rows_at, cols_at in split:
            if route not in routes:
                continue
            block = pieces_s.at[cube.spot(mask, col, route), pl.ds(*rows_at), pl.ds(*cols_at)]

            def sem_of(mask, col):
                return came_sem.at[route, mask, col]

            if not own:
                await_bytes(block, sem_of(mask, col))
            sems = gather_sem.at[route]
            pass_on(cube, route, mask, col, ways, places, block, block, sems, sem_of)

    def small_newton():
        for which in range(2):
            whole = small_gram[which]
            low = whole.astype(jnp.bfloat16)
            power = jnp.dot(low, low, preferred_element_type=jnp.float32)
            mixed = (COEF_B * whole + COEF_C * power).astype(jnp.bfloat16)
            block = low_s[which]
            low_s[which] = (
                COEF_A * block.astype(jnp.float32)
                + jnp.dot(block, mixed, preferred_element_type=jnp.float32)
            ).astype(jnp.bfloat16)
            half = COEF_A * whole + jnp.dot(low, mixed, preferred_element_type=jnp.float32)
            small_gram[which] = COEF_A * half + jnp.dot(
                half.astype(jnp.bfloat16), mixed, preferred_element_type=jnp.float32
            )

    def after(place, k):
        if place == cube.places - 1:
            pl.when(k - (ns << place) < NS_STEPS)(small_newton)

    cube.upward(spread, after=after, between=between, third=False)
    low_out[...] = low_s[...]

    for b in range(blocks):
        for c in range(wide // LANES):
            at = (b + c) % blocks * LANES
            for r in range(each):
                now[b * LANES + r * deep : b * LANES + (r + 1) * deep, at : at + LANES] = pieces_s[
                    b * each + r, :, c * LANES : (c + 1) * LANES
                ]
    for b in range(blocks):
        for c in range(wide // LANES, blocks):
            other = (b + c) % blocks
            block = now[other * LANES : (other + 1) * LANES, b * LANES : (b + 1) * LANES]
            flip = block.astype(jnp.float32).T.astype(jnp.bfloat16)
            now[b * LANES : (b + 1) * LANES, other * LANES : (other + 1) * LANES] = flip

    total = jnp.zeros((), jnp.float32)
    for b in range(0, width, LANES):
        total = total + diagonal(now[b : b + LANES, b : b + LANES].astype(jnp.float32))
    factor = inverse(total)
    square = factor * factor
    strip = min(BAND, width)

    def turned(block, k):
        moved = COEF_A * block.astype(jnp.float32) + jnp.dot(
            block, poly[...], preferred_element_type=jnp.float32
        )
        if k == 0:
            moved = moved * factor
        return moved.astype(jnp.bfloat16)

    for k in range(NS_STEPS):

        def poly_strip(i, carry, k=k):
            at = pl.ds(pl.multiple_of(i * strip, strip), strip)
            low = now[at, :]
            power = jnp.dot(low, now[...], preferred_element_type=jnp.float32)
            if k == 0:
                mixed = COEF_B * square * low.astype(jnp.float32) + (COEF_C * square * square) * power
            else:
                mixed = COEF_B * gram[at, :] + COEF_C * power
            poly[at, :] = mixed.astype(jnp.bfloat16)
            return carry

        lax.fori_loop(0, width // strip, poly_strip, 0)
        if k + 1 == NS_STEPS:
            break
        turn[...] = turned(turn[...], k)

        def gram_strip(i, carry, k=k):
            at = pl.ds(pl.multiple_of(i * strip, strip), strip)
            low = now[at, :]
            full = low.astype(jnp.float32) if k == 0 else gram[at, :]
            half = COEF_A * full + jnp.dot(low, poly[...], preferred_element_type=jnp.float32)
            if k == 0:
                half = half * square
            renewed = COEF_A * half + jnp.dot(
                half.astype(jnp.bfloat16), poly[...], preferred_element_type=jnp.float32
            )
            gram[at, :] = renewed
            now[at, :] = renewed.astype(jnp.bfloat16)
            return carry

        lax.fori_loop(0, width // strip, gram_strip, 0)
    turn[rows:] = turned(turn[rows:], NS_STEPS - 1)
    home = swap(turn.at[pl.ds(rows, rows)], back_s, 1)
    home.start()
    x_out[cube.core] = turned(turn[0:rows], NS_STEPS - 1)
    home.wait()
    x_out[1 - cube.core] = back_s[...]
    await_bytes(outbox.at[pl.ds(0, pieces - 1)], send_sem)
    for route, rows_at, cols_at in split:
        sent = pieces_s.at[:, pl.ds(*rows_at), pl.ds(*cols_at)]
        await_passed(cube, route, sent, gather_sem.at[route])


def muon_rows(sum_in, sum_out, in_moment, out_moment, low, columns, gain, fsdp, ns):
    pieces = fsdp * ns // 2
    rows, width = sum_in.shape
    wide = (width // LANES // 2 + 1) * LANES
    deep = width // pieces
    block = (pieces, deep, wide)
    stages = (fsdp * ns).bit_length() - 1
    starts = (0, columns[0], sum(columns))
    small = (sum(columns) + gain.shape[0], LANES)
    f32, b16 = jnp.float32, jnp.bfloat16
    landing = [
        pltpu.VMEM((slot_count(fsdp, ns, route), ns, rows_at[1], cols_at[1]), b16)
        for route, rows_at, cols_at in halves_of(deep, wide)
    ]
    held = pl.BlockSpec(memory_space=pltpu.VMEM)
    return pl.pallas_call(
        functools.partial(muon_kernel, fsdp, ns, starts),
        in_specs=[held] * 6,
        out_specs=[held] * 3,
        out_shape=[
            jax.ShapeDtypeStruct((2, rows, width), b16),
            jax.ShapeDtypeStruct(low.shape, b16),
            jax.ShapeDtypeStruct(gain.shape, f32),
        ],
        scratch_shapes=[
            pltpu.VMEM((2, rows, width), b16),
            pltpu.VMEM((2 * rows, width), b16),
            pltpu.VMEM((rows, width), b16),
            pltpu.VMEM(block, f32),
            pltpu.VMEM(block, b16),
        ]
        + [
            landing,
            pltpu.VMEM(block, b16),
            pltpu.VMEM((width, width), f32),
            pltpu.VMEM((width, width), b16),
            pltpu.VMEM((width, width), b16),
            pltpu.VMEM((stages,) + small, b16),
            pltpu.VMEM((stages,) + small, b16),
            pltpu.VMEM((2, LANES, LANES), f32),
            pltpu.VMEM(low.shape, b16),
            pltpu.SemaphoreType.DMA,
            pltpu.SemaphoreType.DMA((ROUTES, 3)),
            pltpu.SemaphoreType.DMA((ROUTES, slot_count(fsdp, ns, 2), ns)),
            pltpu.SemaphoreType.DMA((ROUTES, fsdp // 2, ns)),
            pltpu.SemaphoreType.DMA((2, 2)),
            pltpu.SemaphoreType.DMA((stages,)),
            pltpu.SemaphoreType.DMA((stages,)),
        ],
        compiler_params=pltpu.CompilerParams(
            collective_id=2, has_side_effects=True, vmem_limit_bytes=48 * 1024 * 1024
        ),
    )(sum_in, sum_out, in_moment, out_moment, low, gain)


def layer(tokens, out_grad, lengths, params, fsdp, ns):
    flat_low, grad_flat = tokens[0], out_grad[0]
    length, width = flat_low.shape
    (
        all_in,
        all_out,
        x_rows,
        dt_rows,
        vecs,
        gain,
        x_part,
        gate_in,
        conv_flat,
        u_low,
        proj,
        masks,
        hidden,
        inverse,
    ) = gather_and_front(lengths, flat_low, params, fsdp, ns)
    per_device = params[2].shape[0]
    inner = x_rows.shape[0]
    out_low = all_out.reshape(inner, width)
    d_gate, d_u, d_dtlow, vec_parts, grad_amat, d_bc, grad_out, block_out = scan_both(
        proj, masks, dt_rows, u_low, gate_in, flat_low, grad_flat, out_low, vecs
    )
    d_tokens, grad_gain, sum_in, sum_out, sum_small, sum_vec = back_and_scatter(
        [
            grad_out.reshape(fsdp * ns, per_device, width),
            d_gate,
            hidden,
            d_dtlow,
            d_u,
            u_low,
            conv_flat,
            x_part,
            flat_low,
            grad_flat,
        ],
        (inverse, masks, proj, x_rows, dt_rows, vecs, gain, vec_parts, grad_amat, d_bc),
        all_in,
        per_device,
        small_rows(per_device),
        fsdp,
        ns,
    )
    return (block_out[None], d_tokens[None], grad_gain, sum_in, sum_out, sum_small, sum_vec)


def adamw_update(param, first, second, grad):
    first_new = FIRST_MOMENT_BETA * first + (1.0 - FIRST_MOMENT_BETA) * grad
    second_new = BETA_SECOND * second + (1.0 - BETA_SECOND) * grad * grad
    first_hat = first_new / (1.0 - FIRST_MOMENT_BETA**STEP_NO)
    second_hat = second_new / (1.0 - BETA_SECOND**STEP_NO)
    param_new = param * (1.0 - ADAM_RATE * ADAM_DECAY) - ADAM_RATE * first_hat / (
        jnp.sqrt(second_hat) + ADAM_EPS
    )
    return (param_new, first_new, second_new)


def on_device(
    tokens,
    out_grad,
    doc_lengths,
    in_proj,
    inner_projection_weight,
    dt_proj,
    out_proj,
    in_moment,
    x_moment,
    dt_moment,
    out_moment,
    vectors,
    vector_first,
    vector_second,
    norm_gain,
    gain_first,
    gain_second,
):
    fsdp, ns = lax.axis_size("fsdp"), lax.axis_size("ns")
    shards = fsdp * ns
    per_device, columns = inner_projection_weight.shape
    rank, gains = dt_proj.shape[1], norm_gain.shape[0]
    block_out, grad_tokens, grad_gain, sum_in, sum_out, sum_small, sum_vec = layer(
        tokens,
        out_grad,
        doc_lengths,
        (
            in_proj,
            out_proj,
            inner_projection_weight,
            dt_proj,
            vectors,
            norm_gain[None],
        ),
        fsdp,
        ns,
    )
    sum_x = sum_small[:per_device, :columns]
    sum_dt = sum_small[:per_device, LANES : LANES + rank]
    summed = (sum_in, sum_x, sum_dt, sum_out, sum_vec)
    old_moments = (in_moment, x_moment, dt_moment, out_moment)
    moments = tuple((MOMENTUM * moment + grad for moment, grad in zip(old_moments, summed[:4])))
    gap = -per_device % 16
    low = jnp.stack(
        [
            jnp.pad(moments[1], ((0, gap), (0, LANES - columns))),
            jnp.pad(moments[2], ((0, gap), (0, LANES - rank))),
        ]
    )
    big, low, sum_gain = muon_rows(
        sum_in, sum_out, in_moment, out_moment, low, (columns, rank), grad_gain, fsdp, ns
    )
    place = lax.axis_index("fsdp") * ns + lax.axis_index("ns")
    sum_gain = lax.dynamic_slice_in_dim(sum_gain.reshape(-1), place * gains, gains, 0)
    own_blocks = (
        big[0],
        low[0, :per_device, :columns],
        low[1, :per_device, :rank],
        big[1, :per_device],
    )
    weights = (in_proj, inner_projection_weight, dt_proj, out_proj)
    fans = (DMODEL, DINNER, DTRANK, DINNER // 8)
    results = []
    for weight, moment, block, fan in zip(weights, moments, own_blocks, fans):
        rate = 0.5 * math.sqrt(weight.shape[0] * shards / fan)
        results.append((1.0 - SHRINK) * weight - rate * block.astype(jnp.float32))
        results.append(moment)
    vec_new, vec_first, vec_second = adamw_update(vectors, vector_first, vector_second, summed[4])
    gain_new, gain_m, gain_v = adamw_update(norm_gain, gain_first, gain_second, sum_gain)
    return (
        block_out,
        grad_tokens,
        results[0],
        results[1],
        results[2],
        results[3],
        results[4],
        results[5],
        results[6],
        results[7],
        vec_new,
        vec_first,
        vec_second,
        gain_new,
        gain_m,
        gain_v,
    )


def solution(mesh):
    placed = (
        P(("fsdp", "ns"), None, None),
        P(("fsdp", "ns"), None, None),
        P(("fsdp", "ns"), None),
        P(("fsdp", "ns"), None),
        P(("fsdp", "ns"), None),
        P(("fsdp", "ns"), None),
        P(("fsdp", "ns"), None),
        P(("fsdp", "ns"), None),
        P(("fsdp", "ns"), None),
        P(("fsdp", "ns"), None),
        P(("fsdp", "ns"), None),
        P(None, ("fsdp", "ns")),
        P(None, ("fsdp", "ns")),
        P(None, ("fsdp", "ns")),
        P(("fsdp", "ns")),
        P(("fsdp", "ns")),
        P(("fsdp", "ns")),
    )
    return jax.shard_map(
        on_device,
        mesh=mesh,
        in_specs=placed,
        out_specs=(
            P(("fsdp", "ns"), None, None),
            P(("fsdp", "ns"), None, None),
            P(("fsdp", "ns"), None),
            P(("fsdp", "ns"), None),
            P(("fsdp", "ns"), None),
            P(("fsdp", "ns"), None),
            P(("fsdp", "ns"), None),
            P(("fsdp", "ns"), None),
            P(("fsdp", "ns"), None),
            P(("fsdp", "ns"), None),
            P(None, ("fsdp", "ns")),
            P(None, ("fsdp", "ns")),
            P(None, ("fsdp", "ns")),
            P(("fsdp", "ns")),
            P(("fsdp", "ns")),
            P(("fsdp", "ns")),
        ),
        check_vma=False,
    )
```
